32 devices in a mesh: lat: 4 (over y, core), lev: 8 (over z, x).
Axes of the slice: x: 2, y: 2, z: 4, core: 2. Of those that a mesh axis runs over, the one named last changes fastest.
Arguments:
- fields: float32 [4, 128, 32, 1152], P(None, 'lev', 'lat'), may hold values from -6 to 6
- winds: float32 [2, 128, 32, 1152], P(None, 'lev', 'lat'), may hold values from -0.3 to 0.3
- remap_weight: bfloat16 [128, 128], replicated, may hold values from -0.5 to 0.5
- w_first: bfloat16 [512, 512], replicated, may hold values from -0.25 to 0.25
- w_second: bfloat16 [512, 512], replicated, may hold values from -0.25 to 0.25
- w_third: bfloat16 [512, 512], replicated, may hold values from -0.25 to 0.25
- lon_counts: int32 [4, 8], P('lat'), may hold values from 1 to 384, 1152 in all within a row
- group_list: int32 [4, 6], replicated, may hold values from 0 to 31, as said below
Outputs:
- columns_out: bfloat16 [4, 128, 32, 3072], P(None, None, 'lat', 'lev')
The draws below stay inside these ranges and needn't reach their ends.
Inputs may be any that keep to these rules, and one draw needn't show every extreme that they name: `lon_counts`: each row sums to 1152, and its largest entry is exactly 384. `group_list`: row p lists in ascending order the 6 latitude rows whose columns owner p (index p of lat) processes; no row appears twice; every row j with j // 8 equal to 2 appears; at most 2 rows of one owner's list have the same j // 8, and some owner has exactly 2 such rows.
All inputs are finite; a program needn't handle non-finite values.
Results may differ from the reference program's by a relative error of at most 0.0053.
Values may be sent and summed in bfloat16 or wider, within the bound.
No kernel may reach another device: no remote copies, remote signals or barrier semaphores. Data moves between devices by JAX's collectives and lax.ppermute only.
A program may use at most 128 MiB of HBM per device.

```python
import math
import jax
import jax.numpy as jnp
import numpy as np
from jax import lax

F = 4
NLEV = 128
HID = 512
LAT_DEV = 8
NLON = 1152
NLAT = 32
CAP = 384
ROWS_PER = 6
FN = 512
N_LAT = 4
N_LEV = 8


def draw_group_list(key, part):
    band_count = NLAT // LAT_DEV
    middle = band_count // 2
    needed = band_count * ROWS_PER - LAT_DEV
    picked = jax.random.permutation(key, NLAT - LAT_DEV)[:needed].astype(jnp.int32)
    others = picked + LAT_DEV * (picked >= middle * LAT_DEV).astype(jnp.int32)
    central = middle * LAT_DEV + jnp.arange(LAT_DEV, dtype=jnp.int32)
    listed = jnp.sort(jnp.concatenate([central, others]))
    dealt_rows = listed.reshape(ROWS_PER, band_count).T
    owner_order = jax.random.permutation(jax.random.fold_in(key, 7), band_count)
    inverse = jnp.argsort(owner_order)
    return dealt_rows[inverse].astype(jnp.int32)


def block_scale(key, shape, shards, low, top_value):
    gain = 1.0
    for dim, shards_of in shards:
        heights = jax.random.uniform(jax.random.fold_in(jax.random.fold_in(key, 6), dim), (shards_of,), jnp.float32, low / len(shards), top_value / len(shards))
        gain = gain * jnp.repeat(jnp.exp(heights), shape[dim] // shards_of).reshape((-1,) + (1,) * (len(shape) - 1 - dim))
    return gain


def profile(amount, total, most, lean):
    loads = [(1 << 20) // math.isqrt(grade ** lean) + 1 for grade in range(2, amount + 1)]
    spare, holding = total - most - (amount - 1), [1] * (amount - 1)
    while spare > 0:
        movable = [i for i in range(amount - 1) if holding[i] < most]
        mass, budget = sum([loads[i] for i in movable]), spare
        for i in movable:
            extra = min(most - holding[i], max(1, budget * loads[i] // mass), spare)
            holding[i] = holding[i] + extra
            spare = spare - extra
    return np.array([most] + holding)


def ragged_sizes(key, amount, total, bound, skew):
    if amount == 2:
        one = jax.random.randint(key, (), max(1, total - bound), min(bound, total - 1) + 1)
        return jnp.stack([one, total - one])
    sizes = jnp.asarray(profile(amount, total, bound, skew), jnp.int32)
    pairs = (amount - 1) // 2
    donor, taker = sizes[1:1 + 2 * pairs:2], sizes[2:2 + 2 * pairs:2]
    slack = jnp.minimum(donor - 1, bound - taker)
    shifted = jax.random.randint(jax.random.fold_in(key, 1), (pairs,), 0, 1 << 20) % (slack + 1)
    sizes = sizes.at[1:1 + 2 * pairs:2].set(donor - shifted).at[2:2 + 2 * pairs:2].set(taker + shifted)
    return sizes[jax.random.permutation(jax.random.fold_in(key, 2), amount)]


def scatter_about(own_key, extent, scale, limit, pieces=(), held_as=jnp.bfloat16):
    array = jax.random.normal(own_key, extent, jnp.float32) * scale
    if len(pieces) > 0:
        array = block_scale(own_key, extent, pieces, -0.22, 0.18) * array
    return jnp.clip(array, min=-limit, max=limit).astype(held_as)


def setup_inputs(seed: int = 0) -> dict:
    key_list = jax.random.split(jax.random.key(seed), 9)
    return {
        "fields": scatter_about(key_list[0], (F, NLEV, NLAT, NLON), 1.0, 6.0, ((1, 8), (2, 4)), jnp.float32),
        "winds": jnp.clip(jax.random.uniform(key_list[1], (2, NLEV, NLAT, NLON), jnp.float32, -0.3, 0.3) * block_scale(key_list[1], (2, NLEV, NLAT, NLON), ((1, 8), (2, 4)), -0.4, 0.0), -0.3, 0.3),
        "remap_weight": scatter_about(key_list[2], (NLEV, NLEV), NLEV ** -0.5, 0.5),
        "w_first": scatter_about(key_list[3], (FN, HID), FN ** -0.5, 0.25),
        "w_second": scatter_about(key_list[4], (HID, HID), HID ** -0.5, 0.25),
        "w_third": scatter_about(key_list[5], (HID, FN), HID ** -0.5, 0.25),
        "lon_counts": jax.vmap(lambda own: ragged_sizes(own, N_LEV, NLON, CAP, 2))(jax.random.split(key_list[6], N_LAT)).reshape((N_LAT, N_LEV)).astype(jnp.int32),
        "group_list": draw_group_list(jax.random.fold_in(key_list[8], 71), 0),
    }


DIFFUSION = 0.15


def flux_divergence(values, east_wind, north_wind, first_row, total_rows):
    inner_count = values.shape[-2] - 2
    face_flux = 0.25 * (north_wind[..., :-1, :] + north_wind[..., 1:, :]) * (values[..., :-1, :] + values[..., 1:, :])
    face_flux = face_flux - DIFFUSION * (values[..., 1:, :] - values[..., :-1, :])
    faces = first_row + jnp.arange(inner_count + 1, dtype=jnp.int32)
    keep_face = ((faces >= 1) & (faces <= total_rows - 1)).astype(jnp.float32)[:, None]
    face_flux = face_flux * keep_face
    inner = values[..., 1:-1, :]
    inner_wind = east_wind[..., 1:-1, :]
    west_values = jnp.roll(inner, 1, axis=-1)
    west_wind = jnp.roll(inner_wind, 1, axis=-1)
    side_flux = 0.25 * (west_wind + inner_wind) * (west_values + inner) - DIFFUSION * (inner - west_values)
    return -(face_flux[..., 1:, :] - face_flux[..., :-1, :]) - (jnp.roll(side_flux, -1, axis=-1) - side_flux)


def pad_rows(values):
    return jnp.pad(values, ((0, 0), (1, 1), (0, 0)))


def convect(columns, w_first, w_second, w_third):
    pattern = (((0,), (0,)), ((), ()))
    hidden_one = jax.nn.silu(lax.dot_general(w_first, columns, pattern, preferred_element_type=jnp.float32)).astype(jnp.bfloat16)
    hidden_two = jax.nn.silu(lax.dot_general(w_second, hidden_one, pattern, preferred_element_type=jnp.float32)).astype(jnp.bfloat16)
    return lax.dot_general(w_third, hidden_two, pattern, preferred_element_type=jnp.float32).astype(jnp.bfloat16)


def reference(fields, winds, remap_weight, w_first, w_second, w_third, lon_counts, group_list):
    east_padded = pad_rows(winds[0])
    north_padded = pad_rows(winds[1])

    def advect_field(field_values):
        predicted = field_values + flux_divergence(pad_rows(field_values), east_padded, north_padded, 0, NLAT)
        return 0.5 * (field_values + predicted + flux_divergence(pad_rows(predicted), east_padded, north_padded, 0, NLAT))

    advected = lax.map(advect_field, fields)
    rounded = advected.astype(jnp.bfloat16)
    weight_wide = remap_weight.astype(jnp.float32)

    def remap_field(block):
        values = block.astype(jnp.float32)
        return values + jnp.einsum("mn,nrc->mrc", weight_wide, values, precision=lax.Precision.HIGHEST)

    remapped = lax.map(remap_field, rounded)
    listed = jnp.any(group_list.reshape(-1)[None, :] == jnp.arange(NLAT, dtype=jnp.int32)[:, None], axis=1)
    lon_start = jnp.cumsum(lon_counts, axis=1) - lon_counts
    offsets = jnp.arange(CAP, dtype=jnp.int32)
    by_rows = remapped.transpose(2, 0, 1, 3)

    def one_row(row_index):
        row_values = lax.dynamic_index_in_dim(by_rows, row_index, 0, keepdims=False)
        features = row_values.astype(jnp.bfloat16).reshape(F * NLEV, NLON)
        tendency = lax.cond(listed[row_index],
                            lambda: convect(features, w_first, w_second, w_third),
                            lambda: jnp.zeros((F * NLEV, NLON), jnp.bfloat16))
        updated = (row_values + tendency.astype(jnp.float32).reshape(F, NLEV, NLON)).astype(jnp.bfloat16)
        band_number = row_index // LAT_DEV
        lon_index = lon_start[band_number][:, None] + offsets[None, :]
        in_range = offsets[None, :] < lon_counts[band_number][:, None]
        picked = jnp.take(updated, jnp.minimum(lon_index, NLON - 1).reshape(-1).astype(jnp.int32), axis=2)
        return jnp.where(in_range.reshape(-1)[None, None, :], picked, jnp.zeros_like(picked))

    rows_out = lax.map(one_row, jnp.arange(NLAT, dtype=jnp.int32))
    return rows_out.transpose(1, 2, 0, 3)
```

```python
import functools

import jax
import jax.numpy as jnp
from jax import lax
from jax.experimental import pallas as pl
from jax.experimental.pallas import tpu as pltpu
from jax.sharding import PartitionSpec as P

DIFFUSION = 0.15
LANES = 128
HALO = 2
VMEM_BYTES = 48 * 1024 * 1024


def face_weights(wind, axis):
    half = 0.25 * (pltpu.roll(wind, 1, axis) + wind)
    return half + DIFFUSION, half - DIFFUSION


def divergence(values, north, east):
    rows, lons = values.shape
    face = north[0] * pltpu.roll(values, 1, 0) + north[1] * values
    side = east[0] * pltpu.roll(values, 1, 1) + east[1] * values
    return (face - pltpu.roll(face, rows - 1, 0)) + (side - pltpu.roll(side, lons - 1, 1))


def heun(values, north, east):
    predicted = values + divergence(values, north, east)
    return 0.5 * (values + predicted + divergence(predicted, north, east))


def keep_rows(ref, place, values):
    rows, lons = values.shape
    for tile in range(lons // LANES):
        ref[tile, pl.ds(pl.multiple_of(place, rows), rows), :] = values[
            :, tile * LANES : (tile + 1) * LANES
        ]


def clear_tail(ref, tiles):
    for tile in range(tiles, ref.shape[0]):
        ref[tile] = jnp.zeros(ref.shape[1:], ref.dtype)


def slot_starts(counts_ref, owners):
    starts = []
    total = jnp.int32(0)
    for owner in range(owners):
        starts.append(total)
        total = total + counts_ref[0, owner]
    return starts


def pack_rows(starts, sources, out_ref, fields, levels, rows):
    blocks = out_ref.shape[1]
    lane = lax.broadcasted_iota(jnp.int32, (levels, LANES), 1)

    def one_field(field, carry):
        base = field * (levels * rows)
        for owner, start in enumerate(starts):
            tile = start // LANES
            inside = start - tile * LANES
            shift = (LANES - inside) % LANES
            keep = lane < LANES - inside
            for index, (ref, row) in enumerate(sources):
                turned = []
                for j in range(blocks + 1):
                    piece = ref[tile + j, pl.ds(base + row, levels, stride=rows), :]
                    turned.append(pltpu.roll(piece, shift, 1))
                for j in range(blocks):
                    joined = jnp.where(keep, turned[j], turned[j + 1])
                    out_ref[owner, j, index, field] = joined.astype(jnp.bfloat16)
        return carry

    lax.fori_loop(0, fields, one_field, 0)


def inner_kernel(counts_ref, fields_ref, winds_ref, out_ref, first_ref, last_ref, advected_ref):
    step = pl.program_id(0)
    fields, block, rows, lons = fields_ref.shape
    total_levels = advected_ref.shape[1] // (fields * rows)

    @pl.when(step == 0)
    def _():
        clear_tail(advected_ref, lons // LANES)

    def one_level(level, carry):
        east = face_weights(winds_ref[0, level], 1)
        north = face_weights(winds_ref[1, level], 0)
        for field in range(fields):
            values = fields_ref[field, level]
            place = (field * total_levels + step * block + level) * rows
            keep_rows(advected_ref, place, heun(values, north, east))
        return carry

    lax.fori_loop(0, block, one_level, 0)
    for field in range(fields):
        first_ref[field] = fields_ref[field, :, :HALO, :]
        last_ref[field] = fields_ref[field, :, rows - HALO :, :]
    for wind in range(2):
        first_ref[fields + wind] = winds_ref[wind, :, :HALO, :]
        last_ref[fields + wind] = winds_ref[wind, :, rows - HALO :, :]

    @pl.when(step == pl.num_programs(0) - 1)
    def _():
        starts = slot_starts(counts_ref, out_ref.shape[0])
        sources = [(advected_ref, row) for row in range(HALO, rows - HALO)]
        pack_rows(starts, sources, out_ref, fields, total_levels, rows)


def edge_kernel(
    counts_ref, band_ref, fields_ref, winds_ref, before_ref, after_ref, out_ref, top_ref, bottom_ref
):
    step = pl.program_id(0)
    fields, block, rows, lons = fields_ref.shape
    total_levels = top_ref.shape[1] // (fields * rows)
    row = lax.broadcasted_iota(jnp.int32, (rows, lons), 0)

    @pl.when(step == 0)
    def _():
        clear_tail(top_ref, lons // LANES)
        clear_tail(bottom_ref, lons // LANES)

    def upper(own, halo):
        padded = jnp.concatenate([halo, jnp.zeros((rows - HALO, lons), halo.dtype)], axis=0)
        return jnp.where(row < HALO, padded, pltpu.roll(own, HALO, 0))

    def lower(own, halo):
        padded = jnp.concatenate([jnp.zeros((rows - HALO, lons), halo.dtype), halo], axis=0)
        return jnp.where(row >= rows - HALO, padded, pltpu.roll(own, rows - HALO, 0))

    for extend, halo_ref, kept_ref, wall, flag in (
        (upper, before_ref, top_ref, HALO, band_ref[0]),
        (lower, after_ref, bottom_ref, rows - HALO, band_ref[1]),
    ):
        open_face = jnp.logical_not((row == wall) & (flag == 1)).astype(jnp.float32)

        def one_level(level, carry):
            east = face_weights(extend(winds_ref[0, level], halo_ref[fields, level]), 1)
            north = face_weights(extend(winds_ref[1, level], halo_ref[fields + 1, level]), 0)
            north = (north[0] * open_face, north[1] * open_face)
            for field in range(fields):
                values = extend(fields_ref[field, level], halo_ref[field, level])
                place = (field * total_levels + step * block + level) * rows
                keep_rows(kept_ref, place, heun(values, north, east))
            return carry

        lax.fori_loop(0, block, one_level, 0)

    @pl.when(step == pl.num_programs(0) - 1)
    def _():
        starts = slot_starts(counts_ref, out_ref.shape[0])
        sources = [(top_ref, HALO + i) for i in range(HALO)]
        sources += [(bottom_ref, rows - 2 * HALO + i) for i in range(HALO)]
        pack_rows(starts, sources, out_ref, fields, total_levels, rows)


def silu(x):
    half = 0.5 * x
    return half + half * jnp.tanh(half)


def dot(a, b):
    return jnp.dot(a, b, preferred_element_type=jnp.float32)


def column_update(block_ref, remap_ref, first_ref, second_ref, third_ref):
    sources, _, rows, fields = block_ref.shape[:4]
    remapped = []
    for field in range(fields):
        by_row = [
            jnp.concatenate([block_ref[source, 0, row, field] for source in range(sources)], axis=0)
            for row in range(rows)
        ]
        values = jnp.concatenate(by_row, axis=1)
        remapped.append(values.astype(jnp.float32) + dot(remap_ref[...], values))
    remapped = jnp.concatenate(remapped, axis=0)
    hidden = silu(dot(first_ref[...], remapped.astype(jnp.bfloat16))).astype(jnp.bfloat16)
    hidden = silu(dot(second_ref[...], hidden)).astype(jnp.bfloat16)
    tendency = dot(third_ref[...], hidden).astype(jnp.bfloat16).astype(jnp.float32)
    return remapped, tendency


def finished_row(remapped, tendency, listed, index, live):
    lanes = slice(index * LANES, (index + 1) * LANES)
    updated = remapped[:, lanes] + jnp.where(listed == 1, tendency[:, lanes], 0.0)
    return jnp.where(live, updated, 0.0)


def live_lanes(width_ref, features):
    lane = lax.broadcasted_iota(jnp.int32, (features, LANES), 1)
    return lane + pl.program_id(0) * LANES < width_ref[0]


def half_kernel(
    row_list, listed_ref, width_ref, block_ref, remap_ref, first_ref, second_ref, third_ref, out_ref
):
    remapped, tendency = column_update(block_ref, remap_ref, first_ref, second_ref, third_ref)
    live = live_lanes(width_ref, remapped.shape[0])
    for index, row in enumerate(row_list):
        out_ref[index] = finished_row(remapped, tendency, listed_ref[row], index, live).astype(
            jnp.bfloat16
        )


def last_kernel(
    row_list,
    done_list,
    listed_ref,
    width_ref,
    block_ref,
    done_ref,
    remap_ref,
    first_ref,
    second_ref,
    third_ref,
    out_ref,
    tiles_ref,
):
    features, rows, _ = out_ref.shape
    remapped, tendency = column_update(block_ref, remap_ref, first_ref, second_ref, third_ref)
    live = live_lanes(width_ref, features)
    for index, row in enumerate(done_list):
        tiles_ref[pl.ds(row, features, stride=rows), :] = done_ref[index].astype(jnp.float32)
    for index, row in enumerate(row_list):
        tiles_ref[pl.ds(row, features, stride=rows), :] = finished_row(
            remapped, tendency, listed_ref[row], index, live
        )
    out_ref[...] = tiles_ref[...].reshape(features, rows, LANES).astype(jnp.bfloat16)


def shards(fields, winds, remap_weight, w_first, w_second, w_third, lon_counts, group_list):
    field_count, level_count, lat_rows, lon_total = fields.shape
    band_count = lax.axis_size("lat")
    band_index = lax.axis_index("lat")
    owner_count = lax.axis_size("lev")
    first_row = band_index * lat_rows
    all_levels = level_count * owner_count
    features = field_count * all_levels
    blocks = (2 * lon_total // owner_count + LANES - 1) // LANES
    slot_width = blocks * LANES
    inner_rows = tuple(range(HALO, lat_rows - HALO))
    edge_rows = tuple(range(HALO)) + tuple(range(lat_rows - HALO, lat_rows))
    level_block = 4
    steps = level_count // level_block
    stacked = field_count + 2
    padded_lons = lon_total + slot_width
    smem = pl.BlockSpec(memory_space=pltpu.SMEM)
    params = pltpu.CompilerParams(
        dimension_semantics=("arbitrary",), vmem_limit_bytes=VMEM_BYTES
    )

    fields_spec = pl.BlockSpec((field_count, level_block, lat_rows, lon_total), lambda i: (0, i, 0, 0))
    winds_spec = pl.BlockSpec((2, level_block, lat_rows, lon_total), lambda i: (0, i, 0, 0))
    halo_spec = pl.BlockSpec((stacked, level_block, HALO, lon_total), lambda i: (0, i, 0, 0))
    halo_shape = jax.ShapeDtypeStruct((stacked, level_count, HALO, lon_total), jnp.float32)
    half_shape = (owner_count, blocks, len(inner_rows), field_count, level_count, LANES)
    half_spec = pl.BlockSpec(half_shape, lambda i: (0,) * 6)
    kept = pltpu.VMEM(
        (padded_lons // LANES, field_count * level_count * lat_rows, LANES), jnp.float32
    )
    grid_values = field_count * level_count * lat_rows * lon_total

    inner, first, last = pl.pallas_call(
        inner_kernel,
        grid=(steps,),
        in_specs=[smem, fields_spec, winds_spec],
        out_specs=[half_spec, halo_spec, halo_spec],
        out_shape=[jax.ShapeDtypeStruct(half_shape, jnp.bfloat16), halo_shape, halo_shape],
        scratch_shapes=[kept],
        compiler_params=params,
        cost_estimate=pl.CostEstimate(
            flops=40 * grid_values, bytes_accessed=8 * grid_values, transcendentals=0
        ),
        name="inner_rows",
    )(lon_counts, fields, winds)

    up = [(i, i + 1) for i in range(band_count - 1)]
    down = [(j, i) for i, j in up]
    inner_block = lax.all_to_all(inner, "lev", split_axis=0, concat_axis=0, tiled=True)
    before = lax.ppermute(last, "lat", up)
    after = lax.ppermute(first, "lat", down)

    walls = jnp.stack([band_index == 0, band_index == band_count - 1]).astype(jnp.int32)
    edge = pl.pallas_call(
        edge_kernel,
        grid=(steps,),
        in_specs=[smem, smem, fields_spec, winds_spec, halo_spec, halo_spec],
        out_specs=half_spec,
        out_shape=jax.ShapeDtypeStruct(half_shape, jnp.bfloat16),
        scratch_shapes=[kept, kept],
        compiler_params=params,
        cost_estimate=pl.CostEstimate(
            flops=80 * grid_values, bytes_accessed=10 * grid_values, transcendentals=0
        ),
        name="edge_rows",
    )(lon_counts, walls, fields, winds, before, after)
    edge_block = lax.all_to_all(edge, "lev", split_axis=0, concat_axis=0, tiled=True)

    listed = jnp.any(
        group_list[:, :, None] == (first_row + jnp.arange(lat_rows, dtype=jnp.int32))[None, None, :],
        axis=(0, 1),
    ).astype(jnp.int32)
    width = lax.dynamic_slice_in_dim(lon_counts[0], lax.axis_index("lev"), 1)
    weights = (remap_weight, w_first.T, w_second.T, w_third.T)

    def by_level(block):
        if level_count % 16 == 0:
            return block
        return block.transpose(1, 2, 3, 0, 4, 5).reshape(
            1, blocks, len(inner_rows), field_count, all_levels, LANES
        )

    def whole(shape):
        return pl.BlockSpec(shape, lambda i: (0,) * len(shape))

    inner_block, edge_block = by_level(inner_block), by_level(edge_block)
    sources, piece = inner_block.shape[0], inner_block.shape[4]
    block_spec = pl.BlockSpec(
        (sources, 1, len(inner_rows), field_count, piece, LANES), lambda i: (0, i, 0, 0, 0, 0)
    )
    weight_specs = [whole(w.shape) for w in weights]
    done_spec = pl.BlockSpec((len(inner_rows), features, LANES), lambda i: (0, 0, i))
    cost = pl.CostEstimate(
        flops=2 * features * len(inner_rows) * slot_width * (3 * w_first.shape[1] + all_levels),
        bytes_accessed=4 * features * len(inner_rows) * slot_width,
        transcendentals=2 * w_first.shape[1] * len(inner_rows) * slot_width,
    )
    done = pl.pallas_call(
        functools.partial(half_kernel, inner_rows),
        grid=(blocks,),
        in_specs=[smem, smem, block_spec] + weight_specs,
        out_specs=done_spec,
        out_shape=jax.ShapeDtypeStruct((len(inner_rows), features, slot_width), jnp.bfloat16),
        compiler_params=params,
        cost_estimate=cost,
        name="inner_columns",
    )(listed, width, inner_block, *weights)
    out = pl.pallas_call(
        functools.partial(last_kernel, edge_rows, inner_rows),
        grid=(blocks,),
        in_specs=[smem, smem, block_spec, done_spec] + weight_specs,
        out_specs=pl.BlockSpec((features, lat_rows, LANES), lambda i: (0, 0, i)),
        out_shape=jax.ShapeDtypeStruct((features, lat_rows, slot_width), jnp.bfloat16),
        scratch_shapes=[pltpu.VMEM((features * lat_rows, LANES), jnp.float32)],
        compiler_params=params,
        cost_estimate=cost,
        name="edge_columns",
    )(listed, width, edge_block, done, *weights)
    return out.reshape(field_count, all_levels, lat_rows, slot_width)


def solution(mesh):
    in_specs = (
        P(None, "lev", "lat", None),
        P(None, "lev", "lat", None),
        P(),
        P(),
        P(),
        P(),
        P("lat", None),
        P(),
    )
    out_specs = P(None, None, "lat", "lev")
    return jax.shard_map(shards, mesh=mesh, in_specs=in_specs, out_specs=out_specs, check_vma=False)
```

```python
import functools

import jax
import jax.numpy as jnp
from jax import lax
from jax.experimental import pallas as pl
from jax.experimental.pallas import tpu as pltpu
from jax.sharding import PartitionSpec as P

DIFFUSION = 0.15
LANES = 128
HALO = 2
MIB = 1024 * 1024


def from_west(x):
    return pltpu.roll(x, 1, 1)


def from_east(x):
    return pltpu.roll(x, x.shape[1] - 1, 1)


def flux(weights, before, after):
    return weights[0] * before + weights[1] * after


def face_weights(before, after):
    half = 0.25 * (before + after)
    return half + DIFFUSION, half - DIFFUSION


def divergences(values, rows, north, east):
    above = flux(north(rows[0]), values[rows[0] - 1], values[rows[0]])
    result = {}
    for row in rows:
        below = flux(north(row + 1), values[row], values[row + 1])
        side = flux(east(row), from_west(values[row]), values[row])
        result[row] = (above - below) + (side - from_east(side))
        above = below
    return result


def heun_rows(values, north, east):
    count = len(values)
    first = divergences(values, range(1, count - 1), north, east)
    predicted = {row: values[row] + first[row] for row in first}
    inner = range(2, count - 2)
    second = divergences(predicted, inner, north, east)
    return [0.5 * (values[row] + predicted[row] + second[row]) for row in inner]


def start_grid(fields_ref, winds_ref, grid_ref, sems):
    fields, tiles = fields_ref.shape[0], grid_ref.shape[1]

    def copy(array, tile, source):
        lanes = pl.ds(tile * LANES, LANES)
        return pltpu.make_async_copy(
            source.at[:, lanes], grid_ref.at[array, tile], sems.at[array, tile]
        )

    for wind in range(2):
        for tile in range(tiles):
            copy(fields + wind, tile, winds_ref.at[wind]).start()
    for field in range(fields):
        for tile in range(tiles):
            copy(field, tile, fields_ref.at[field]).start()

    def wait(array):
        for tile in range(tiles):
            copy(array, tile, fields_ref.at[0]).wait()

    return wait


def load_row(grid_ref, array, row, group, size, rows):
    start = group * (size * rows) + row
    pieces = [
        grid_ref[array, tile, pl.ds(start, size, stride=rows), :]
        for tile in range(grid_ref.shape[1])
    ]
    return jnp.concatenate(pieces, axis=1)


def store_weights(north_ref, east_ref, levels, east_winds, north_winds, wall=None):
    count = len(north_winds)
    for face in range(1, count):
        pair = face_weights(north_winds[face - 1], north_winds[face])
        for side in range(2):
            shut = wall is not None and wall[0] == face
            north_ref[face, side, levels, :] = pair[side] * wall[1] if shut else pair[side]
    for row in range(1, count - 1):
        pair = face_weights(from_west(east_winds[row]), east_winds[row])
        for side in range(2):
            east_ref[row, side, levels, :] = pair[side]


def keep_row(kept_ref, index, levels, value):
    for tile in range(value.shape[1] // LANES):
        kept_ref[tile, index, levels, :] = value[:, tile * LANES : (tile + 1) * LANES]


def clear_tail(kept_ref, tiles):
    for tile in range(tiles, kept_ref.shape[0]):
        kept_ref[tile] = jnp.zeros(kept_ref.shape[1:], kept_ref.dtype)


def slot_starts(counts_ref, owners):
    starts = []
    total = jnp.int32(0)
    for owner in range(owners):
        starts.append(total)
        total = total + counts_ref[0, owner]
    return starts


def pack_rows(kept_ref, starts, blocks, store):
    _, rows, levels, _ = kept_ref.shape
    lane = lax.broadcasted_iota(jnp.int32, (levels, LANES), 1)
    for slot, start in enumerate(starts):
        tile = start // LANES
        inside = start - tile * LANES
        shift = (LANES - inside) % LANES
        keep = lane < LANES - inside
        for row in range(rows):
            turned = [
                pltpu.roll(kept_ref[tile + j, row], shift, 1) for j in range(blocks + 1)
            ]
            for j in range(blocks):
                joined = jnp.where(keep, turned[j], turned[j + 1])
                store(slot, j, row, joined.astype(jnp.bfloat16))


def inner_kernel(
    rows,
    counts_ref,
    fields_ref,
    winds_ref,
    out_ref,
    grid_ref,
    north_ref,
    east_ref,
    kept_ref,
    sems,
    packed_ref,
    sent,
):
    fields = fields_ref.shape[0]
    owners, _, blocks, _, levels, _ = out_ref.shape
    size = min(8, levels)
    groups = levels // size
    wait = start_grid(fields_ref, winds_ref, grid_ref, sems)
    clear_tail(kept_ref, grid_ref.shape[1])
    starts = slot_starts(counts_ref, owners)

    def field_out(field):
        return pltpu.make_async_copy(packed_ref.at[field], out_ref.at[:, field], sent.at[field])

    wait(fields)
    wait(fields + 1)

    def weights(group, carry):
        east = [load_row(grid_ref, fields, row, group, size, rows) for row in range(rows)]
        north = [load_row(grid_ref, fields + 1, row, group, size, rows) for row in range(rows)]
        store_weights(north_ref, east_ref, pl.ds(group * size, size), east, north)
        return carry

    lax.fori_loop(0, groups, weights, 0)

    def one_field(field, carry):
        wait(field)

        def one_group(group, carry):
            place = pl.ds(group * size, size)
            values = [load_row(grid_ref, field, row, group, size, rows) for row in range(rows)]

            def north(face):
                return north_ref[face, 0, place, :], north_ref[face, 1, place, :]

            def east(row):
                return east_ref[row, 0, place, :], east_ref[row, 1, place, :]

            for index, value in enumerate(heun_rows(values, north, east)):
                keep_row(kept_ref, index, place, value)
            return carry

        lax.fori_loop(0, groups, one_group, 0)

        def store(slot, block, row, value):
            packed_ref[field, slot, block, row] = value

        pack_rows(kept_ref, starts, blocks, store)
        field_out(field).start()
        return carry

    lax.fori_loop(0, fields, one_field, 0)
    for field in range(fields):
        field_out(field).wait()


def halo_kernel(rows, fields_ref, winds_ref, first_ref, last_ref, grid_ref, sems):
    fields = fields_ref.shape[0]
    levels = first_ref.shape[2]
    size = min(8, levels)
    wait = start_grid(fields_ref, winds_ref, grid_ref, sems)
    for array in (fields, fields + 1) + tuple(range(fields)):
        wait(array)
        for group in range(levels // size):
            place = pl.ds(group * size, size)
            for row in range(HALO):
                last = rows - HALO + row
                first_ref[array, row, place, :] = load_row(grid_ref, array, row, group, size, rows)
                last_ref[array, row, place, :] = load_row(grid_ref, array, last, group, size, rows)


def edge_kernel(
    rows,
    split,
    counts_ref,
    place_ref,
    fields_ref,
    winds_ref,
    before_ref,
    after_ref,
    *refs,
):
    outs, (grid_ref, north_ref, east_ref, kept_ref, sems, start_ref) = refs[:-6], refs[-6:]
    early_refs, late_refs = outs[: len(outs) // 2], outs[len(outs) // 2 :]
    fields = fields_ref.shape[0]
    owners = start_ref.shape[0]
    blocks = split + late_refs[0].shape[-4]
    levels = before_ref.shape[2]
    size = min(8, levels)
    groups = levels // size
    wait = start_grid(fields_ref, winds_ref, grid_ref, sems)
    clear_tail(kept_ref, grid_ref.shape[1])
    for owner, start in enumerate(slot_starts(counts_ref, owners)):
        start_ref[owner] = start
    count = 3 * HALO

    def run(array, group, top):
        place = pl.ds(group * size, size)
        own = range(2 * HALO) if top else range(rows - 2 * HALO, rows)
        own = [load_row(grid_ref, array, row, group, size, rows) for row in own]
        if top:
            return [before_ref[array, row, place, :] for row in range(HALO)] + own
        return own + [after_ref[array, row, place, :] for row in range(HALO)]

    wait(fields)
    wait(fields + 1)
    for top in (True, False):
        north_side, east_side = north_ref.at[int(top)], east_ref.at[int(top)]
        wall = HALO if top else count - HALO
        is_open = jnp.where(place_ref[0 if top else 1] == 1, 0.0, 1.0)

        def weights(group, carry):
            store_weights(
                north_side,
                east_side,
                pl.ds(group * size, size),
                run(fields, group, top),
                run(fields + 1, group, top),
                (wall, is_open),
            )
            return carry

        lax.fori_loop(0, groups, weights, 0)

    def one_field(field, carry):
        wait(field)

        def one_group(group, carry):
            place = pl.ds(group * size, size)
            for top in (True, False):
                side = int(top)

                def north(face):
                    return north_ref[side, face, 0, place, :], north_ref[side, face, 1, place, :]

                def east(row):
                    return east_ref[side, row, 0, place, :], east_ref[side, row, 1, place, :]

                done = heun_rows(run(field, group, top), north, east)
                for index, value in enumerate(done):
                    keep_row(kept_ref, index + (0 if top else HALO), place, value)
            return carry

        lax.fori_loop(0, groups, one_group, 0)

        def store(slot, block, row, value):
            if block < split:
                early_refs[slot][field, block, row] = value
            elif early_refs:
                late_refs[slot][field, block - split, row] = value
            else:
                late_refs[0][slot, field, block, row] = value

        slots = [start_ref[place_ref[2] ^ turn] for turn in range(owners)]
        if not early_refs:
            slots = [start_ref[owner] for owner in range(owners)]
        pack_rows(kept_ref, slots, blocks, store)
        return carry

    lax.fori_loop(0, fields, one_field, 0)


def silu(x):
    half = 0.5 * x
    return half + half * jnp.tanh(half)


def dot(a, b):
    return jnp.dot(a, b, preferred_element_type=jnp.float32)


def gathered(block_ref, field):
    sources, _, _, rows = block_ref.shape[:4]
    by_row = [
        jnp.concatenate([block_ref[source, field, 0, row] for source in range(sources)], axis=0)
        for row in range(rows)
    ]
    return jnp.concatenate(by_row, axis=1)


def sort_turns(own, refs, sorted_ref):
    fields, _, rows, levels, _ = refs[0].shape
    for turn, ref in enumerate(refs):
        place = pl.ds(pl.multiple_of((own ^ turn) * levels, levels), levels)
        for field in range(fields):
            for row in range(rows):
                sorted_ref[field, place, row * LANES : (row + 1) * LANES] = ref[field, 0, row]


def column_update(columns, fields, remap_ref, first_ref, second_ref, third_ref):
    remapped = []
    for field in range(fields):
        values = columns(field)
        remapped.append(values.astype(jnp.float32) + dot(remap_ref[...], values))
    remapped = jnp.concatenate(remapped, axis=0)
    hidden = silu(dot(first_ref[...], remapped.astype(jnp.bfloat16))).astype(jnp.bfloat16)
    hidden = silu(dot(second_ref[...], hidden)).astype(jnp.bfloat16)
    tendency = dot(third_ref[...], hidden).astype(jnp.bfloat16).astype(jnp.float32)
    return remapped, tendency


def finished_row(remapped, tendency, listed, index, live):
    lanes = slice(index * LANES, (index + 1) * LANES)
    updated = remapped[:, lanes] + jnp.where(listed == 1, tendency[:, lanes], 0.0)
    return jnp.where(live, updated, 0.0)


def live_lanes(width_ref, features, block):
    lane = lax.broadcasted_iota(jnp.int32, (features, LANES), 1)
    return lane + block * LANES < width_ref[0]


def half_kernel(
    row_list,
    listed_ref,
    width_ref,
    block_ref,
    remap_ref,
    first_ref,
    second_ref,
    third_ref,
    out_ref,
    first_out,
    second_out,
    third_out,
):
    @pl.when(pl.program_id(0) == 0)
    def _():
        first_out[...] = first_ref[...].T
        second_out[...] = second_ref[...].T
        third_out[...] = third_ref[...].T

    remapped, tendency = column_update(
        functools.partial(gathered, block_ref),
        block_ref.shape[1],
        remap_ref,
        first_out,
        second_out,
        third_out,
    )
    live = live_lanes(width_ref, remapped.shape[0], pl.program_id(0))
    for index, row in enumerate(row_list):
        out_ref[index] = finished_row(remapped, tendency, listed_ref[row], index, live).astype(
            jnp.bfloat16
        )


def last_kernel(row_list, done_list, base, turns, listed_ref, width_ref, *refs):
    *refs, done_ref, remap_ref, first_ref, second_ref, third_ref, out_ref, tiles_ref, sorted_ref = (
        refs
    )
    features, rows, _ = out_ref.shape
    fields = sorted_ref.shape[0]
    if turns:
        sort_turns(width_ref[1], refs[-turns:], sorted_ref)

        def columns(field):
            return sorted_ref[field]
    else:
        columns = functools.partial(gathered, refs[-1])
    remapped, tendency = column_update(
        columns, fields, remap_ref, first_ref, second_ref, third_ref
    )
    live = live_lanes(width_ref, features, pl.program_id(0) + base)
    for index, row in enumerate(done_list):
        tiles_ref[pl.ds(row, features, stride=rows), :] = done_ref[index].astype(jnp.float32)
    for index, row in enumerate(row_list):
        tiles_ref[pl.ds(row, features, stride=rows), :] = finished_row(
            remapped, tendency, listed_ref[row], index, live
        )
    out_ref[...] = tiles_ref[...].reshape(features, rows, LANES).astype(jnp.bfloat16)


def shards(fields, winds, remap_weight, w_first, w_second, w_third, lon_counts, group_list):
    field_count, level_count, lat_rows, lon_total = fields.shape
    band_count = lax.axis_size("lat")
    band_index = lax.axis_index("lat")
    owner_count = lax.axis_size("lev")
    first_row = band_index * lat_rows
    all_levels = level_count * owner_count
    features = field_count * all_levels
    blocks = (2 * lon_total // owner_count + LANES - 1) // LANES
    slot_width = blocks * LANES
    split = blocks - 1
    inner_rows = tuple(range(HALO, lat_rows - HALO))
    edge_rows = tuple(range(HALO)) + tuple(range(lat_rows - HALO, lat_rows))
    half = len(inner_rows)
    stacked = field_count + 2
    tiles = lon_total // LANES
    smem = pl.BlockSpec(memory_space=pltpu.SMEM)
    anywhere = pl.BlockSpec(memory_space=pl.ANY)
    params = pltpu.CompilerParams(vmem_limit_bytes=60 * MIB)
    values = field_count * level_count * lat_rows * lon_total

    def payload(count):
        return (owner_count, field_count, count, half, level_count, LANES)

    flat_fields = fields.reshape(field_count, level_count * lat_rows, lon_total)
    flat_winds = winds.reshape(2, level_count * lat_rows, lon_total)
    halo_shape = jax.ShapeDtypeStruct((stacked, HALO, level_count, lon_total), jnp.float32)

    def scratch(sides, count):
        return [
            pltpu.VMEM((stacked, tiles, level_count * lat_rows, LANES), jnp.float32),
            pltpu.VMEM(sides + (count, 2, level_count, lon_total), jnp.float32),
            pltpu.VMEM(sides + (count - 1, 2, level_count, lon_total), jnp.float32),
            pltpu.VMEM((tiles + blocks, half, level_count, LANES), jnp.float32),
            pltpu.SemaphoreType.DMA((stacked, tiles)),
        ]

    inner = pl.pallas_call(
        functools.partial(inner_kernel, lat_rows),
        in_specs=[smem, anywhere, anywhere],
        out_specs=anywhere,
        out_shape=jax.ShapeDtypeStruct(payload(blocks), jnp.bfloat16),
        scratch_shapes=scratch((), lat_rows)
        + [
            pltpu.VMEM((field_count, owner_count) + payload(blocks)[2:], jnp.bfloat16),
            pltpu.SemaphoreType.DMA((field_count,)),
        ],
        compiler_params=params,
        cost_estimate=pl.CostEstimate(
            flops=40 * values, bytes_accessed=8 * values, transcendentals=0
        ),
        name="inner_rows",
    )(lon_counts, flat_fields, flat_winds)

    late_fields, late_winds, inner = lax.optimization_barrier((flat_fields, flat_winds, inner))
    first, last = pl.pallas_call(
        functools.partial(halo_kernel, lat_rows),
        in_specs=[anywhere, anywhere],
        out_shape=[halo_shape, halo_shape],
        scratch_shapes=[scratch((), lat_rows)[0], scratch((), lat_rows)[-1]],
        compiler_params=params,
        cost_estimate=pl.CostEstimate(
            flops=values, bytes_accessed=8 * values, transcendentals=0
        ),
        name="halo_rows",
    )(late_fields, late_winds)

    up = [(i, i + 1) for i in range(band_count - 1)]
    down = [(j, i) for i, j in up]

    def exchange(x):
        return lax.all_to_all(x, "lev", split_axis=0, concat_axis=0, tiled=True)

    inner_block = exchange(inner)
    before = lax.ppermute(last, "lat", up)
    after = lax.ppermute(first, "lat", down)

    own = lax.axis_index("lev")
    place = jnp.stack([band_index == 0, band_index == band_count - 1, own]).astype(jnp.int32)
    by_turn = split > 0
    if by_turn:
        edge_shapes = [payload(split)[1:]] * owner_count
        edge_shapes += [payload(blocks - split)[1:]] * owner_count
    else:
        edge_shapes = [payload(blocks)]
    edge = pl.pallas_call(
        functools.partial(edge_kernel, lat_rows, split),
        in_specs=[smem, smem, anywhere, anywhere] + [pl.BlockSpec(memory_space=pltpu.VMEM)] * 2,
        out_shape=[jax.ShapeDtypeStruct(shape, jnp.bfloat16) for shape in edge_shapes],
        scratch_shapes=scratch((2,), 3 * HALO) + [pltpu.SMEM((owner_count,), jnp.int32)],
        compiler_params=params,
        cost_estimate=pl.CostEstimate(
            flops=80 * values, bytes_accessed=10 * values, transcendentals=0
        ),
        name="edge_rows",
    )(lon_counts, place, late_fields, late_winds, before, after)

    def turned_exchange(x, turn):
        return lax.ppermute(x, "lev", [(i, i ^ turn) for i in range(owner_count)]) if turn else x

    if by_turn:
        early, late = list(edge[:owner_count]), list(edge[owner_count:])
        early = [turned_exchange(x, turn) for turn, x in enumerate(early)]
    else:
        early, late = [], edge

    listed = jnp.any(
        group_list[:, :, None] == (first_row + jnp.arange(lat_rows, dtype=jnp.int32))[None, None, :],
        axis=(0, 1),
    ).astype(jnp.int32)
    width = jnp.stack([lon_counts[0][own], own]).astype(jnp.int32)

    def by_level(block):
        if level_count % 16 == 0:
            return block
        return block.transpose(1, 2, 3, 0, 4, 5).reshape(
            1, field_count, block.shape[2], half, all_levels, LANES
        )

    def whole(shape):
        return pl.BlockSpec(shape, lambda i: (0,) * len(shape))

    def block_spec(block):
        return pl.BlockSpec(
            block.shape[:2] + (1,) + block.shape[3:], lambda i: (0, 0, i, 0, 0, 0)
        )

    def cost(count):
        columns = half * count * LANES
        return pl.CostEstimate(
            flops=2 * features * columns * (3 * w_first.shape[1] + all_levels),
            bytes_accessed=4 * features * columns,
            transcendentals=2 * w_first.shape[1] * columns,
        )

    weights = (w_first, w_second, w_third)
    weight_specs = [whole(w.shape) for w in (remap_weight,) + weights]
    inner_block = by_level(inner_block)
    done, *turned = pl.pallas_call(
        functools.partial(half_kernel, inner_rows),
        grid=(blocks,),
        in_specs=[smem, smem, block_spec(inner_block)] + weight_specs,
        out_specs=[pl.BlockSpec((half, features, LANES), lambda i: (0, 0, i))]
        + [whole(w.shape[::-1]) for w in weights],
        out_shape=[jax.ShapeDtypeStruct((half, features, slot_width), jnp.bfloat16)]
        + [jax.ShapeDtypeStruct(w.shape[::-1], w.dtype) for w in weights],
        compiler_params=params,
        cost_estimate=cost(blocks),
        name="inner_columns",
    )(listed, width, inner_block, remap_weight, *weights)

    if by_turn:
        for turn in range(1, owner_count):
            early[turn], late[turn], done = lax.optimization_barrier(
                (early[turn], late[turn], done)
            )
        late = [turned_exchange(x, turn) for turn, x in enumerate(late)]
    else:
        late = [by_level(exchange(late[0]))]
    out = None
    base = 0
    for part in ([early] if early else []) + [late]:
        turns = len(part) if by_turn else 0
        count = part[0].shape[1 if turns else 2]
        offset = base
        if turns:
            specs = [
                pl.BlockSpec((field_count, 1, half, level_count, LANES), lambda i: (0, i, 0, 0, 0))
            ] * len(part)
        else:
            specs = [block_spec(part[0])]
        out = pl.pallas_call(
            functools.partial(last_kernel, edge_rows, inner_rows, offset, turns),
            grid=(count,),
            in_specs=[smem, smem]
            + [anywhere] * (base > 0)
            + specs
            + [pl.BlockSpec((half, features, LANES), lambda i, o=offset: (0, 0, i + o))]
            + weight_specs,
            out_specs=pl.BlockSpec((features, lat_rows, LANES), lambda i, o=offset: (0, 0, i + o)),
            out_shape=jax.ShapeDtypeStruct((features, lat_rows, slot_width), jnp.bfloat16),
            scratch_shapes=[
                pltpu.VMEM((features * lat_rows, LANES), jnp.float32),
                pltpu.VMEM((field_count, all_levels, half * LANES), jnp.bfloat16),
            ],
            input_output_aliases={2: 0} if base > 0 else {},
            compiler_params=params,
            cost_estimate=cost(count),
            name="edge_columns",
        )(listed, width, *([out] if base > 0 else []), *part, done, remap_weight, *turned)
        base += count
    return out.reshape(field_count, all_levels, lat_rows, slot_width)


def solution(mesh):
    in_specs = (
        P(None, "lev", "lat", None),
        P(None, "lev", "lat", None),
        P(),
        P(),
        P(),
        P(),
        P("lat", None),
        P(),
    )
    out_specs = P(None, None, "lat", "lev")
    return jax.shard_map(shards, mesh=mesh, in_specs=in_specs, out_specs=out_specs, check_vma=False)
```

```python
import functools

import jax
import jax.numpy as jnp
from jax import lax
from jax.experimental import pallas as pl
from jax.experimental.pallas import tpu as pltpu
from jax.sharding import PartitionSpec as P

DIFFUSION = 0.15
LANES = 128
HALO = 2
MIB = 1024 * 1024


def from_west(x):
    return pltpu.roll(x, 1, 1)


def from_east(x):
    return pltpu.roll(x, x.shape[1] - 1, 1)


def flux(weights, before, after):
    return weights[0] * before + weights[1] * after


def face_weights(before, after):
    half = 0.25 * (before + after)
    return half + DIFFUSION, half - DIFFUSION


def divergences(values, rows, north, east):
    above = flux(north(rows[0]), values[rows[0] - 1], values[rows[0]])
    result = {}
    for row in rows:
        below = flux(north(row + 1), values[row], values[row + 1])
        side = flux(east(row), from_west(values[row]), values[row])
        result[row] = (above - below) + (side - from_east(side))
        above = below
    return result


def heun_rows(values, north, east):
    count = len(values)
    first = divergences(values, range(1, count - 1), north, east)
    predicted = {row: values[row] + first[row] for row in first}
    inner = range(2, count - 2)
    second = divergences(predicted, inner, north, east)
    return [0.5 * (values[row] + predicted[row] + second[row]) for row in inner]


def start_grid(fields_ref, winds_ref, grid_ref, sems):
    fields, tiles = fields_ref.shape[0], grid_ref.shape[1]

    def copy(array, tile, source):
        lanes = pl.ds(tile * LANES, LANES)
        return pltpu.make_async_copy(
            source.at[:, lanes], grid_ref.at[array, tile], sems.at[array, tile]
        )

    for wind in range(2):
        for tile in range(tiles):
            copy(fields + wind, tile, winds_ref.at[wind]).start()
    for field in range(fields):
        for tile in range(tiles):
            copy(field, tile, fields_ref.at[field]).start()

    def wait(array):
        for tile in range(tiles):
            copy(array, tile, fields_ref.at[0]).wait()

    return wait


def load_row(grid_ref, array, row, group, size, rows):
    start = group * (size * rows) + row
    pieces = [
        grid_ref[array, tile, pl.ds(start, size, stride=rows), :]
        for tile in range(grid_ref.shape[1])
    ]
    return jnp.concatenate(pieces, axis=1)


def store_weights(north_ref, east_ref, levels, east_winds, north_winds, wall=None):
    count = len(north_winds)
    for face in range(1, count):
        pair = face_weights(north_winds[face - 1], north_winds[face])
        for side in range(2):
            shut = wall is not None and wall[0] == face
            north_ref[face, side, levels, :] = pair[side] * wall[1] if shut else pair[side]
    for row in range(1, count - 1):
        pair = face_weights(from_west(east_winds[row]), east_winds[row])
        for side in range(2):
            east_ref[row, side, levels, :] = pair[side]


def keep_row(kept_ref, index, levels, value):
    for tile in range(value.shape[1] // LANES):
        kept_ref[tile, index, levels, :] = value[:, tile * LANES : (tile + 1) * LANES]


def clear_tail(kept_ref, tiles):
    for tile in range(tiles, kept_ref.shape[0]):
        kept_ref[tile] = jnp.zeros(kept_ref.shape[1:], kept_ref.dtype)


def slot_starts(counts_ref, owners):
    starts = []
    total = jnp.int32(0)
    for owner in range(owners):
        starts.append(total)
        total = total + counts_ref[0, owner]
    return starts


def pack_rows(kept_ref, starts, blocks, store):
    _, rows, levels, _ = kept_ref.shape
    lane = lax.broadcasted_iota(jnp.int32, (levels, LANES), 1)
    for slot, start in enumerate(starts):
        tile = start // LANES
        inside = start - tile * LANES
        shift = (LANES - inside) % LANES
        keep = lane < LANES - inside
        for row in range(rows):
            turned = [
                pltpu.roll(kept_ref[tile + j, row], shift, 1) for j in range(blocks + 1)
            ]
            for j in range(blocks):
                joined = jnp.where(keep, turned[j], turned[j + 1])
                store(slot, j, row, joined.astype(jnp.bfloat16))


def inner_kernel(
    rows,
    counts_ref,
    fields_ref,
    winds_ref,
    out_ref,
    grid_ref,
    north_ref,
    east_ref,
    kept_ref,
    sems,
    packed_ref,
    sent,
):
    fields = fields_ref.shape[0]
    owners, _, blocks, _, levels, _ = out_ref.shape
    size = min(8, levels)
    groups = levels // size
    wait = start_grid(fields_ref, winds_ref, grid_ref, sems)
    clear_tail(kept_ref, grid_ref.shape[1])
    starts = slot_starts(counts_ref, owners)

    def field_out(field):
        return pltpu.make_async_copy(packed_ref.at[field], out_ref.at[:, field], sent.at[field])

    wait(fields)
    wait(fields + 1)

    def weights(group, carry):
        east = [load_row(grid_ref, fields, row, group, size, rows) for row in range(rows)]
        north = [load_row(grid_ref, fields + 1, row, group, size, rows) for row in range(rows)]
        store_weights(north_ref, east_ref, pl.ds(group * size, size), east, north)
        return carry

    lax.fori_loop(0, groups, weights, 0)

    def one_field(field, carry):
        wait(field)

        def one_group(group, carry):
            place = pl.ds(group * size, size)
            values = [load_row(grid_ref, field, row, group, size, rows) for row in range(rows)]

            def north(face):
                return north_ref[face, 0, place, :], north_ref[face, 1, place, :]

            def east(row):
                return east_ref[row, 0, place, :], east_ref[row, 1, place, :]

            for index, value in enumerate(heun_rows(values, north, east)):
                keep_row(kept_ref, index, place, value)
            return carry

        lax.fori_loop(0, groups, one_group, 0)

        def store(slot, block, row, value):
            packed_ref[field, slot, block, row] = value

        pack_rows(kept_ref, starts, blocks, store)
        field_out(field).start()
        return carry

    lax.fori_loop(0, fields, one_field, 0)
    for field in range(fields):
        field_out(field).wait()


def halo_kernel(rows, fields_ref, winds_ref, first_ref, last_ref, grid_ref, sems):
    fields = fields_ref.shape[0]
    levels = first_ref.shape[2]
    size = min(8, levels)
    wait = start_grid(fields_ref, winds_ref, grid_ref, sems)
    for array in (fields, fields + 1) + tuple(range(fields)):
        wait(array)
        for row in range(HALO):
            for ref, source in ((first_ref, row), (last_ref, rows - HALO + row)):
                value = [
                    load_row(grid_ref, array, source, group, size, rows)
                    for group in range(levels // size)
                ]
                ref[array, row] = jnp.concatenate(value, axis=0).astype(ref.dtype)


def edge_kernel(
    rows,
    by_turn,
    counts_ref,
    fields_ref,
    winds_ref,
    before_ref,
    after_ref,
    *refs,
):
    outs, scratch = refs[:-7], refs[-7:]
    grid_ref, north_ref, east_ref, kept_ref, sems, start_ref, halo_ref = scratch
    fields = fields_ref.shape[0]
    owners = start_ref.shape[0]
    blocks = outs[0].shape[-4]
    levels = before_ref.shape[2]
    size = min(8, levels)
    groups = levels // size
    wait = start_grid(fields_ref, winds_ref, grid_ref, sems)
    clear_tail(kept_ref, grid_ref.shape[1])
    for owner, start in enumerate(slot_starts(counts_ref, owners)):
        start_ref[owner] = start
    count = 3 * HALO

    def run(array, group, top):
        own = range(2 * HALO) if top else range(rows - 2 * HALO, rows)
        own = [load_row(grid_ref, array, row, group, size, rows) for row in own]
        place = pl.ds(group * size, size)
        halo = [halo_ref[int(top), array, row, place, :] for row in range(HALO)]
        return halo + own if top else own + halo

    for side, ref in enumerate((after_ref, before_ref)):
        for array in range(fields + 2):
            for row in range(HALO):
                halo_ref[side, array, row] = ref[array, row].astype(jnp.float32)

    wait(fields)
    wait(fields + 1)
    for top in (True, False):
        north_side, east_side = north_ref.at[int(top)], east_ref.at[int(top)]
        wall = HALO if top else count - HALO
        band = lax.axis_index("lat")
        is_open = jnp.where(band == (0 if top else lax.axis_size("lat") - 1), 0.0, 1.0)

        def weights(group, carry):
            store_weights(
                north_side,
                east_side,
                pl.ds(group * size, size),
                run(fields, group, top),
                run(fields + 1, group, top),
                (wall, is_open),
            )
            return carry

        lax.fori_loop(0, groups, weights, 0)

    def one_field(field, carry):
        wait(field)

        def one_group(group, carry):
            place = pl.ds(group * size, size)
            for top in (True, False):
                side = int(top)

                def north(face):
                    return north_ref[side, face, 0, place, :], north_ref[side, face, 1, place, :]

                def east(row):
                    return east_ref[side, row, 0, place, :], east_ref[side, row, 1, place, :]

                done = heun_rows(run(field, group, top), north, east)
                for index, value in enumerate(done):
                    keep_row(kept_ref, index + (0 if top else HALO), place, value)
            return carry

        lax.fori_loop(0, groups, one_group, 0)

        def store(slot, block, row, value):
            if by_turn:
                outs[slot][field, block, row] = value
            else:
                outs[0][slot, field, block, row] = value

        own = lax.axis_index("lev") if by_turn else 0
        slots = [start_ref[own ^ turn] for turn in range(owners)]
        pack_rows(kept_ref, slots, blocks, store)
        return carry

    lax.fori_loop(0, fields, one_field, 0)


def silu(x):
    half = 0.5 * x
    return half + half * jnp.tanh(half)


def dot(a, b):
    return jnp.dot(a, b, preferred_element_type=jnp.float32)


def gathered(block_ref, field):
    sources, _, _, rows = block_ref.shape[:4]
    by_row = [
        jnp.concatenate([block_ref[source, field, 0, row] for source in range(sources)], axis=0)
        for row in range(rows)
    ]
    return jnp.concatenate(by_row, axis=1)


def sort_turns(own, refs, sorted_ref):
    fields, _, rows, levels, _ = refs[0].shape
    for turn, ref in enumerate(refs):
        place = pl.ds(pl.multiple_of((own ^ turn) * levels, levels), levels)
        for field in range(fields):
            for row in range(rows):
                sorted_ref[field, place, row * LANES : (row + 1) * LANES] = ref[field, 0, row]


def column_update(columns, fields, remap_ref, first_ref, second_ref, third_ref):
    remapped = []
    for field in range(fields):
        values = columns(field)
        remapped.append(values.astype(jnp.float32) + dot(remap_ref[...], values))
    remapped = jnp.concatenate(remapped, axis=0)
    hidden = silu(dot(first_ref[...], remapped.astype(jnp.bfloat16))).astype(jnp.bfloat16)
    hidden = silu(dot(second_ref[...], hidden)).astype(jnp.bfloat16)
    tendency = dot(third_ref[...], hidden).astype(jnp.bfloat16).astype(jnp.float32)
    return remapped, tendency


def finished_row(remapped, tendency, listed, index, live):
    lanes = slice(index * LANES, (index + 1) * LANES)
    updated = remapped[:, lanes] + jnp.where(listed, tendency[:, lanes], 0.0)
    return jnp.where(live, updated, 0.0)


def live_lanes(counts_ref, features, block):
    lane = lax.broadcasted_iota(jnp.int32, (features, LANES), 1)
    return lane + block * LANES < counts_ref[0, lax.axis_index("lev")]


def is_listed(groups_ref, row):
    found = jnp.bool_(False)
    for owner in range(groups_ref.shape[0]):
        for index in range(groups_ref.shape[1]):
            found = found | (groups_ref[owner, index] == row)
    return found


def half_kernel(
    rows,
    row_list,
    groups_ref,
    counts_ref,
    block_ref,
    remap_ref,
    first_ref,
    second_ref,
    third_ref,
    out_ref,
    first_out,
    second_out,
    third_out,
):
    @pl.when(pl.program_id(0) == 0)
    def _():
        first_out[...] = first_ref[...].T
        second_out[...] = second_ref[...].T
        third_out[...] = third_ref[...].T

    remapped, tendency = column_update(
        functools.partial(gathered, block_ref),
        block_ref.shape[1],
        remap_ref,
        first_out,
        second_out,
        third_out,
    )
    live = live_lanes(counts_ref, remapped.shape[0], pl.program_id(0))
    first_row = lax.axis_index("lat") * rows
    for index, row in enumerate(row_list):
        listed = is_listed(groups_ref, first_row + row)
        updated = finished_row(remapped, tendency, listed, index, live)
        out_ref[index] = updated.astype(jnp.bfloat16)


def last_kernel(row_list, done_list, by_turn, groups_ref, counts_ref, *refs):
    *refs, done_ref, remap_ref, first_ref, second_ref, third_ref, out_ref, tiles_ref, sorted_ref = (
        refs
    )
    features, rows, _ = out_ref.shape
    fields = sorted_ref.shape[0]
    if by_turn:
        sort_turns(lax.axis_index("lev"), refs, sorted_ref)

        def columns(field):
            return sorted_ref[field]
    else:
        columns = functools.partial(gathered, refs[0])
    remapped, tendency = column_update(
        columns, fields, remap_ref, first_ref, second_ref, third_ref
    )
    live = live_lanes(counts_ref, features, pl.program_id(0))
    first_row = lax.axis_index("lat") * rows
    for index, row in enumerate(done_list):
        tiles_ref[pl.ds(row, features, stride=rows), :] = done_ref[index].astype(jnp.float32)
    for index, row in enumerate(row_list):
        listed = is_listed(groups_ref, first_row + row)
        tiles_ref[pl.ds(row, features, stride=rows), :] = finished_row(
            remapped, tendency, listed, index, live
        )
    out_ref[...] = tiles_ref[...].reshape(features, rows, LANES).astype(jnp.bfloat16)


def shards(fields, winds, remap_weight, w_first, w_second, w_third, lon_counts, group_list):
    field_count, level_count, lat_rows, lon_total = fields.shape
    band_count = lax.axis_size("lat")
    owner_count = lax.axis_size("lev")
    all_levels = level_count * owner_count
    features = field_count * all_levels
    blocks = (2 * lon_total // owner_count + LANES - 1) // LANES
    slot_width = blocks * LANES
    inner_rows = tuple(range(HALO, lat_rows - HALO))
    edge_rows = tuple(range(HALO)) + tuple(range(lat_rows - HALO, lat_rows))
    half = len(inner_rows)
    stacked = field_count + 2
    tiles = lon_total // LANES
    smem = pl.BlockSpec(memory_space=pltpu.SMEM)
    anywhere = pl.BlockSpec(memory_space=pl.ANY)
    params = pltpu.CompilerParams(vmem_limit_bytes=60 * MIB)
    light = pltpu.CompilerParams(vmem_limit_bytes=24 * MIB)
    values = field_count * level_count * lat_rows * lon_total

    def payload(count):
        return (owner_count, field_count, count, half, level_count, LANES)

    flat_fields = fields.reshape(field_count, level_count * lat_rows, lon_total)
    flat_winds = winds.reshape(2, level_count * lat_rows, lon_total)
    halo_shape = jax.ShapeDtypeStruct((stacked, HALO, level_count, lon_total), jnp.bfloat16)

    def scratch(sides, count):
        return [
            pltpu.VMEM((stacked, tiles, level_count * lat_rows, LANES), jnp.float32),
            pltpu.VMEM(sides + (count, 2, level_count, lon_total), jnp.float32),
            pltpu.VMEM(sides + (count - 1, 2, level_count, lon_total), jnp.float32),
            pltpu.VMEM((tiles + blocks, half, level_count, LANES), jnp.float32),
            pltpu.SemaphoreType.DMA((stacked, tiles)),
        ]

    inner = pl.pallas_call(
        functools.partial(inner_kernel, lat_rows),
        in_specs=[smem, anywhere, anywhere],
        out_specs=anywhere,
        out_shape=jax.ShapeDtypeStruct(payload(blocks), jnp.bfloat16),
        scratch_shapes=scratch((), lat_rows)
        + [
            pltpu.VMEM((field_count, owner_count) + payload(blocks)[2:], jnp.bfloat16),
            pltpu.SemaphoreType.DMA((field_count,)),
        ],
        compiler_params=params,
        cost_estimate=pl.CostEstimate(
            flops=40 * values, bytes_accessed=8 * values, transcendentals=0
        ),
        name="inner_rows",
    )(lon_counts, flat_fields, flat_winds)

    late_fields, late_winds, inner = lax.optimization_barrier((flat_fields, flat_winds, inner))
    first, last = pl.pallas_call(
        functools.partial(halo_kernel, lat_rows),
        in_specs=[anywhere, anywhere],
        out_shape=[halo_shape, halo_shape],
        scratch_shapes=[scratch((), lat_rows)[0], scratch((), lat_rows)[-1]],
        compiler_params=params,
        cost_estimate=pl.CostEstimate(
            flops=values, bytes_accessed=8 * values, transcendentals=0
        ),
        name="halo_rows",
    )(late_fields, late_winds)

    up = [(i, i + 1) for i in range(band_count - 1)]
    down = [(j, i) for i, j in up]

    def exchange(x):
        return lax.all_to_all(x, "lev", split_axis=0, concat_axis=0, tiled=True)

    inner_block = exchange(inner)
    before = lax.ppermute(last, "lat", up)
    after = lax.ppermute(first, "lat", down)

    by_turn = owner_count == 8
    edge_shapes = [payload(blocks)[1:]] * owner_count if by_turn else [payload(blocks)]
    edge = pl.pallas_call(
        functools.partial(edge_kernel, lat_rows, by_turn),
        in_specs=[smem, anywhere, anywhere] + [pl.BlockSpec(memory_space=pltpu.VMEM)] * 2,
        out_shape=[jax.ShapeDtypeStruct(shape, jnp.bfloat16) for shape in edge_shapes],
        scratch_shapes=scratch((2,), 3 * HALO)
        + [
            pltpu.SMEM((owner_count,), jnp.int32),
            pltpu.VMEM((2,) + halo_shape.shape, jnp.float32),
        ],
        compiler_params=params,
        cost_estimate=pl.CostEstimate(
            flops=80 * values, bytes_accessed=10 * values, transcendentals=0
        ),
        name="edge_rows",
    )(lon_counts, late_fields, late_winds, before, after)

    if by_turn:
        edge = [
            lax.ppermute(x, "lev", [(i, i ^ turn) for i in range(owner_count)]) if turn else x
            for turn, x in enumerate(edge)
        ]
    else:
        edge = [exchange(edge[0])]

    def by_level(block):
        if level_count % 16 == 0:
            return block
        return block.transpose(1, 2, 3, 0, 4, 5).reshape(
            1, field_count, block.shape[2], half, all_levels, LANES
        )

    def whole(shape):
        return pl.BlockSpec(shape, lambda i: (0,) * len(shape))

    def block_spec(block):
        return pl.BlockSpec(
            block.shape[:2] + (1,) + block.shape[3:], lambda i: (0, 0, i, 0, 0, 0)
        )

    def cost(count):
        columns = half * count * LANES
        return pl.CostEstimate(
            flops=2 * features * columns * (3 * w_first.shape[1] + all_levels),
            bytes_accessed=4 * features * columns,
            transcendentals=2 * w_first.shape[1] * columns,
        )

    weights = (w_first, w_second, w_third)
    weight_specs = [pl.BlockSpec(memory_space=pltpu.VMEM)] * 4
    inner_block = by_level(inner_block)
    done, *turned = pl.pallas_call(
        functools.partial(half_kernel, lat_rows, inner_rows),
        grid=(blocks,),
        in_specs=[smem, smem, block_spec(inner_block)] + weight_specs,
        out_specs=[pl.BlockSpec((half, features, LANES), lambda i: (0, 0, i))]
        + [whole(w.shape[::-1]) for w in weights],
        out_shape=[jax.ShapeDtypeStruct((half, features, slot_width), jnp.bfloat16)]
        + [jax.ShapeDtypeStruct(w.shape[::-1], w.dtype) for w in weights],
        compiler_params=light,
        cost_estimate=cost(blocks),
        name="inner_columns",
    )(group_list, lon_counts, inner_block, remap_weight, *weights)

    if by_turn:
        edge_specs = [
            pl.BlockSpec((field_count, 1, half, level_count, LANES), lambda i: (0, i, 0, 0, 0))
        ] * owner_count
    else:
        edge = [by_level(edge[0])]
        edge_specs = [block_spec(edge[0])]
    out = pl.pallas_call(
        functools.partial(last_kernel, edge_rows, inner_rows, by_turn),
        grid=(blocks,),
        in_specs=[smem, smem]
        + edge_specs
        + [pl.BlockSpec((half, features, LANES), lambda i: (0, 0, i))]
        + weight_specs,
        out_specs=pl.BlockSpec((features, lat_rows, LANES), lambda i: (0, 0, i)),
        out_shape=jax.ShapeDtypeStruct((features, lat_rows, slot_width), jnp.bfloat16),
        scratch_shapes=[
            pltpu.VMEM((features * lat_rows, LANES), jnp.float32),
            pltpu.VMEM((field_count, all_levels, half * LANES), jnp.bfloat16),
        ],
        compiler_params=light,
        cost_estimate=cost(blocks),
        name="edge_columns",
    )(group_list, lon_counts, *edge, done, remap_weight, *turned)
    return out.reshape(field_count, all_levels, lat_rows, slot_width)


def solution(mesh):
    in_specs = (
        P(None, "lev", "lat", None),
        P(None, "lev", "lat", None),
        P(),
        P(),
        P(),
        P(),
        P("lat", None),
        P(),
    )
    out_specs = P(None, None, "lat", "lev")
    return jax.shard_map(shards, mesh=mesh, in_specs=in_specs, out_specs=out_specs, check_vma=False)
```

```python
import functools

import jax
import jax.numpy as jnp
from jax import lax
from jax.experimental import pallas as pl
from jax.experimental.pallas import tpu as pltpu
from jax.sharding import PartitionSpec as P

DIFFUSION = 0.15
LANES = 128
HALO = 2
MIB = 1024 * 1024


def from_west(x):
    return pltpu.roll(x, 1, 1)


def from_east(x):
    return pltpu.roll(x, x.shape[1] - 1, 1)


def face_weights(before, after):
    half = 0.25 * (before + after)
    return half + DIFFUSION, half - DIFFUSION


def step_rows(values, rows, weights):
    result = {}
    for row in rows:
        here, west, away, above, below = weights(row)
        side = west * from_west(values[row]) + away * from_east(values[row])
        across = above * values[row - 1] + below * values[row + 1]
        result[row] = here * values[row] + (side + across)
    return result


def heun_rows(values, weights):
    count = len(values)
    predicted = step_rows(values, range(1, count - 1), weights)
    stepped = step_rows(predicted, range(2, count - 2), weights)
    return [0.5 * (values[row] + stepped[row]) for row in stepped]


def start_grid(fields_ref, winds_ref, grid_ref, sems):
    fields, tiles = fields_ref.shape[0], grid_ref.shape[1]

    def copy(array, tile, source):
        lanes = pl.ds(tile * LANES, LANES)
        return pltpu.make_async_copy(
            source.at[:, lanes], grid_ref.at[array, tile], sems.at[array, tile]
        )

    for wind in range(2):
        for tile in range(tiles):
            copy(fields + wind, tile, winds_ref.at[wind]).start()
    for field in range(fields):
        for tile in range(tiles):
            copy(field, tile, fields_ref.at[field]).start()

    def wait(array):
        for tile in range(tiles):
            copy(array, tile, fields_ref.at[0]).wait()

    return wait


def load_row(grid_ref, array, row, group, size, rows):
    start = group * (size * rows) + row
    pieces = [
        grid_ref[array, tile, pl.ds(start, size, stride=rows), :]
        for tile in range(grid_ref.shape[1])
    ]
    return jnp.concatenate(pieces, axis=1)


def store_weights(weight_ref, levels, east_winds, north_winds, wall=None):
    count = len(north_winds)
    faces = {}
    for face in range(1, count):
        pair = face_weights(north_winds[face - 1], north_winds[face])
        shut = wall is not None and wall[0] == face
        faces[face] = [part * wall[1] for part in pair] if shut else pair
    for row in range(1, count - 1):
        west, own = face_weights(from_west(east_winds[row]), east_winds[row])
        here = 1.0 + (own - from_east(west)) + (faces[row][1] - faces[row + 1][0])
        parts = (here, west, -from_east(own), faces[row][0], -faces[row + 1][1])
        for part, value in enumerate(parts):
            weight_ref[row, part, levels, :] = value


def keep_row(kept_ref, index, levels, value):
    for tile in range(value.shape[1] // LANES):
        kept_ref[tile, index, levels, :] = value[:, tile * LANES : (tile + 1) * LANES]


def clear_tail(kept_ref, tiles):
    for tile in range(tiles, kept_ref.shape[0]):
        kept_ref[tile] = jnp.zeros(kept_ref.shape[1:], kept_ref.dtype)


def keep_starts(counts_ref, start_ref):
    total = jnp.int32(0)
    for owner in range(start_ref.shape[0]):
        start_ref[owner] = total
        total = total + counts_ref[0, owner]


def turned_starts(start_ref, by_turn, slots):
    own = lax.axis_index("lev") if by_turn else 0
    return [start_ref[own ^ turn] for turn in range(slots)]


def pack_rows(kept_ref, starts, blocks, store):
    _, rows, levels, _ = kept_ref.shape
    lane = lax.broadcasted_iota(jnp.int32, (levels, LANES), 1)
    for slot, start in enumerate(starts):
        tile = start // LANES
        inside = start - tile * LANES
        shift = (LANES - inside) % LANES
        keep = lane < LANES - inside
        for row in range(rows):
            turned = [
                pltpu.roll(kept_ref[tile + j, row], shift, 1) for j in range(blocks + 1)
            ]
            for j in range(blocks):
                joined = jnp.where(keep, turned[j], turned[j + 1])
                store(slot, j, row, joined.astype(jnp.bfloat16))


def inner_kernel(
    rows,
    by_turn,
    counts_ref,
    fields_ref,
    winds_ref,
    *refs,
):
    outs, scratch = refs[:-9], refs[-9:]
    grid_ref, weight_ref, kept_ref, sems = scratch[:4]
    start_ref, packed_ref, raw_ref, halo_ref, sent = scratch[4:]
    *outs, first_ref, last_ref = outs
    fields = fields_ref.shape[0]
    owners = start_ref.shape[0]
    _, slots, blocks, _, levels, _ = packed_ref.shape
    tiles = grid_ref.shape[1]
    size = min(8, levels)
    groups = levels // size
    wait = start_grid(fields_ref, winds_ref, grid_ref, sems)
    clear_tail(kept_ref, grid_ref.shape[1])
    keep_starts(counts_ref, start_ref)

    def field_out(field):
        if not by_turn:
            return [
                pltpu.make_async_copy(
                    packed_ref.at[field], outs[0].at[:, field], sent.at[field, 0]
                )
            ]
        copies = [
            pltpu.make_async_copy(
                packed_ref.at[field, slot], outs[slot].at[field], sent.at[field, slot]
            )
            for slot in range(slots)
        ]
        copies.append(
            pltpu.make_async_copy(raw_ref.at[field], outs[slots].at[field], sent.at[field, slots])
        )
        return copies

    def keep_halo(array):
        for row in range(HALO):
            for side, source in enumerate((row, rows - HALO + row)):
                value = [
                    load_row(grid_ref, array, source, group, size, rows) for group in range(groups)
                ]
                halo_ref[side, array, row] = jnp.concatenate(value, axis=0).astype(halo_ref.dtype)

    def halo_out(array):
        return [
            pltpu.make_async_copy(
                halo_ref.at[side, array], ref.at[array], sent.at[array, slots + 1 + side]
            )
            for side, ref in enumerate((first_ref, last_ref))
        ]

    wait(fields)
    wait(fields + 1)

    def weights(group, carry):
        east = [load_row(grid_ref, fields, row, group, size, rows) for row in range(rows)]
        north = [load_row(grid_ref, fields + 1, row, group, size, rows) for row in range(rows)]
        store_weights(weight_ref, pl.ds(group * size, size), east, north)
        return carry

    lax.fori_loop(0, groups, weights, 0)
    for array in (fields, fields + 1):
        keep_halo(array)
        for copy in halo_out(array):
            copy.start()

    def one_field(field, carry):
        wait(field)
        keep_halo(field)

        def one_group(group, carry):
            place = pl.ds(group * size, size)
            values = [load_row(grid_ref, field, row, group, size, rows) for row in range(rows)]

            def row_weights(row):
                return [weight_ref[row, part, place, :] for part in range(5)]

            for index, value in enumerate(heun_rows(values, row_weights)):
                keep_row(kept_ref, index, place, value)
            return carry

        lax.fori_loop(0, groups, one_group, 0)

        def store(slot, block, row, value):
            packed_ref[field, slot, block, row] = value

        if by_turn:
            for tile in range(tiles):
                raw_ref[field, tile] = kept_ref[tile].astype(raw_ref.dtype)
        pack_rows(kept_ref, turned_starts(start_ref, by_turn, slots), blocks, store)
        for copy in halo_out(field) + field_out(field):
            copy.start()
        return carry

    lax.fori_loop(0, fields, one_field, 0)
    for field in range(fields):
        for copy in field_out(field):
            copy.wait()
    for array in range(fields + 2):
        for copy in halo_out(array):
            copy.wait()


def mirror_kernel(counts_ref, raw_ref, *refs):
    outs, (kept_ref, start_ref) = refs[:-2], refs[-2:]
    fields, tiles = raw_ref.shape[:2]
    keep_starts(counts_ref, start_ref)
    clear_tail(kept_ref, tiles)

    def one_field(field, carry):
        for tile in range(tiles):
            kept_ref[tile] = raw_ref[field, tile].astype(jnp.float32)

        def store(slot, block, row, value):
            outs[slot][field, block, row] = value

        starts = turned_starts(start_ref, True, len(outs))
        pack_rows(kept_ref, starts, outs[0].shape[1], store)
        return carry

    lax.fori_loop(0, fields, one_field, 0)


def edge_kernel(
    rows,
    by_turn,
    counts_ref,
    fields_ref,
    winds_ref,
    before_ref,
    after_ref,
    *refs,
):
    outs, scratch = refs[:-6], refs[-6:]
    grid_ref, weight_ref, kept_ref, sems, start_ref, halo_ref = scratch
    fields = fields_ref.shape[0]
    owners = start_ref.shape[0]
    blocks = outs[0].shape[-4]
    levels = before_ref.shape[2]
    size = min(8, levels)
    groups = levels // size
    wait = start_grid(fields_ref, winds_ref, grid_ref, sems)
    clear_tail(kept_ref, grid_ref.shape[1])
    keep_starts(counts_ref, start_ref)
    count = 3 * HALO

    def run(array, group, top):
        own = range(2 * HALO) if top else range(rows - 2 * HALO, rows)
        own = [load_row(grid_ref, array, row, group, size, rows) for row in own]
        place = pl.ds(group * size, size)
        halo = [halo_ref[int(top), array, row, place, :] for row in range(HALO)]
        return halo + own if top else own + halo

    for side, ref in enumerate((after_ref, before_ref)):
        for array in range(fields + 2):
            for row in range(HALO):
                halo_ref[side, array, row] = ref[array, row].astype(jnp.float32)

    wait(fields)
    wait(fields + 1)
    for top in (True, False):
        wall = HALO if top else count - HALO
        band = lax.axis_index("lat")
        is_open = jnp.where(band == (0 if top else lax.axis_size("lat") - 1), 0.0, 1.0)

        def weights(group, carry):
            store_weights(
                weight_ref.at[int(top)],
                pl.ds(group * size, size),
                run(fields, group, top),
                run(fields + 1, group, top),
                (wall, is_open),
            )
            return carry

        lax.fori_loop(0, groups, weights, 0)

    def one_field(field, carry):
        wait(field)

        def one_group(group, carry):
            place = pl.ds(group * size, size)
            for top in (True, False):
                side = int(top)

                def row_weights(row):
                    return [weight_ref[side, row, part, place, :] for part in range(5)]

                done = heun_rows(run(field, group, top), row_weights)
                for index, value in enumerate(done):
                    keep_row(kept_ref, index + (0 if top else HALO), place, value)
            return carry

        lax.fori_loop(0, groups, one_group, 0)

        def store(slot, block, row, value):
            if by_turn:
                outs[slot][field, block, row] = value
            else:
                outs[0][slot, field, block, row] = value

        pack_rows(kept_ref, turned_starts(start_ref, by_turn, owners), blocks, store)
        return carry

    lax.fori_loop(0, fields, one_field, 0)


def silu(x):
    half = 0.5 * x
    return half + half * jnp.tanh(half)


def dot(a, b):
    return jnp.dot(a, b, preferred_element_type=jnp.float32)


def gathered(block_ref, field):
    sources, _, _, rows = block_ref.shape[:4]
    by_row = [
        jnp.concatenate([block_ref[source, field, 0, row] for source in range(sources)], axis=0)
        for row in range(rows)
    ]
    return jnp.concatenate(by_row, axis=1)


def sort_turns(own, refs, sorted_ref):
    fields, _, rows, levels, _ = refs[0].shape
    for turn, ref in enumerate(refs):
        place = pl.ds(pl.multiple_of((own ^ turn) * levels, levels), levels)
        for field in range(fields):
            for row in range(rows):
                sorted_ref[field, place, row * LANES : (row + 1) * LANES] = ref[field, 0, row]


def column_update(columns, fields, remap_ref, first_ref, second_ref, third_ref):
    remapped = []
    for field in range(fields):
        values = columns(field)
        remapped.append(values.astype(jnp.float32) + dot(remap_ref[...], values))
    remapped = jnp.concatenate(remapped, axis=0)
    hidden = silu(dot(first_ref[...], remapped.astype(jnp.bfloat16))).astype(jnp.bfloat16)
    hidden = silu(dot(second_ref[...], hidden)).astype(jnp.bfloat16)
    tendency = dot(third_ref[...], hidden).astype(jnp.bfloat16).astype(jnp.float32)
    return remapped, tendency


def finished_row(remapped, tendency, listed, index, live):
    lanes = slice(index * LANES, (index + 1) * LANES)
    updated = remapped[:, lanes] + jnp.where(listed, tendency[:, lanes], 0.0)
    return jnp.where(live, updated, 0.0)


def live_lanes(counts_ref, features, block):
    lane = lax.broadcasted_iota(jnp.int32, (features, LANES), 1)
    return lane + block * LANES < counts_ref[0, lax.axis_index("lev")]


def is_listed(groups_ref, row):
    found = jnp.bool_(False)
    for owner in range(groups_ref.shape[0]):
        for index in range(groups_ref.shape[1]):
            found = found | (groups_ref[owner, index] == row)
    return found


def column_source(by_turn, refs, sorted_ref):
    if not by_turn:
        return functools.partial(gathered, refs[0])
    sort_turns(lax.axis_index("lev"), refs, sorted_ref)
    return lambda field: sorted_ref[field]


def half_kernel(rows, row_list, by_turn, groups_ref, counts_ref, *refs):
    out_ref, first_out, second_out, third_out, sorted_ref = refs[-5:]
    *refs, remap_ref, first_ref, second_ref, third_ref = refs[:-5]

    @pl.when(pl.program_id(0) == 0)
    def _():
        first_out[...] = first_ref[...].T
        second_out[...] = second_ref[...].T
        third_out[...] = third_ref[...].T

    columns = column_source(by_turn, refs, sorted_ref)
    fields = sorted_ref.shape[0]
    remapped, tendency = column_update(
        columns, fields, remap_ref, first_out, second_out, third_out
    )
    live = live_lanes(counts_ref, remapped.shape[0], pl.program_id(0))
    first_row = lax.axis_index("lat") * rows
    for index, row in enumerate(row_list):
        listed = is_listed(groups_ref, first_row + row)
        updated = finished_row(remapped, tendency, listed, index, live)
        out_ref[index] = updated.astype(jnp.bfloat16)


def last_kernel(row_list, done_list, by_turn, groups_ref, counts_ref, *refs):
    *refs, done_ref, remap_ref, first_ref, second_ref, third_ref, out_ref, tiles_ref, sorted_ref = (
        refs
    )
    features, rows, _ = out_ref.shape
    fields = sorted_ref.shape[0]
    columns = column_source(by_turn, refs, sorted_ref)
    remapped, tendency = column_update(
        columns, fields, remap_ref, first_ref, second_ref, third_ref
    )
    live = live_lanes(counts_ref, features, pl.program_id(0))
    first_row = lax.axis_index("lat") * rows
    for index, row in enumerate(done_list):
        tiles_ref[pl.ds(row, features, stride=rows), :] = done_ref[index].astype(jnp.float32)
    for index, row in enumerate(row_list):
        listed = is_listed(groups_ref, first_row + row)
        tiles_ref[pl.ds(row, features, stride=rows), :] = finished_row(
            remapped, tendency, listed, index, live
        )
    out_ref[...] = tiles_ref[...].reshape(features, rows, LANES).astype(jnp.bfloat16)


def shards(fields, winds, remap_weight, w_first, w_second, w_third, lon_counts, group_list):
    field_count, level_count, lat_rows, lon_total = fields.shape
    band_count = lax.axis_size("lat")
    owner_count = lax.axis_size("lev")
    all_levels = level_count * owner_count
    features = field_count * all_levels
    blocks = (2 * lon_total // owner_count + LANES - 1) // LANES
    slot_width = blocks * LANES
    inner_rows = tuple(range(HALO, lat_rows - HALO))
    edge_rows = tuple(range(HALO)) + tuple(range(lat_rows - HALO, lat_rows))
    half = len(inner_rows)
    stacked = field_count + 2
    tiles = lon_total // LANES
    smem = pl.BlockSpec(memory_space=pltpu.SMEM)
    anywhere = pl.BlockSpec(memory_space=pl.ANY)
    params = pltpu.CompilerParams(vmem_limit_bytes=60 * MIB)
    light = pltpu.CompilerParams(vmem_limit_bytes=24 * MIB)
    values = field_count * level_count * lat_rows * lon_total

    def payload(count):
        return (owner_count, field_count, count, half, level_count, LANES)

    flat_fields = fields.reshape(field_count, level_count * lat_rows, lon_total)
    flat_winds = winds.reshape(2, level_count * lat_rows, lon_total)
    halo_shape = jax.ShapeDtypeStruct((stacked, HALO, level_count, lon_total), jnp.bfloat16)

    def scratch(sides, count):
        return [
            pltpu.VMEM((stacked, tiles, level_count * lat_rows, LANES), jnp.float32),
            pltpu.VMEM(sides + (count - 1, 5, level_count, lon_total), jnp.float32),
            pltpu.VMEM((tiles + blocks, half, level_count, LANES), jnp.float32),
            pltpu.SemaphoreType.DMA((stacked, tiles)),
        ]

    by_turn = owner_count == 8
    near = owner_count // 2
    slots = near if by_turn else owner_count
    raw_shape = (field_count, tiles, half, level_count, LANES)
    piece = jax.ShapeDtypeStruct(payload(blocks)[1:], jnp.bfloat16)
    whole_payload = jax.ShapeDtypeStruct(payload(blocks), jnp.bfloat16)
    raw = jax.ShapeDtypeStruct(raw_shape, jnp.bfloat16)
    inner_shapes = [piece] * near + [raw] if by_turn else [whole_payload]
    starts_scratch = pltpu.SMEM((owner_count,), jnp.int32)
    *inner, first, last = pl.pallas_call(
        functools.partial(inner_kernel, lat_rows, by_turn),
        in_specs=[smem, anywhere, anywhere],
        out_specs=[anywhere] * (len(inner_shapes) + 2),
        out_shape=inner_shapes + [halo_shape, halo_shape],
        scratch_shapes=scratch((), lat_rows)
        + [
            starts_scratch,
            pltpu.VMEM((field_count, slots) + payload(blocks)[2:], jnp.bfloat16),
            pltpu.VMEM(raw_shape, jnp.bfloat16),
            pltpu.VMEM((2,) + halo_shape.shape, halo_shape.dtype),
            pltpu.SemaphoreType.DMA((stacked, slots + 3)),
        ],
        compiler_params=params,
        cost_estimate=pl.CostEstimate(flops=1, bytes_accessed=1, transcendentals=0),
        name="inner_rows",
    )(lon_counts, flat_fields, flat_winds)

    up = [(i, i + 1) for i in range(band_count - 1)]
    down = [(j, i) for i, j in up]

    def exchange(x):
        return lax.all_to_all(x, "lev", split_axis=0, concat_axis=0, tiled=True)

    def turned_exchange(x, turn):
        return lax.ppermute(x, "lev", [(i, i ^ turn) for i in range(owner_count)]) if turn else x

    if by_turn:
        crossed = turned_exchange(inner[near], near)
        inner_parts = [turned_exchange(x, turn) for turn, x in enumerate(inner[:near])]
    else:
        inner_parts = [exchange(inner[0])]
    before = lax.ppermute(last, "lat", up)
    after = lax.ppermute(first, "lat", down)

    edge_shapes = [piece] * owner_count if by_turn else [whole_payload]
    edge = pl.pallas_call(
        functools.partial(edge_kernel, lat_rows, by_turn),
        in_specs=[smem, anywhere, anywhere] + [pl.BlockSpec(memory_space=pltpu.VMEM)] * 2,
        out_shape=edge_shapes,
        scratch_shapes=scratch((2,), 3 * HALO)
        + [
            starts_scratch,
            pltpu.VMEM((2,) + halo_shape.shape, jnp.float32),
        ],
        compiler_params=params,
        cost_estimate=pl.CostEstimate(flops=1, bytes_accessed=1, transcendentals=0),
        name="edge_rows",
    )(lon_counts, flat_fields, flat_winds, before, after)

    if by_turn:
        edge = list(edge)
        mirrored = pl.pallas_call(
            mirror_kernel,
            in_specs=[smem, pl.BlockSpec(memory_space=pltpu.VMEM)],
            out_shape=[piece] * near,
            scratch_shapes=[scratch((), lat_rows)[2], starts_scratch],
            compiler_params=light,
            cost_estimate=pl.CostEstimate(flops=1, bytes_accessed=1, transcendentals=0),
            name="mirror_rows",
        )(lon_counts, crossed)
        edge[1:near], mirrored = lax.optimization_barrier((edge[1:near], mirrored))
        near_parts = inner_parts[1:]
        near_parts, edge[near + 1 :] = lax.optimization_barrier((near_parts, edge[near + 1 :]))
        inner_parts = inner_parts[:1] + near_parts
        edge_parts = [turned_exchange(x, turn) for turn, x in enumerate(edge)]
        inner_parts += [turned_exchange(x, turn) for turn, x in enumerate(mirrored)]
    else:
        edge_parts = [exchange(edge[0])]

    def by_level(block):
        if level_count % 16 == 0:
            return block
        return block.transpose(1, 2, 3, 0, 4, 5).reshape(
            1, field_count, block.shape[2], half, all_levels, LANES
        )

    def whole(shape):
        return pl.BlockSpec(shape, lambda i: (0,) * len(shape))

    def block_spec(block):
        return pl.BlockSpec(
            block.shape[:2] + (1,) + block.shape[3:], lambda i: (0, 0, i, 0, 0, 0)
        )

    def cost(count):
        return pl.CostEstimate(flops=1, bytes_accessed=1, transcendentals=0)

    weights = (w_first, w_second, w_third)
    weight_specs = [pl.BlockSpec(memory_space=pltpu.VMEM)] * 4
    if by_turn:
        part_specs = [
            pl.BlockSpec((field_count, 1, half, level_count, LANES), lambda i: (0, i, 0, 0, 0))
        ] * owner_count
    else:
        inner_parts = [by_level(inner_parts[0])]
        edge_parts = [by_level(edge_parts[0])]
        part_specs = [block_spec(edge_parts[0])]
    sorted_scratch = pltpu.VMEM((field_count, all_levels, half * LANES), jnp.bfloat16)
    done_spec = pl.BlockSpec((half, features, LANES), lambda i: (0, 0, i))
    done, *turned = pl.pallas_call(
        functools.partial(half_kernel, lat_rows, inner_rows, by_turn),
        grid=(blocks,),
        in_specs=[smem, smem] + part_specs + weight_specs,
        out_specs=[done_spec] + [whole(w.shape[::-1]) for w in weights],
        out_shape=[jax.ShapeDtypeStruct((half, features, slot_width), jnp.bfloat16)]
        + [jax.ShapeDtypeStruct(w.shape[::-1], w.dtype) for w in weights],
        scratch_shapes=[sorted_scratch],
        compiler_params=light,
        cost_estimate=cost(blocks),
        name="inner_columns",
    )(group_list, lon_counts, *inner_parts, remap_weight, *weights)
    out = pl.pallas_call(
        functools.partial(last_kernel, edge_rows, inner_rows, by_turn),
        grid=(blocks,),
        in_specs=[smem, smem] + part_specs + [done_spec] + weight_specs,
        out_specs=pl.BlockSpec((features, lat_rows, LANES), lambda i: (0, 0, i)),
        out_shape=jax.ShapeDtypeStruct((features, lat_rows, slot_width), jnp.bfloat16),
        scratch_shapes=[pltpu.VMEM((features * lat_rows, LANES), jnp.float32), sorted_scratch],
        compiler_params=light,
        cost_estimate=cost(blocks),
        name="edge_columns",
    )(group_list, lon_counts, *edge_parts, done, remap_weight, *turned)
    return out.reshape(field_count, all_levels, lat_rows, slot_width)


def solution(mesh):
    in_specs = (
        P(None, "lev", "lat", None),
        P(None, "lev", "lat", None),
        P(),
        P(),
        P(),
        P(),
        P("lat", None),
        P(),
    )
    out_specs = P(None, None, "lat", "lev")
    return jax.shard_map(shards, mesh=mesh, in_specs=in_specs, out_specs=out_specs, check_vma=False)
```

```python
import functools

import jax
import jax.numpy as jnp
from jax import lax
from jax.experimental import pallas as pl
from jax.experimental.pallas import tpu as pltpu
from jax.sharding import PartitionSpec as P

DIFFUSION = 0.15
LANES = 128
HALO = 2
MIB = 1024 * 1024


def from_west(x):
    return pltpu.roll(x, 1, 1)


def from_east(x):
    return pltpu.roll(x, x.shape[1] - 1, 1)


def face_weights(before, after):
    half = 0.25 * (before + after)
    return half + DIFFUSION, half - DIFFUSION


def step_rows(values, rows, weights):
    result = {}
    for row in rows:
        here, west, away, above, below = weights(row)
        side = west * from_west(values[row]) + away * from_east(values[row])
        across = above * values[row - 1] + below * values[row + 1]
        result[row] = here * values[row] + (side + across)
    return result


def heun_rows(values, weights):
    count = len(values)
    predicted = step_rows(values, range(1, count - 1), weights)
    stepped = step_rows(predicted, range(2, count - 2), weights)
    return [0.5 * (values[row] + stepped[row]) for row in stepped]


def start_grid(fields_ref, winds_ref, grid_ref, sems):
    fields, tiles = fields_ref.shape[0], grid_ref.shape[1]

    def copy(array, tile, source):
        lanes = pl.ds(tile * LANES, LANES)
        return pltpu.make_async_copy(
            source.at[:, lanes], grid_ref.at[array, tile], sems.at[array, tile]
        )

    for wind in range(2):
        for tile in range(tiles):
            copy(fields + wind, tile, winds_ref.at[wind]).start()
    for field in range(fields):
        for tile in range(tiles):
            copy(field, tile, fields_ref.at[field]).start()

    def wait(array):
        for tile in range(tiles):
            copy(array, tile, fields_ref.at[0]).wait()

    return wait


def load_row(grid_ref, array, row, group, size, rows):
    start = group * (size * rows) + row
    pieces = [
        grid_ref[array, tile, pl.ds(start, size, stride=rows), :]
        for tile in range(grid_ref.shape[1])
    ]
    return jnp.concatenate(pieces, axis=1)


def store_weights(weight_ref, levels, east_winds, north_winds, wall=None):
    count = len(north_winds)
    faces = {}
    for face in range(1, count):
        pair = face_weights(north_winds[face - 1], north_winds[face])
        shut = wall is not None and wall[0] == face
        faces[face] = [part * wall[1] for part in pair] if shut else pair
    for row in range(1, count - 1):
        west, own = face_weights(from_west(east_winds[row]), east_winds[row])
        here = 1.0 + (own - from_east(west)) + (faces[row][1] - faces[row + 1][0])
        parts = (here, west, -from_east(own), faces[row][0], -faces[row + 1][1])
        for part, value in enumerate(parts):
            weight_ref[row, part, levels, :] = value


def keep_row(kept_ref, index, levels, value):
    for tile in range(value.shape[1] // LANES):
        kept_ref[tile, index, levels, :] = value[:, tile * LANES : (tile + 1) * LANES]


def clear_tail(kept_ref, tiles):
    for tile in range(tiles, kept_ref.shape[0]):
        kept_ref[tile] = jnp.zeros(kept_ref.shape[1:], kept_ref.dtype)


def keep_starts(counts_ref, start_ref):
    total = jnp.int32(0)
    for owner in range(start_ref.shape[0]):
        start_ref[owner] = total
        total = total + counts_ref[0, owner]


def turned_starts(start_ref, by_turn, slots):
    own = lax.axis_index("lev") if by_turn else 0
    return [start_ref[own ^ turn] for turn in range(slots)]


def pack_rows(kept_ref, starts, blocks, store):
    _, rows, levels, _ = kept_ref.shape
    lane = lax.broadcasted_iota(jnp.int32, (levels, LANES), 1)
    for slot, start in enumerate(starts):
        tile = start // LANES
        inside = start - tile * LANES
        shift = (LANES - inside) % LANES
        keep = lane < LANES - inside
        for row in range(rows):
            turned = [
                pltpu.roll(kept_ref[tile + j, row], shift, 1) for j in range(blocks + 1)
            ]
            for j in range(blocks):
                joined = jnp.where(keep, turned[j], turned[j + 1])
                store(slot, j, row, joined.astype(jnp.bfloat16))


def inner_kernel(
    rows,
    by_turn,
    counts_ref,
    fields_ref,
    winds_ref,
    *refs,
):
    outs, scratch = refs[:-9], refs[-9:]
    grid_ref, weight_ref, kept_ref, sems = scratch[:4]
    start_ref, packed_ref, raw_ref, halo_ref, sent = scratch[4:]
    *outs, first_ref, last_ref = outs
    fields = fields_ref.shape[0]
    owners = start_ref.shape[0]
    _, slots, blocks, _, levels, _ = packed_ref.shape
    tiles = grid_ref.shape[1]
    size = min(8, levels)
    groups = levels // size
    wait = start_grid(fields_ref, winds_ref, grid_ref, sems)
    clear_tail(kept_ref, grid_ref.shape[1])
    keep_starts(counts_ref, start_ref)

    def field_out(field):
        if not by_turn:
            return [
                pltpu.make_async_copy(
                    packed_ref.at[field], outs[0].at[:, field], sent.at[field, 0]
                )
            ]
        copies = [
            pltpu.make_async_copy(
                packed_ref.at[field, slot], outs[slot].at[field], sent.at[field, slot]
            )
            for slot in range(slots)
        ]
        copies.append(
            pltpu.make_async_copy(raw_ref.at[field], outs[slots].at[field], sent.at[field, slots])
        )
        return copies

    def keep_halo(array):
        for row in range(HALO):
            for side, source in enumerate((row, rows - HALO + row)):
                value = [
                    load_row(grid_ref, array, source, group, size, rows) for group in range(groups)
                ]
                halo_ref[side, array, row] = jnp.concatenate(value, axis=0).astype(halo_ref.dtype)

    def halo_out(array):
        return [
            pltpu.make_async_copy(
                halo_ref.at[side, array], ref.at[array], sent.at[array, slots + 1 + side]
            )
            for side, ref in enumerate((first_ref, last_ref))
        ]

    wait(fields)
    wait(fields + 1)

    def weights(group, carry):
        east = [load_row(grid_ref, fields, row, group, size, rows) for row in range(rows)]
        north = [load_row(grid_ref, fields + 1, row, group, size, rows) for row in range(rows)]
        store_weights(weight_ref, pl.ds(group * size, size), east, north)
        return carry

    lax.fori_loop(0, groups, weights, 0)
    for array in (fields, fields + 1):
        keep_halo(array)
        for copy in halo_out(array):
            copy.start()

    def one_field(field, carry):
        wait(field)
        keep_halo(field)

        def one_group(group, carry):
            place = pl.ds(group * size, size)
            values = [load_row(grid_ref, field, row, group, size, rows) for row in range(rows)]

            def row_weights(row):
                return [weight_ref[row, part, place, :] for part in range(5)]

            for index, value in enumerate(heun_rows(values, row_weights)):
                keep_row(kept_ref, index, place, value)
            return carry

        lax.fori_loop(0, groups, one_group, 0)

        def store(slot, block, row, value):
            packed_ref[field, slot, block, row] = value

        if by_turn:
            for tile in range(tiles):
                raw_ref[field, tile] = kept_ref[tile].astype(raw_ref.dtype)
        pack_rows(kept_ref, turned_starts(start_ref, by_turn, slots), blocks, store)
        for copy in halo_out(field) + field_out(field):
            copy.start()
        return carry

    lax.fori_loop(0, fields, one_field, 0)
    for field in range(fields):
        for copy in field_out(field):
            copy.wait()
    for array in range(fields + 2):
        for copy in halo_out(array):
            copy.wait()


def mirror_kernel(counts_ref, raw_ref, *refs):
    outs, (kept_ref, start_ref) = refs[:-2], refs[-2:]
    fields, tiles = raw_ref.shape[:2]
    keep_starts(counts_ref, start_ref)
    clear_tail(kept_ref, tiles)

    def one_field(field, carry):
        for tile in range(tiles):
            kept_ref[tile] = raw_ref[field, tile].astype(jnp.float32)

        def store(slot, block, row, value):
            outs[slot][field, block, row] = value

        starts = turned_starts(start_ref, True, len(outs))
        pack_rows(kept_ref, starts, outs[0].shape[1], store)
        return carry

    lax.fori_loop(0, fields, one_field, 0)


def edge_kernel(
    rows,
    by_turn,
    counts_ref,
    fields_ref,
    winds_ref,
    before_ref,
    after_ref,
    *refs,
):
    outs, scratch = refs[:-6], refs[-6:]
    grid_ref, weight_ref, kept_ref, sems, start_ref, halo_ref = scratch
    fields = fields_ref.shape[0]
    owners = start_ref.shape[0]
    blocks = outs[0].shape[-4]
    levels = before_ref.shape[2]
    size = min(8, levels)
    groups = levels // size
    wait = start_grid(fields_ref, winds_ref, grid_ref, sems)
    clear_tail(kept_ref, grid_ref.shape[1])
    keep_starts(counts_ref, start_ref)
    count = 3 * HALO

    def run(array, group, top):
        own = range(2 * HALO) if top else range(rows - 2 * HALO, rows)
        own = [load_row(grid_ref, array, row, group, size, rows) for row in own]
        place = pl.ds(group * size, size)
        halo = [halo_ref[int(top), array, row, place, :] for row in range(HALO)]
        return halo + own if top else own + halo

    for side, ref in enumerate((after_ref, before_ref)):
        for array in range(fields + 2):
            for row in range(HALO):
                halo_ref[side, array, row] = ref[array, row].astype(jnp.float32)

    wait(fields)
    wait(fields + 1)
    for top in (True, False):
        wall = HALO if top else count - HALO
        band = lax.axis_index("lat")
        is_open = jnp.where(band == (0 if top else lax.axis_size("lat") - 1), 0.0, 1.0)

        def weights(group, carry):
            store_weights(
                weight_ref.at[int(top)],
                pl.ds(group * size, size),
                run(fields, group, top),
                run(fields + 1, group, top),
                (wall, is_open),
            )
            return carry

        lax.fori_loop(0, groups, weights, 0)

    def one_field(field, carry):
        wait(field)

        def one_group(group, carry):
            place = pl.ds(group * size, size)
            for top in (True, False):
                side = int(top)

                def row_weights(row):
                    return [weight_ref[side, row, part, place, :] for part in range(5)]

                done = heun_rows(run(field, group, top), row_weights)
                for index, value in enumerate(done):
                    keep_row(kept_ref, index + (0 if top else HALO), place, value)
            return carry

        lax.fori_loop(0, groups, one_group, 0)

        def store(slot, block, row, value):
            if by_turn:
                outs[slot][field, block, row] = value
            else:
                outs[0][slot, field, block, row] = value

        pack_rows(kept_ref, turned_starts(start_ref, by_turn, owners), blocks, store)
        return carry

    lax.fori_loop(0, fields, one_field, 0)


def silu(x):
    half = 0.5 * x
    return half + half * jnp.tanh(half)


def dot(a, b):
    return jnp.dot(a, b, preferred_element_type=jnp.float32)


def gathered(block_ref, field):
    sources, _, _, rows = block_ref.shape[:4]
    by_row = [
        jnp.concatenate([block_ref[source, field, 0, row] for source in range(sources)], axis=0)
        for row in range(rows)
    ]
    return jnp.concatenate(by_row, axis=1)


def sort_turns(own, refs, sorted_ref):
    fields, _, rows, levels, _ = refs[0].shape
    for turn, ref in enumerate(refs):
        place = pl.ds(pl.multiple_of((own ^ turn) * levels, levels), levels)
        for field in range(fields):
            for row in range(rows):
                sorted_ref[field, place, row * LANES : (row + 1) * LANES] = ref[field, 0, row]


def column_update(columns, fields, remap_ref, first_ref, second_ref, third_ref):
    remapped = []
    for field in range(fields):
        values = columns(field)
        remapped.append(values.astype(jnp.float32) + dot(remap_ref[...], values))
    remapped = jnp.concatenate(remapped, axis=0)
    hidden = silu(dot(first_ref[...], remapped.astype(jnp.bfloat16))).astype(jnp.bfloat16)
    hidden = silu(dot(second_ref[...], hidden)).astype(jnp.bfloat16)
    tendency = dot(third_ref[...], hidden).astype(jnp.bfloat16).astype(jnp.float32)
    return remapped, tendency


def finished_row(remapped, tendency, listed, index, live):
    lanes = slice(index * LANES, (index + 1) * LANES)
    updated = remapped[:, lanes] + jnp.where(listed, tendency[:, lanes], 0.0)
    return jnp.where(live, updated, 0.0)


def live_lanes(counts_ref, features, block):
    lane = lax.broadcasted_iota(jnp.int32, (features, LANES), 1)
    return lane + block * LANES < counts_ref[0, lax.axis_index("lev")]


def is_listed(groups_ref, row):
    found = jnp.bool_(False)
    for owner in range(groups_ref.shape[0]):
        for index in range(groups_ref.shape[1]):
            found = found | (groups_ref[owner, index] == row)
    return found


def column_source(by_turn, refs, sorted_ref):
    if not by_turn:
        return functools.partial(gathered, refs[0])
    sort_turns(lax.axis_index("lev"), refs, sorted_ref)
    return lambda field: sorted_ref[field]


def half_kernel(rows, row_list, by_turn, groups_ref, counts_ref, *refs):
    out_ref, first_out, second_out, third_out, sorted_ref = refs[-5:]
    *refs, remap_ref, first_ref, second_ref, third_ref = refs[:-5]

    @pl.when(pl.program_id(0) == 0)
    def _():
        first_out[...] = first_ref[...].T
        second_out[...] = second_ref[...].T
        third_out[...] = third_ref[...].T

    columns = column_source(by_turn, refs, sorted_ref)
    fields = sorted_ref.shape[0]
    remapped, tendency = column_update(
        columns, fields, remap_ref, first_out, second_out, third_out
    )
    live = live_lanes(counts_ref, remapped.shape[0], pl.program_id(0))
    first_row = lax.axis_index("lat") * rows
    for index, row in enumerate(row_list):
        listed = is_listed(groups_ref, first_row + row)
        updated = finished_row(remapped, tendency, listed, index, live)
        out_ref[index] = updated.astype(jnp.bfloat16)


def last_kernel(row_list, done_list, by_turn, groups_ref, counts_ref, *refs):
    *refs, done_ref, remap_ref, first_ref, second_ref, third_ref, out_ref, tiles_ref, sorted_ref = (
        refs
    )
    features, rows, _ = out_ref.shape
    fields = sorted_ref.shape[0]
    columns = column_source(by_turn, refs, sorted_ref)
    remapped, tendency = column_update(
        columns, fields, remap_ref, first_ref, second_ref, third_ref
    )
    live = live_lanes(counts_ref, features, pl.program_id(0))
    first_row = lax.axis_index("lat") * rows
    for index, row in enumerate(done_list):
        tiles_ref[pl.ds(row, features, stride=rows), :] = done_ref[index].astype(jnp.float32)
    for index, row in enumerate(row_list):
        listed = is_listed(groups_ref, first_row + row)
        tiles_ref[pl.ds(row, features, stride=rows), :] = finished_row(
            remapped, tendency, listed, index, live
        )
    out_ref[...] = tiles_ref[...].reshape(features, rows, LANES).astype(jnp.bfloat16)


def shards(fields, winds, remap_weight, w_first, w_second, w_third, lon_counts, group_list):
    field_count, level_count, lat_rows, lon_total = fields.shape
    band_count = lax.axis_size("lat")
    owner_count = lax.axis_size("lev")
    all_levels = level_count * owner_count
    features = field_count * all_levels
    blocks = (2 * lon_total // owner_count + LANES - 1) // LANES
    slot_width = blocks * LANES
    inner_rows = tuple(range(HALO, lat_rows - HALO))
    edge_rows = tuple(range(HALO)) + tuple(range(lat_rows - HALO, lat_rows))
    half = len(inner_rows)
    stacked = field_count + 2
    tiles = lon_total // LANES
    smem = pl.BlockSpec(memory_space=pltpu.SMEM)
    anywhere = pl.BlockSpec(memory_space=pl.ANY)
    params = pltpu.CompilerParams(vmem_limit_bytes=60 * MIB)
    light = pltpu.CompilerParams(vmem_limit_bytes=24 * MIB)
    values = field_count * level_count * lat_rows * lon_total

    def payload(count):
        return (owner_count, field_count, count, half, level_count, LANES)

    flat_fields = fields.reshape(field_count, level_count * lat_rows, lon_total)
    flat_winds = winds.reshape(2, level_count * lat_rows, lon_total)
    halo_shape = jax.ShapeDtypeStruct((stacked, HALO, level_count, lon_total), jnp.bfloat16)

    def scratch(sides, count):
        return [
            pltpu.VMEM((stacked, tiles, level_count * lat_rows, LANES), jnp.float32),
            pltpu.VMEM(sides + (count - 1, 5, level_count, lon_total), jnp.float32),
            pltpu.VMEM((tiles + blocks, half, level_count, LANES), jnp.float32),
            pltpu.SemaphoreType.DMA((stacked, tiles)),
        ]

    by_turn = owner_count == 8
    near = owner_count // 2
    slots = near if by_turn else owner_count
    raw_shape = (field_count, tiles, half, level_count, LANES)
    piece = jax.ShapeDtypeStruct(payload(blocks)[1:], jnp.bfloat16)
    whole_payload = jax.ShapeDtypeStruct(payload(blocks), jnp.bfloat16)
    raw = jax.ShapeDtypeStruct(raw_shape, jnp.bfloat16)
    inner_shapes = [piece] * near + [raw] if by_turn else [whole_payload]
    starts_scratch = pltpu.SMEM((owner_count,), jnp.int32)
    *inner, first, last = pl.pallas_call(
        functools.partial(inner_kernel, lat_rows, by_turn),
        in_specs=[smem, anywhere, anywhere],
        out_specs=[anywhere] * (len(inner_shapes) + 2),
        out_shape=inner_shapes + [halo_shape, halo_shape],
        scratch_shapes=scratch((), lat_rows)
        + [
            starts_scratch,
            pltpu.VMEM((field_count, slots) + payload(blocks)[2:], jnp.bfloat16),
            pltpu.VMEM(raw_shape, jnp.bfloat16),
            pltpu.VMEM((2,) + halo_shape.shape, halo_shape.dtype),
            pltpu.SemaphoreType.DMA((stacked, slots + 3)),
        ],
        compiler_params=params,
        cost_estimate=pl.CostEstimate(flops=1, bytes_accessed=1, transcendentals=0),
        name="inner_rows",
    )(lon_counts, flat_fields, flat_winds)

    up = [(i, i + 1) for i in range(band_count - 1)]
    down = [(j, i) for i, j in up]

    def exchange(x):
        return lax.all_to_all(x, "lev", split_axis=0, concat_axis=0, tiled=True)

    def turned_exchange(x, turn):
        return lax.ppermute(x, "lev", [(i, i ^ turn) for i in range(owner_count)]) if turn else x

    if by_turn:
        crossed = turned_exchange(inner[near], near + near // 2)
        inner_parts = [turned_exchange(x, turn) for turn, x in enumerate(inner[:near])]
    else:
        inner_parts = [exchange(inner[0])]
    before = lax.ppermute(last, "lat", up)
    after = lax.ppermute(first, "lat", down)

    edge_shapes = [piece] * owner_count if by_turn else [whole_payload]
    edge = pl.pallas_call(
        functools.partial(edge_kernel, lat_rows, by_turn),
        in_specs=[smem, anywhere, anywhere] + [pl.BlockSpec(memory_space=pltpu.VMEM)] * 2,
        out_shape=edge_shapes,
        scratch_shapes=scratch((2,), 3 * HALO)
        + [
            starts_scratch,
            pltpu.VMEM((2,) + halo_shape.shape, jnp.float32),
        ],
        compiler_params=params,
        cost_estimate=pl.CostEstimate(flops=1, bytes_accessed=1, transcendentals=0),
        name="edge_rows",
    )(lon_counts, flat_fields, flat_winds, before, after)

    if by_turn:
        edge = list(edge)
        mirrored = pl.pallas_call(
            mirror_kernel,
            in_specs=[smem, pl.BlockSpec(memory_space=pltpu.VMEM)],
            out_shape=[piece] * near,
            scratch_shapes=[scratch((), lat_rows)[2], starts_scratch],
            compiler_params=light,
            cost_estimate=pl.CostEstimate(flops=1, bytes_accessed=1, transcendentals=0),
            name="mirror_rows",
        )(lon_counts, crossed)
        edge[1:near], mirrored = lax.optimization_barrier((edge[1:near], mirrored))
        near_parts = inner_parts[1:]
        near_parts, edge[near + 1 :] = lax.optimization_barrier((near_parts, edge[near + 1 :]))
        inner_parts = inner_parts[:1] + near_parts
        edge_parts = [turned_exchange(x, turn) for turn, x in enumerate(edge)]
        mirrored = [turned_exchange(x, turn) for turn, x in enumerate(mirrored)]
        inner_parts += [mirrored[turn ^ (near // 2)] for turn in range(near)]
    else:
        edge_parts = [exchange(edge[0])]

    def by_level(block):
        if level_count % 16 == 0:
            return block
        return block.transpose(1, 2, 3, 0, 4, 5).reshape(
            1, field_count, block.shape[2], half, all_levels, LANES
        )

    def whole(shape):
        return pl.BlockSpec(shape, lambda i: (0,) * len(shape))

    def block_spec(block):
        return pl.BlockSpec(
            block.shape[:2] + (1,) + block.shape[3:], lambda i: (0, 0, i, 0, 0, 0)
        )

    def cost(count):
        return pl.CostEstimate(flops=1, bytes_accessed=1, transcendentals=0)

    weights = (w_first, w_second, w_third)
    weight_specs = [pl.BlockSpec(memory_space=pltpu.VMEM)] * 4
    if by_turn:
        part_specs = [
            pl.BlockSpec((field_count, 1, half, level_count, LANES), lambda i: (0, i, 0, 0, 0))
        ] * owner_count
    else:
        inner_parts = [by_level(inner_parts[0])]
        edge_parts = [by_level(edge_parts[0])]
        part_specs = [block_spec(edge_parts[0])]
    sorted_scratch = pltpu.VMEM((field_count, all_levels, half * LANES), jnp.bfloat16)
    done_spec = pl.BlockSpec((half, features, LANES), lambda i: (0, 0, i))
    done, *turned = pl.pallas_call(
        functools.partial(half_kernel, lat_rows, inner_rows, by_turn),
        grid=(blocks,),
        in_specs=[smem, smem] + part_specs + weight_specs,
        out_specs=[done_spec] + [whole(w.shape[::-1]) for w in weights],
        out_shape=[jax.ShapeDtypeStruct((half, features, slot_width), jnp.bfloat16)]
        + [jax.ShapeDtypeStruct(w.shape[::-1], w.dtype) for w in weights],
        scratch_shapes=[sorted_scratch],
        compiler_params=light,
        cost_estimate=cost(blocks),
        name="inner_columns",
    )(group_list, lon_counts, *inner_parts, remap_weight, *weights)
    out = pl.pallas_call(
        functools.partial(last_kernel, edge_rows, inner_rows, by_turn),
        grid=(blocks,),
        in_specs=[smem, smem] + part_specs + [done_spec] + weight_specs,
        out_specs=pl.BlockSpec((features, lat_rows, LANES), lambda i: (0, 0, i)),
        out_shape=jax.ShapeDtypeStruct((features, lat_rows, slot_width), jnp.bfloat16),
        scratch_shapes=[pltpu.VMEM((features * lat_rows, LANES), jnp.float32), sorted_scratch],
        compiler_params=light,
        cost_estimate=cost(blocks),
        name="edge_columns",
    )(group_list, lon_counts, *edge_parts, done, remap_weight, *turned)
    return out.reshape(field_count, all_levels, lat_rows, slot_width)


def solution(mesh):
    in_specs = (
        P(None, "lev", "lat", None),
        P(None, "lev", "lat", None),
        P(),
        P(),
        P(),
        P(),
        P("lat", None),
        P(),
    )
    out_specs = P(None, None, "lat", "lev")
    return jax.shard_map(shards, mesh=mesh, in_specs=in_specs, out_specs=out_specs, check_vma=False)
```

```python
import functools

import jax
import jax.numpy as jnp
from jax import lax
from jax.experimental import pallas as pl
from jax.experimental.pallas import tpu as pltpu
from jax.sharding import PartitionSpec as P

DIFFUSION = 0.15
LANES = 128
HALO = 2
MIB = 1024 * 1024


def from_west(x):
    return pltpu.roll(x, 1, 1)


def from_east(x):
    return pltpu.roll(x, x.shape[1] - 1, 1)


def face_weights(before, after):
    half = 0.25 * (before + after)
    return half + DIFFUSION, half - DIFFUSION


def step_rows(values, rows, weights):
    result = {}
    for row in rows:
        here, west, away, above, below = weights(row)
        side = west * from_west(values[row]) + away * from_east(values[row])
        across = above * values[row - 1] + below * values[row + 1]
        result[row] = here * values[row] + (side + across)
    return result


def heun_rows(values, weights):
    count = len(values)
    predicted = step_rows(values, range(1, count - 1), weights)
    stepped = step_rows(predicted, range(2, count - 2), weights)
    return [0.5 * (values[row] + stepped[row]) for row in stepped]


def start_grid(fields_ref, winds_ref, grid_ref, sems):
    fields, tiles = fields_ref.shape[0], grid_ref.shape[1]

    def copy(array, tile, source):
        lanes = pl.ds(tile * LANES, LANES)
        return pltpu.make_async_copy(
            source.at[:, lanes], grid_ref.at[array, tile], sems.at[array, tile]
        )

    for wind in range(2):
        for tile in range(tiles):
            copy(fields + wind, tile, winds_ref.at[wind]).start()
    for field in range(fields):
        for tile in range(tiles):
            copy(field, tile, fields_ref.at[field]).start()

    def wait(array):
        for tile in range(tiles):
            copy(array, tile, fields_ref.at[0]).wait()

    return wait


def load_row(grid_ref, array, row, group, size, rows):
    start = group * (size * rows) + row
    pieces = [
        grid_ref[array, tile, pl.ds(start, size, stride=rows), :]
        for tile in range(grid_ref.shape[1])
    ]
    return jnp.concatenate(pieces, axis=1)


def store_weights(weight_ref, levels, east_winds, north_winds, wall=None):
    count = len(north_winds)
    faces = {}
    for face in range(1, count):
        pair = face_weights(north_winds[face - 1], north_winds[face])
        shut = wall is not None and wall[0] == face
        faces[face] = [part * wall[1] for part in pair] if shut else pair
    for row in range(1, count - 1):
        west, own = face_weights(from_west(east_winds[row]), east_winds[row])
        here = 1.0 + (own - from_east(west)) + (faces[row][1] - faces[row + 1][0])
        parts = (here, west, -from_east(own), faces[row][0], -faces[row + 1][1])
        for part, value in enumerate(parts):
            weight_ref[row, part, levels, :] = value


def keep_row(kept_ref, index, levels, value):
    for tile in range(value.shape[1] // LANES):
        kept_ref[tile, index, levels, :] = value[:, tile * LANES : (tile + 1) * LANES]


def clear_tail(kept_ref, tiles):
    for tile in range(tiles, kept_ref.shape[0]):
        kept_ref[tile] = jnp.zeros(kept_ref.shape[1:], kept_ref.dtype)


def keep_starts(counts_ref, start_ref):
    total = jnp.int32(0)
    for owner in range(start_ref.shape[0]):
        start_ref[owner] = total
        total = total + counts_ref[0, owner]


def turned_starts(start_ref, by_turn, slots):
    own = lax.axis_index("lev") if by_turn else 0
    return [start_ref[own ^ turn] for turn in range(slots)]


def pack_rows(kept_ref, starts, blocks, store):
    _, rows, levels, _ = kept_ref.shape
    lane = lax.broadcasted_iota(jnp.int32, (levels, LANES), 1)
    for slot, start in enumerate(starts):
        tile = start // LANES
        inside = start - tile * LANES
        shift = (LANES - inside) % LANES
        keep = lane < LANES - inside
        for row in range(rows):
            turned = [
                pltpu.roll(kept_ref[tile + j, row], shift, 1) for j in range(blocks + 1)
            ]
            for j in range(blocks):
                joined = jnp.where(keep, turned[j], turned[j + 1])
                store(slot, j, row, joined.astype(jnp.bfloat16))


def inner_kernel(
    rows,
    by_turn,
    counts_ref,
    fields_ref,
    winds_ref,
    *refs,
):
    outs, scratch = refs[:-9], refs[-9:]
    grid_ref, weight_ref, kept_ref, sems = scratch[:4]
    start_ref, packed_ref, raw_ref, halo_ref, sent = scratch[4:]
    *outs, first_ref, last_ref = outs
    fields = fields_ref.shape[0]
    owners = start_ref.shape[0]
    _, slots, blocks, _, levels, _ = packed_ref.shape
    tiles = grid_ref.shape[1]
    size = min(8, levels)
    groups = levels // size
    wait = start_grid(fields_ref, winds_ref, grid_ref, sems)
    clear_tail(kept_ref, grid_ref.shape[1])
    keep_starts(counts_ref, start_ref)

    def field_out(field):
        if not by_turn:
            return [
                pltpu.make_async_copy(
                    packed_ref.at[field], outs[0].at[:, field], sent.at[field, 0]
                )
            ]
        return [pltpu.make_async_copy(raw_ref.at[field], outs[0].at[field], sent.at[field, 0])]

    def keep_halo(array):
        for row in range(HALO):
            for side, source in enumerate((row, rows - HALO + row)):
                value = [
                    load_row(grid_ref, array, source, group, size, rows) for group in range(groups)
                ]
                halo_ref[side, array, row] = jnp.concatenate(value, axis=0).astype(halo_ref.dtype)

    def halo_out(array):
        return [
            pltpu.make_async_copy(
                halo_ref.at[side, array], ref.at[array], sent.at[array, slots + 1 + side]
            )
            for side, ref in enumerate((first_ref, last_ref))
        ]

    wait(fields)
    wait(fields + 1)

    def weights(group, carry):
        east = [load_row(grid_ref, fields, row, group, size, rows) for row in range(rows)]
        north = [load_row(grid_ref, fields + 1, row, group, size, rows) for row in range(rows)]
        store_weights(weight_ref, pl.ds(group * size, size), east, north)
        return carry

    lax.fori_loop(0, groups, weights, 0)
    for array in (fields, fields + 1):
        keep_halo(array)
        for copy in halo_out(array):
            copy.start()

    def one_field(field, carry):
        wait(field)
        keep_halo(field)

        def one_group(group, carry):
            place = pl.ds(group * size, size)
            values = [load_row(grid_ref, field, row, group, size, rows) for row in range(rows)]

            def row_weights(row):
                return [weight_ref[row, part, place, :] for part in range(5)]

            for index, value in enumerate(heun_rows(values, row_weights)):
                keep_row(kept_ref, index, place, value)
            return carry

        lax.fori_loop(0, groups, one_group, 0)

        def store(slot, block, row, value):
            packed_ref[field, slot, block, row] = value

        if by_turn:
            for tile in range(tiles):
                raw_ref[field, tile] = kept_ref[tile].astype(raw_ref.dtype)
        else:
            pack_rows(kept_ref, turned_starts(start_ref, False, slots), blocks, store)
        for copy in halo_out(field) + field_out(field):
            copy.start()
        return carry

    lax.fori_loop(0, fields, one_field, 0)
    for field in range(fields):
        for copy in field_out(field):
            copy.wait()
    for array in range(fields + 2):
        for copy in halo_out(array):
            copy.wait()


def mirror_kernel(counts_ref, raw_ref, *refs):
    outs, (kept_ref, start_ref) = refs[:-2], refs[-2:]
    fields, tiles = raw_ref.shape[:2]
    keep_starts(counts_ref, start_ref)
    clear_tail(kept_ref, tiles)

    def one_field(field, carry):
        for tile in range(tiles):
            kept_ref[tile] = raw_ref[field, tile].astype(jnp.float32)

        def store(slot, block, row, value):
            outs[slot][field, block, row] = value

        starts = turned_starts(start_ref, True, len(outs))
        pack_rows(kept_ref, starts, outs[0].shape[1], store)
        return carry

    lax.fori_loop(0, fields, one_field, 0)


def edge_kernel(
    rows,
    by_turn,
    counts_ref,
    fields_ref,
    winds_ref,
    before_ref,
    after_ref,
    *refs,
):
    outs, scratch = refs[:-6], refs[-6:]
    grid_ref, weight_ref, kept_ref, sems, start_ref, halo_ref = scratch
    fields = fields_ref.shape[0]
    owners = start_ref.shape[0]
    blocks = outs[0].shape[-4]
    levels = before_ref.shape[2]
    size = min(8, levels)
    groups = levels // size
    wait = start_grid(fields_ref, winds_ref, grid_ref, sems)
    clear_tail(kept_ref, grid_ref.shape[1])
    keep_starts(counts_ref, start_ref)
    count = 3 * HALO

    def run(array, group, top):
        own = range(2 * HALO) if top else range(rows - 2 * HALO, rows)
        own = [load_row(grid_ref, array, row, group, size, rows) for row in own]
        place = pl.ds(group * size, size)
        halo = [halo_ref[int(top), array, row, place, :] for row in range(HALO)]
        return halo + own if top else own + halo

    for side, ref in enumerate((after_ref, before_ref)):
        for array in range(fields + 2):
            for row in range(HALO):
                halo_ref[side, array, row] = ref[array, row].astype(jnp.float32)

    wait(fields)
    wait(fields + 1)
    for top in (True, False):
        wall = HALO if top else count - HALO
        band = lax.axis_index("lat")
        is_open = jnp.where(band == (0 if top else lax.axis_size("lat") - 1), 0.0, 1.0)

        def weights(group, carry):
            store_weights(
                weight_ref.at[int(top)],
                pl.ds(group * size, size),
                run(fields, group, top),
                run(fields + 1, group, top),
                (wall, is_open),
            )
            return carry

        lax.fori_loop(0, groups, weights, 0)

    def one_field(field, carry):
        wait(field)

        def one_group(group, carry):
            place = pl.ds(group * size, size)
            for top in (True, False):
                side = int(top)

                def row_weights(row):
                    return [weight_ref[side, row, part, place, :] for part in range(5)]

                done = heun_rows(run(field, group, top), row_weights)
                for index, value in enumerate(done):
                    keep_row(kept_ref, index + (0 if top else HALO), place, value)
            return carry

        lax.fori_loop(0, groups, one_group, 0)

        def store(slot, block, row, value):
            if by_turn:
                outs[slot][field, block, row] = value
            else:
                outs[0][slot, field, block, row] = value

        pack_rows(kept_ref, turned_starts(start_ref, by_turn, owners), blocks, store)
        return carry

    lax.fori_loop(0, fields, one_field, 0)


def silu(x):
    half = 0.5 * x
    return half + half * jnp.tanh(half)


def dot(a, b):
    return jnp.dot(a, b, preferred_element_type=jnp.float32)


def gathered(block_ref, field):
    sources, _, _, rows = block_ref.shape[:4]
    by_row = [
        jnp.concatenate([block_ref[source, field, 0, row] for source in range(sources)], axis=0)
        for row in range(rows)
    ]
    return jnp.concatenate(by_row, axis=1)


def sort_turns(own, refs, sorted_ref):
    fields, _, rows, levels, _ = refs[0].shape
    for turn, ref in enumerate(refs):
        place = pl.ds(pl.multiple_of((own ^ turn) * levels, levels), levels)
        for field in range(fields):
            for row in range(rows):
                sorted_ref[field, place, row * LANES : (row + 1) * LANES] = ref[field, 0, row]


def column_update(columns, fields, remap_ref, first_ref, second_ref, third_ref):
    remapped = []
    for field in range(fields):
        values = columns(field)
        remapped.append(values.astype(jnp.float32) + dot(remap_ref[...], values))
    remapped = jnp.concatenate(remapped, axis=0)
    hidden = silu(dot(first_ref[...], remapped.astype(jnp.bfloat16))).astype(jnp.bfloat16)
    hidden = silu(dot(second_ref[...], hidden)).astype(jnp.bfloat16)
    tendency = dot(third_ref[...], hidden).astype(jnp.bfloat16).astype(jnp.float32)
    return remapped, tendency


def finished_row(remapped, tendency, listed, index, live):
    lanes = slice(index * LANES, (index + 1) * LANES)
    updated = remapped[:, lanes] + jnp.where(listed, tendency[:, lanes], 0.0)
    return jnp.where(live, updated, 0.0)


def live_lanes(counts_ref, features, block):
    lane = lax.broadcasted_iota(jnp.int32, (features, LANES), 1)
    return lane + block * LANES < counts_ref[0, lax.axis_index("lev")]


def is_listed(groups_ref, row):
    found = jnp.bool_(False)
    for owner in range(groups_ref.shape[0]):
        for index in range(groups_ref.shape[1]):
            found = found | (groups_ref[owner, index] == row)
    return found


def column_source(by_turn, refs, sorted_ref):
    if not by_turn:
        return functools.partial(gathered, refs[0])
    sort_turns(lax.axis_index("lev"), refs, sorted_ref)
    return lambda field: sorted_ref[field]


def turn_kernel(*refs):
    count = len(refs) // 2
    for source_ref, out_ref in zip(refs[:count], refs[count:]):
        out_ref[...] = source_ref[...].T


def half_kernel(rows, row_list, by_turn, groups_ref, counts_ref, *refs):
    out_ref, sorted_ref = refs[-2:]
    *refs, remap_ref, first_ref, second_ref, third_ref = refs[:-2]
    columns = column_source(by_turn, refs, sorted_ref)
    fields = sorted_ref.shape[0]
    remapped, tendency = column_update(
        columns, fields, remap_ref, first_ref, second_ref, third_ref
    )
    live = live_lanes(counts_ref, remapped.shape[0], pl.program_id(0))
    first_row = lax.axis_index("lat") * rows
    for index, row in enumerate(row_list):
        listed = is_listed(groups_ref, first_row + row)
        updated = finished_row(remapped, tendency, listed, index, live)
        out_ref[index] = updated.astype(jnp.bfloat16)


def last_kernel(row_list, done_list, by_turn, groups_ref, counts_ref, *refs):
    *refs, done_ref, remap_ref, first_ref, second_ref, third_ref, out_ref, tiles_ref, sorted_ref = (
        refs
    )
    features, rows, _ = out_ref.shape
    fields = sorted_ref.shape[0]
    columns = column_source(by_turn, refs, sorted_ref)
    remapped, tendency = column_update(
        columns, fields, remap_ref, first_ref, second_ref, third_ref
    )
    live = live_lanes(counts_ref, features, pl.program_id(0))
    first_row = lax.axis_index("lat") * rows
    for index, row in enumerate(done_list):
        tiles_ref[pl.ds(row, features, stride=rows), :] = done_ref[index].astype(jnp.float32)
    for index, row in enumerate(row_list):
        listed = is_listed(groups_ref, first_row + row)
        tiles_ref[pl.ds(row, features, stride=rows), :] = finished_row(
            remapped, tendency, listed, index, live
        )
    out_ref[...] = tiles_ref[...].reshape(features, rows, LANES).astype(jnp.bfloat16)


def shards(fields, winds, remap_weight, w_first, w_second, w_third, lon_counts, group_list):
    field_count, level_count, lat_rows, lon_total = fields.shape
    band_count = lax.axis_size("lat")
    owner_count = lax.axis_size("lev")
    all_levels = level_count * owner_count
    features = field_count * all_levels
    blocks = (2 * lon_total // owner_count + LANES - 1) // LANES
    slot_width = blocks * LANES
    inner_rows = tuple(range(HALO, lat_rows - HALO))
    edge_rows = tuple(range(HALO)) + tuple(range(lat_rows - HALO, lat_rows))
    half = len(inner_rows)
    stacked = field_count + 2
    tiles = lon_total // LANES
    smem = pl.BlockSpec(memory_space=pltpu.SMEM)
    anywhere = pl.BlockSpec(memory_space=pl.ANY)
    params = pltpu.CompilerParams(vmem_limit_bytes=60 * MIB)
    light = pltpu.CompilerParams(vmem_limit_bytes=24 * MIB)
    values = field_count * level_count * lat_rows * lon_total

    def payload(count):
        return (owner_count, field_count, count, half, level_count, LANES)

    flat_fields = fields.reshape(field_count, level_count * lat_rows, lon_total)
    flat_winds = winds.reshape(2, level_count * lat_rows, lon_total)
    halo_shape = jax.ShapeDtypeStruct((stacked, HALO, level_count, lon_total), jnp.bfloat16)

    def scratch(sides, count):
        return [
            pltpu.VMEM((stacked, tiles, level_count * lat_rows, LANES), jnp.float32),
            pltpu.VMEM(sides + (count - 1, 5, level_count, lon_total), jnp.float32),
            pltpu.VMEM((tiles + blocks, half, level_count, LANES), jnp.float32),
            pltpu.SemaphoreType.DMA((stacked, tiles)),
        ]

    by_turn = owner_count == 8
    near = owner_count // 2
    slots = near if by_turn else owner_count
    raw_shape = (field_count, tiles, half, level_count, LANES)
    piece = jax.ShapeDtypeStruct(payload(blocks)[1:], jnp.bfloat16)
    whole_payload = jax.ShapeDtypeStruct(payload(blocks), jnp.bfloat16)
    raw = jax.ShapeDtypeStruct(raw_shape, jnp.bfloat16)
    inner_shapes = [raw] if by_turn else [whole_payload]
    starts_scratch = pltpu.SMEM((owner_count,), jnp.int32)
    *inner, first, last = pl.pallas_call(
        functools.partial(inner_kernel, lat_rows, by_turn),
        in_specs=[smem, anywhere, anywhere],
        out_specs=[anywhere] * (len(inner_shapes) + 2),
        out_shape=inner_shapes + [halo_shape, halo_shape],
        scratch_shapes=scratch((), lat_rows)
        + [
            starts_scratch,
            pltpu.VMEM((field_count, slots) + payload(blocks)[2:], jnp.bfloat16),
            pltpu.VMEM(raw_shape, jnp.bfloat16),
            pltpu.VMEM((2,) + halo_shape.shape, halo_shape.dtype),
            pltpu.SemaphoreType.DMA((stacked, slots + 3)),
        ],
        compiler_params=params,
        cost_estimate=pl.CostEstimate(flops=1, bytes_accessed=1, transcendentals=0),
        name="inner_rows",
    )(lon_counts, flat_fields, flat_winds)

    up = [(i, i + 1) for i in range(band_count - 1)]
    down = [(j, i) for i, j in up]

    def exchange(x):
        return lax.all_to_all(x, "lev", split_axis=0, concat_axis=0, tiled=True)

    def turned_exchange(x, turn):
        return lax.ppermute(x, "lev", [(i, i ^ turn) for i in range(owner_count)]) if turn else x

    def pack_half(raw_rows):
        return pl.pallas_call(
            mirror_kernel,
            in_specs=[smem, pl.BlockSpec(memory_space=pltpu.VMEM)],
            out_shape=[piece] * near,
            scratch_shapes=[scratch((), lat_rows)[2], starts_scratch],
            compiler_params=light,
            cost_estimate=pl.CostEstimate(flops=1, bytes_accessed=1, transcendentals=0),
            name="half_slots",
        )(lon_counts, raw_rows)

    if by_turn:
        crossed = turned_exchange(inner[0], near + near // 2)
        inner_parts = [turned_exchange(x, turn) for turn, x in enumerate(pack_half(inner[0]))]
    else:
        inner_parts = [exchange(inner[0])]
    before = lax.ppermute(last, "lat", up)
    after = lax.ppermute(first, "lat", down)

    edge_shapes = [piece] * owner_count if by_turn else [whole_payload]
    edge = pl.pallas_call(
        functools.partial(edge_kernel, lat_rows, by_turn),
        in_specs=[smem, anywhere, anywhere] + [pl.BlockSpec(memory_space=pltpu.VMEM)] * 2,
        out_shape=edge_shapes,
        scratch_shapes=scratch((2,), 3 * HALO)
        + [
            starts_scratch,
            pltpu.VMEM((2,) + halo_shape.shape, jnp.float32),
        ],
        compiler_params=params,
        cost_estimate=pl.CostEstimate(flops=1, bytes_accessed=1, transcendentals=0),
        name="edge_rows",
    )(lon_counts, flat_fields, flat_winds, before, after)

    weights = (w_first, w_second, w_third)
    weights, _ = lax.optimization_barrier((weights, edge[0]))
    turned = pl.pallas_call(
        turn_kernel,
        in_specs=[pl.BlockSpec(memory_space=pltpu.VMEM)] * len(weights),
        out_shape=[jax.ShapeDtypeStruct(w.shape[::-1], w.dtype) for w in weights],
        compiler_params=light,
        cost_estimate=pl.CostEstimate(flops=1, bytes_accessed=1, transcendentals=0),
        name="turned_weights",
    )(*weights)
    if by_turn:
        edge = list(edge)
        edge[near:], _ = lax.optimization_barrier((edge[near:], turned))
        mirrored = pack_half(crossed)
        edge[1:near], mirrored = lax.optimization_barrier((edge[1:near], mirrored))
        near_parts = inner_parts[1:]
        near_parts, edge[near :] = lax.optimization_barrier((near_parts, edge[near :]))
        inner_parts = inner_parts[:1] + near_parts
        edge_parts = [turned_exchange(x, turn) for turn, x in enumerate(edge)]
        mirrored = [turned_exchange(x, turn) for turn, x in enumerate(mirrored)]
        inner_parts += [mirrored[turn ^ (near // 2)] for turn in range(near)]
    else:
        edge_parts = [exchange(edge[0])]

    def by_level(block):
        if level_count % 16 == 0:
            return block
        return block.transpose(1, 2, 3, 0, 4, 5).reshape(
            1, field_count, block.shape[2], half, all_levels, LANES
        )

    def block_spec(block):
        return pl.BlockSpec(
            block.shape[:2] + (1,) + block.shape[3:], lambda i: (0, 0, i, 0, 0, 0)
        )

    def cost(count):
        return pl.CostEstimate(flops=1, bytes_accessed=1, transcendentals=0)

    weight_specs = [pl.BlockSpec(memory_space=pltpu.VMEM)] * 4
    if by_turn:
        part_specs = [
            pl.BlockSpec((field_count, 1, half, level_count, LANES), lambda i: (0, i, 0, 0, 0))
        ] * owner_count
    else:
        inner_parts = [by_level(inner_parts[0])]
        edge_parts = [by_level(edge_parts[0])]
        part_specs = [block_spec(edge_parts[0])]
    sorted_scratch = pltpu.VMEM((field_count, all_levels, half * LANES), jnp.bfloat16)
    done_spec = pl.BlockSpec((half, features, LANES), lambda i: (0, 0, i))
    done = pl.pallas_call(
        functools.partial(half_kernel, lat_rows, inner_rows, by_turn),
        grid=(blocks,),
        in_specs=[smem, smem] + part_specs + weight_specs,
        out_specs=done_spec,
        out_shape=jax.ShapeDtypeStruct((half, features, slot_width), jnp.bfloat16),
        scratch_shapes=[sorted_scratch],
        compiler_params=light,
        cost_estimate=cost(blocks),
        name="inner_columns",
    )(group_list, lon_counts, *inner_parts, remap_weight, *turned)
    out = pl.pallas_call(
        functools.partial(last_kernel, edge_rows, inner_rows, by_turn),
        grid=(blocks,),
        in_specs=[smem, smem] + part_specs + [done_spec] + weight_specs,
        out_specs=pl.BlockSpec((features, lat_rows, LANES), lambda i: (0, 0, i)),
        out_shape=jax.ShapeDtypeStruct((features, lat_rows, slot_width), jnp.bfloat16),
        scratch_shapes=[pltpu.VMEM((features * lat_rows, LANES), jnp.float32), sorted_scratch],
        compiler_params=light,
        cost_estimate=cost(blocks),
        name="edge_columns",
    )(group_list, lon_counts, *edge_parts, done, remap_weight, *turned)
    return out.reshape(field_count, all_levels, lat_rows, slot_width)


def solution(mesh):
    in_specs = (
        P(None, "lev", "lat", None),
        P(None, "lev", "lat", None),
        P(),
        P(),
        P(),
        P(),
        P("lat", None),
        P(),
    )
    out_specs = P(None, None, "lat", "lev")
    return jax.shard_map(shards, mesh=mesh, in_specs=in_specs, out_specs=out_specs, check_vma=False)
```

```python
import functools

import jax
import jax.numpy as jnp
from jax import lax
from jax.experimental import pallas as pl
from jax.experimental.pallas import tpu as pltpu
from jax.sharding import PartitionSpec as P

DIFFUSION = 0.15
LANES = 128
HALO = 2
MIB = 1024 * 1024


def from_west(x):
    return pltpu.roll(x, 1, 1)


def from_east(x):
    return pltpu.roll(x, x.shape[1] - 1, 1)


def face_weights(before, after):
    half = 0.25 * (before + after)
    return half + DIFFUSION, half - DIFFUSION


def step_rows(values, rows, weights):
    result = {}
    for row in rows:
        here, west, away, above, below = weights(row)
        side = west * from_west(values[row]) + away * from_east(values[row])
        across = above * values[row - 1] + below * values[row + 1]
        result[row] = here * values[row] + (side + across)
    return result


def heun_rows(values, weights):
    count = len(values)
    predicted = step_rows(values, range(1, count - 1), weights)
    stepped = step_rows(predicted, range(2, count - 2), weights)
    return [0.5 * (values[row] + stepped[row]) for row in stepped]


def start_grid(fields_ref, winds_ref, grid_ref, sems):
    fields, tiles = fields_ref.shape[0], grid_ref.shape[1]

    def copy(array, tile, source):
        lanes = pl.ds(tile * LANES, LANES)
        return pltpu.make_async_copy(
            source.at[:, lanes], grid_ref.at[array, tile], sems.at[array, tile]
        )

    for wind in range(2):
        for tile in range(tiles):
            copy(fields + wind, tile, winds_ref.at[wind]).start()
    for field in range(fields):
        for tile in range(tiles):
            copy(field, tile, fields_ref.at[field]).start()

    def wait(array):
        for tile in range(tiles):
            copy(array, tile, fields_ref.at[0]).wait()

    return wait


def load_row(grid_ref, array, row, group, size, rows):
    start = group * (size * rows) + row
    pieces = [
        grid_ref[array, tile, pl.ds(start, size, stride=rows), :]
        for tile in range(grid_ref.shape[1])
    ]
    return jnp.concatenate(pieces, axis=1)


def store_weights(weight_ref, levels, east_winds, north_winds, wall=None):
    count = len(north_winds)
    faces = {}
    for face in range(1, count):
        pair = face_weights(north_winds[face - 1], north_winds[face])
        shut = wall is not None and wall[0] == face
        faces[face] = [part * wall[1] for part in pair] if shut else pair
    for row in range(1, count - 1):
        west, own = face_weights(from_west(east_winds[row]), east_winds[row])
        here = 1.0 + (own - from_east(west)) + (faces[row][1] - faces[row + 1][0])
        parts = (here, west, -from_east(own), faces[row][0], -faces[row + 1][1])
        for part, value in enumerate(parts):
            weight_ref[row, part, levels, :] = value


def keep_row(kept_ref, index, levels, value):
    for tile in range(value.shape[1] // LANES):
        kept_ref[tile, index, levels, :] = value[:, tile * LANES : (tile + 1) * LANES]


def clear_tail(kept_ref, tiles):
    for tile in range(tiles, kept_ref.shape[0]):
        kept_ref[tile] = jnp.zeros(kept_ref.shape[1:], kept_ref.dtype)


def keep_starts(counts_ref, start_ref):
    total = jnp.int32(0)
    for owner in range(start_ref.shape[0]):
        start_ref[owner] = total
        total = total + counts_ref[0, owner]


def turned_starts(start_ref, by_turn, slots):
    own = lax.axis_index("lev") if by_turn else 0
    return [start_ref[own ^ turn] for turn in range(slots)]


def pack_rows(kept_ref, starts, blocks, store):
    _, rows, levels, _ = kept_ref.shape
    lane = lax.broadcasted_iota(jnp.int32, (levels, LANES), 1)
    for slot, start in enumerate(starts):
        tile = start // LANES
        inside = start - tile * LANES
        shift = (LANES - inside) % LANES
        keep = lane < LANES - inside
        for row in range(rows):
            turned = [
                pltpu.roll(kept_ref[tile + j, row], shift, 1) for j in range(blocks + 1)
            ]
            for j in range(blocks):
                joined = jnp.where(keep, turned[j], turned[j + 1])
                store(slot, j, row, joined.astype(jnp.bfloat16))


def inner_kernel(
    rows,
    by_turn,
    counts_ref,
    fields_ref,
    winds_ref,
    *refs,
):
    outs, scratch = refs[:-9], refs[-9:]
    grid_ref, weight_ref, kept_ref, sems = scratch[:4]
    start_ref, packed_ref, raw_ref, halo_ref, sent = scratch[4:]
    *outs, first_ref, last_ref = outs
    fields = fields_ref.shape[0]
    owners = start_ref.shape[0]
    _, slots, blocks, _, levels, _ = packed_ref.shape
    tiles = grid_ref.shape[1]
    size = min(8, levels)
    groups = levels // size
    wait = start_grid(fields_ref, winds_ref, grid_ref, sems)
    clear_tail(kept_ref, grid_ref.shape[1])
    keep_starts(counts_ref, start_ref)

    def field_out(field):
        if not by_turn:
            return [
                pltpu.make_async_copy(
                    packed_ref.at[field], outs[0].at[:, field], sent.at[field, 0]
                )
            ]
        return [pltpu.make_async_copy(raw_ref.at[field], outs[0].at[field], sent.at[field, 0])]

    def keep_halo(array):
        for row in range(HALO):
            for side, source in enumerate((row, rows - HALO + row)):
                value = [
                    load_row(grid_ref, array, source, group, size, rows) for group in range(groups)
                ]
                halo_ref[side, array, row] = jnp.concatenate(value, axis=0).astype(halo_ref.dtype)

    def halo_out(array):
        return [
            pltpu.make_async_copy(
                halo_ref.at[side, array], ref.at[array], sent.at[array, slots + 1 + side]
            )
            for side, ref in enumerate((first_ref, last_ref))
        ]

    wait(fields)
    wait(fields + 1)

    def weights(group, carry):
        east = [load_row(grid_ref, fields, row, group, size, rows) for row in range(rows)]
        north = [load_row(grid_ref, fields + 1, row, group, size, rows) for row in range(rows)]
        store_weights(weight_ref, pl.ds(group * size, size), east, north)
        return carry

    lax.fori_loop(0, groups, weights, 0)
    for array in (fields, fields + 1):
        keep_halo(array)
        for copy in halo_out(array):
            copy.start()

    def one_field(field, carry):
        wait(field)
        keep_halo(field)

        def one_group(group, carry):
            place = pl.ds(group * size, size)
            values = [load_row(grid_ref, field, row, group, size, rows) for row in range(rows)]

            def row_weights(row):
                return [weight_ref[row, part, place, :] for part in range(5)]

            for index, value in enumerate(heun_rows(values, row_weights)):
                keep_row(kept_ref, index, place, value)
            return carry

        lax.fori_loop(0, groups, one_group, 0)

        def store(slot, block, row, value):
            packed_ref[field, slot, block, row] = value

        if by_turn:
            for tile in range(tiles):
                raw_ref[field, tile] = kept_ref[tile].astype(raw_ref.dtype)
        else:
            pack_rows(kept_ref, turned_starts(start_ref, False, slots), blocks, store)
        for copy in halo_out(field) + field_out(field):
            copy.start()
        return carry

    lax.fori_loop(0, fields, one_field, 0)
    for field in range(fields):
        for copy in field_out(field):
            copy.wait()
    for array in range(fields + 2):
        for copy in halo_out(array):
            copy.wait()


def mirror_kernel(counts_ref, raw_ref, *refs):
    outs, (kept_ref, start_ref) = refs[:-2], refs[-2:]
    fields, tiles = raw_ref.shape[:2]
    keep_starts(counts_ref, start_ref)
    clear_tail(kept_ref, tiles)

    def one_field(field, carry):
        for tile in range(tiles):
            kept_ref[tile] = raw_ref[field, tile].astype(jnp.float32)

        def store(slot, block, row, value):
            outs[slot][field, block, row] = value

        starts = turned_starts(start_ref, True, len(outs))
        pack_rows(kept_ref, starts, outs[0].shape[1], store)
        return carry

    lax.fori_loop(0, fields, one_field, 0)


def edge_kernel(
    rows,
    by_turn,
    counts_ref,
    fields_ref,
    winds_ref,
    before_ref,
    after_ref,
    *refs,
):
    outs, scratch = refs[:-6], refs[-6:]
    grid_ref, weight_ref, kept_ref, sems, start_ref, halo_ref = scratch
    fields = fields_ref.shape[0]
    owners = start_ref.shape[0]
    blocks = outs[0].shape[-4]
    levels = before_ref.shape[2]
    size = min(8, levels)
    groups = levels // size
    wait = start_grid(fields_ref, winds_ref, grid_ref, sems)
    clear_tail(kept_ref, grid_ref.shape[1])
    keep_starts(counts_ref, start_ref)
    count = 3 * HALO

    def run(array, group, top):
        own = range(2 * HALO) if top else range(rows - 2 * HALO, rows)
        own = [load_row(grid_ref, array, row, group, size, rows) for row in own]
        place = pl.ds(group * size, size)
        halo = [halo_ref[int(top), array, row, place, :] for row in range(HALO)]
        return halo + own if top else own + halo

    for side, ref in enumerate((after_ref, before_ref)):
        for array in range(fields + 2):
            for row in range(HALO):
                halo_ref[side, array, row] = ref[array, row].astype(jnp.float32)

    wait(fields)
    wait(fields + 1)
    for top in (True, False):
        wall = HALO if top else count - HALO
        band = lax.axis_index("lat")
        is_open = jnp.where(band == (0 if top else lax.axis_size("lat") - 1), 0.0, 1.0)

        def weights(group, carry):
            store_weights(
                weight_ref.at[int(top)],
                pl.ds(group * size, size),
                run(fields, group, top),
                run(fields + 1, group, top),
                (wall, is_open),
            )
            return carry

        lax.fori_loop(0, groups, weights, 0)

    def one_field(field, carry):
        wait(field)

        def one_group(group, carry):
            place = pl.ds(group * size, size)
            for top in (True, False):
                side = int(top)

                def row_weights(row):
                    return [weight_ref[side, row, part, place, :] for part in range(5)]

                done = heun_rows(run(field, group, top), row_weights)
                for index, value in enumerate(done):
                    keep_row(kept_ref, index + (0 if top else HALO), place, value)
            return carry

        lax.fori_loop(0, groups, one_group, 0)

        def store(slot, block, row, value):
            if by_turn:
                outs[slot][field, block, row] = value
            else:
                outs[0][slot, field, block, row] = value

        pack_rows(kept_ref, turned_starts(start_ref, by_turn, owners), blocks, store)
        return carry

    lax.fori_loop(0, fields, one_field, 0)


def silu(x):
    half = 0.5 * x
    return half + half * jnp.tanh(half)


def dot(a, b):
    return jnp.dot(a, b, preferred_element_type=jnp.float32)


def gathered(block_ref, field):
    sources, _, _, rows = block_ref.shape[:4]
    by_row = [
        jnp.concatenate([block_ref[source, field, 0, row] for source in range(sources)], axis=0)
        for row in range(rows)
    ]
    return jnp.concatenate(by_row, axis=1)


def sort_turns(own, refs, sorted_ref):
    fields, _, rows, levels, _ = refs[0].shape
    for turn, ref in enumerate(refs):
        place = pl.ds(pl.multiple_of((own ^ turn) * levels, levels), levels)
        for field in range(fields):
            for row in range(rows):
                sorted_ref[field, place, row * LANES : (row + 1) * LANES] = ref[field, 0, row]


def column_update(columns, fields, remap_ref, first_ref, second_ref, third_ref):
    remapped = []
    for field in range(fields):
        values = columns(field)
        remapped.append(values.astype(jnp.float32) + dot(remap_ref[...], values))
    remapped = jnp.concatenate(remapped, axis=0)
    hidden = silu(dot(first_ref[...], remapped.astype(jnp.bfloat16))).astype(jnp.bfloat16)
    hidden = silu(dot(second_ref[...], hidden)).astype(jnp.bfloat16)
    tendency = dot(third_ref[...], hidden).astype(jnp.bfloat16).astype(jnp.float32)
    return remapped, tendency


def finished_row(remapped, tendency, listed, index, live):
    lanes = slice(index * LANES, (index + 1) * LANES)
    updated = remapped[:, lanes] + jnp.where(listed, tendency[:, lanes], 0.0)
    return jnp.where(live, updated, 0.0)


def live_lanes(counts_ref, features, block):
    lane = lax.broadcasted_iota(jnp.int32, (features, LANES), 1)
    return lane + block * LANES < counts_ref[0, lax.axis_index("lev")]


def is_listed(groups_ref, row):
    found = jnp.bool_(False)
    for owner in range(groups_ref.shape[0]):
        for index in range(groups_ref.shape[1]):
            found = found | (groups_ref[owner, index] == row)
    return found


def column_source(by_turn, refs, sorted_ref):
    if not by_turn:
        return functools.partial(gathered, refs[0])
    sort_turns(lax.axis_index("lev"), refs, sorted_ref)
    return lambda field: sorted_ref[field]


def turn_kernel(*refs):
    count = len(refs) // 2
    for source_ref, out_ref in zip(refs[:count], refs[count:]):
        out_ref[...] = source_ref[...].T


def half_kernel(rows, row_list, by_turn, groups_ref, counts_ref, *refs):
    out_ref, sorted_ref = refs[-2:]
    *refs, remap_ref, first_ref, second_ref, third_ref = refs[:-2]
    columns = column_source(by_turn, refs, sorted_ref)
    fields = sorted_ref.shape[0]
    remapped, tendency = column_update(
        columns, fields, remap_ref, first_ref, second_ref, third_ref
    )
    live = live_lanes(counts_ref, remapped.shape[0], pl.program_id(0))
    first_row = lax.axis_index("lat") * rows
    for index, row in enumerate(row_list):
        listed = is_listed(groups_ref, first_row + row)
        updated = finished_row(remapped, tendency, listed, index, live)
        out_ref[index] = updated.astype(jnp.bfloat16)


def last_kernel(row_list, done_list, by_turn, groups_ref, counts_ref, *refs):
    *refs, done_ref, remap_ref, first_ref, second_ref, third_ref, out_ref, tiles_ref, sorted_ref = (
        refs
    )
    features, rows, _ = out_ref.shape
    fields = sorted_ref.shape[0]
    columns = column_source(by_turn, refs, sorted_ref)
    remapped, tendency = column_update(
        columns, fields, remap_ref, first_ref, second_ref, third_ref
    )
    live = live_lanes(counts_ref, features, pl.program_id(0))
    first_row = lax.axis_index("lat") * rows
    for index, row in enumerate(done_list):
        tiles_ref[pl.ds(row, features, stride=rows), :] = done_ref[index].astype(jnp.float32)
    for index, row in enumerate(row_list):
        listed = is_listed(groups_ref, first_row + row)
        tiles_ref[pl.ds(row, features, stride=rows), :] = finished_row(
            remapped, tendency, listed, index, live
        )
    out_ref[...] = tiles_ref[...].reshape(features, rows, LANES).astype(jnp.bfloat16)


def shards(fields, winds, remap_weight, w_first, w_second, w_third, lon_counts, group_list):
    field_count, level_count, lat_rows, lon_total = fields.shape
    band_count = lax.axis_size("lat")
    owner_count = lax.axis_size("lev")
    all_levels = level_count * owner_count
    features = field_count * all_levels
    blocks = (2 * lon_total // owner_count + LANES - 1) // LANES
    slot_width = blocks * LANES
    inner_rows = tuple(range(HALO, lat_rows - HALO))
    edge_rows = tuple(range(HALO)) + tuple(range(lat_rows - HALO, lat_rows))
    half = len(inner_rows)
    stacked = field_count + 2
    tiles = lon_total // LANES
    smem = pl.BlockSpec(memory_space=pltpu.SMEM)
    anywhere = pl.BlockSpec(memory_space=pl.ANY)
    params = pltpu.CompilerParams(vmem_limit_bytes=60 * MIB)
    light = pltpu.CompilerParams(vmem_limit_bytes=24 * MIB)
    values = field_count * level_count * lat_rows * lon_total

    def payload(count):
        return (owner_count, field_count, count, half, level_count, LANES)

    flat_fields = fields.reshape(field_count, level_count * lat_rows, lon_total)
    flat_winds = winds.reshape(2, level_count * lat_rows, lon_total)
    halo_shape = jax.ShapeDtypeStruct((stacked, HALO, level_count, lon_total), jnp.bfloat16)

    def scratch(sides, count):
        return [
            pltpu.VMEM((stacked, tiles, level_count * lat_rows, LANES), jnp.float32),
            pltpu.VMEM(sides + (count - 1, 5, level_count, lon_total), jnp.float32),
            pltpu.VMEM((tiles + blocks, half, level_count, LANES), jnp.float32),
            pltpu.SemaphoreType.DMA((stacked, tiles)),
        ]

    by_turn = owner_count == 8
    near = owner_count // 2
    slots = near if by_turn else owner_count
    raw_shape = (field_count, tiles, half, level_count, LANES)
    piece = jax.ShapeDtypeStruct(payload(blocks)[1:], jnp.bfloat16)
    whole_payload = jax.ShapeDtypeStruct(payload(blocks), jnp.bfloat16)
    raw = jax.ShapeDtypeStruct(raw_shape, jnp.bfloat16)
    inner_shapes = [raw] if by_turn else [whole_payload]
    starts_scratch = pltpu.SMEM((owner_count,), jnp.int32)
    *inner, first, last = pl.pallas_call(
        functools.partial(inner_kernel, lat_rows, by_turn),
        in_specs=[smem, anywhere, anywhere],
        out_specs=[anywhere] * (len(inner_shapes) + 2),
        out_shape=inner_shapes + [halo_shape, halo_shape],
        scratch_shapes=scratch((), lat_rows)
        + [
            starts_scratch,
            pltpu.VMEM((field_count, slots) + payload(blocks)[2:], jnp.bfloat16),
            pltpu.VMEM(raw_shape, jnp.bfloat16),
            pltpu.VMEM((2,) + halo_shape.shape, halo_shape.dtype),
            pltpu.SemaphoreType.DMA((stacked, slots + 3)),
        ],
        compiler_params=params,
        cost_estimate=pl.CostEstimate(flops=1, bytes_accessed=1, transcendentals=0),
        name="inner_rows",
    )(lon_counts, flat_fields, flat_winds)

    up = [(i, i + 1) for i in range(band_count - 1)]
    down = [(j, i) for i, j in up]

    def exchange(x):
        return lax.all_to_all(x, "lev", split_axis=0, concat_axis=0, tiled=True)

    def turned_exchange(x, turn):
        return lax.ppermute(x, "lev", [(i, i ^ turn) for i in range(owner_count)]) if turn else x

    def pack_half(raw_rows):
        return pl.pallas_call(
            mirror_kernel,
            in_specs=[smem, pl.BlockSpec(memory_space=pltpu.VMEM)],
            out_shape=[piece] * near,
            scratch_shapes=[scratch((), lat_rows)[2], starts_scratch],
            compiler_params=light,
            cost_estimate=pl.CostEstimate(flops=1, bytes_accessed=1, transcendentals=0),
            name="half_slots",
        )(lon_counts, raw_rows)

    if by_turn:
        crossed = turned_exchange(inner[0], near + near // 2)
        inner_parts = [turned_exchange(x, turn) for turn, x in enumerate(pack_half(inner[0]))]
    else:
        inner_parts = [exchange(inner[0])]
    before = lax.ppermute(last, "lat", up)
    after = lax.ppermute(first, "lat", down)

    edge_shapes = [piece] * owner_count if by_turn else [whole_payload]
    edge = pl.pallas_call(
        functools.partial(edge_kernel, lat_rows, by_turn),
        in_specs=[smem, anywhere, anywhere] + [pl.BlockSpec(memory_space=pltpu.VMEM)] * 2,
        out_shape=edge_shapes,
        scratch_shapes=scratch((2,), 3 * HALO)
        + [
            starts_scratch,
            pltpu.VMEM((2,) + halo_shape.shape, jnp.float32),
        ],
        compiler_params=params,
        cost_estimate=pl.CostEstimate(flops=1, bytes_accessed=1, transcendentals=0),
        name="edge_rows",
    )(lon_counts, flat_fields, flat_winds, before, after)

    weights = (w_first, w_second, w_third)
    weights, _ = lax.optimization_barrier((weights, edge[0]))
    turned = pl.pallas_call(
        turn_kernel,
        in_specs=[pl.BlockSpec(memory_space=pltpu.VMEM)] * len(weights),
        out_shape=[jax.ShapeDtypeStruct(w.shape[::-1], w.dtype) for w in weights],
        compiler_params=light,
        cost_estimate=pl.CostEstimate(flops=1, bytes_accessed=1, transcendentals=0),
        name="turned_weights",
    )(*weights)
    if by_turn:
        edge = list(edge)
        edge[near:], _ = lax.optimization_barrier((edge[near:], turned))
        mirrored = pack_half(crossed)
        edge[2:near], mirrored = lax.optimization_barrier((edge[2:near], mirrored))
        near_parts = inner_parts[1:]
        near_parts, edge[near :] = lax.optimization_barrier((near_parts, edge[near :]))
        inner_parts = inner_parts[:1] + near_parts
        edge_parts = [turned_exchange(x, turn) for turn, x in enumerate(edge)]
        mirrored = [turned_exchange(x, turn) for turn, x in enumerate(mirrored)]
        inner_parts += [mirrored[turn ^ (near // 2)] for turn in range(near)]
    else:
        edge_parts = [exchange(edge[0])]

    def by_level(block):
        if level_count % 16 == 0:
            return block
        return block.transpose(1, 2, 3, 0, 4, 5).reshape(
            1, field_count, block.shape[2], half, all_levels, LANES
        )

    def block_spec(block):
        return pl.BlockSpec(
            block.shape[:2] + (1,) + block.shape[3:], lambda i: (0, 0, i, 0, 0, 0)
        )

    def cost(count):
        return pl.CostEstimate(flops=1, bytes_accessed=1, transcendentals=0)

    weight_specs = [pl.BlockSpec(memory_space=pltpu.VMEM)] * 4
    if by_turn:
        part_specs = [
            pl.BlockSpec((field_count, 1, half, level_count, LANES), lambda i: (0, i, 0, 0, 0))
        ] * owner_count
    else:
        inner_parts = [by_level(inner_parts[0])]
        edge_parts = [by_level(edge_parts[0])]
        part_specs = [block_spec(edge_parts[0])]
    sorted_scratch = pltpu.VMEM((field_count, all_levels, half * LANES), jnp.bfloat16)
    done_spec = pl.BlockSpec((half, features, LANES), lambda i: (0, 0, i))
    done = pl.pallas_call(
        functools.partial(half_kernel, lat_rows, inner_rows, by_turn),
        grid=(blocks,),
        in_specs=[smem, smem] + part_specs + weight_specs,
        out_specs=done_spec,
        out_shape=jax.ShapeDtypeStruct((half, features, slot_width), jnp.bfloat16),
        scratch_shapes=[sorted_scratch],
        compiler_params=light,
        cost_estimate=cost(blocks),
        name="inner_columns",
    )(group_list, lon_counts, *inner_parts, remap_weight, *turned)
    out = pl.pallas_call(
        functools.partial(last_kernel, edge_rows, inner_rows, by_turn),
        grid=(blocks,),
        in_specs=[smem, smem] + part_specs + [done_spec] + weight_specs,
        out_specs=pl.BlockSpec((features, lat_rows, LANES), lambda i: (0, 0, i)),
        out_shape=jax.ShapeDtypeStruct((features, lat_rows, slot_width), jnp.bfloat16),
        scratch_shapes=[pltpu.VMEM((features * lat_rows, LANES), jnp.float32), sorted_scratch],
        compiler_params=light,
        cost_estimate=cost(blocks),
        name="edge_columns",
    )(group_list, lon_counts, *edge_parts, done, remap_weight, *turned)
    return out.reshape(field_count, all_levels, lat_rows, slot_width)


def solution(mesh):
    in_specs = (
        P(None, "lev", "lat", None),
        P(None, "lev", "lat", None),
        P(),
        P(),
        P(),
        P(),
        P("lat", None),
        P(),
    )
    out_specs = P(None, None, "lat", "lev")
    return jax.shard_map(shards, mesh=mesh, in_specs=in_specs, out_specs=out_specs, check_vma=False)
```

```python
import functools

import jax
import jax.numpy as jnp
from jax import lax
from jax.experimental import pallas as pl
from jax.experimental.pallas import tpu as pltpu
from jax.sharding import PartitionSpec as P

DIFFUSION = 0.15
LANES = 128
HALO = 2
MIB = 1024 * 1024


def from_west(x):
    return pltpu.roll(x, 1, 1)


def from_east(x):
    return pltpu.roll(x, x.shape[1] - 1, 1)


def face_weights(before, after):
    half = 0.25 * (before + after)
    return half + DIFFUSION, half - DIFFUSION


def step_rows(values, rows, weights):
    result = {}
    for row in rows:
        here, west, away, above, below = weights(row)
        side = west * from_west(values[row]) + away * from_east(values[row])
        across = above * values[row - 1] + below * values[row + 1]
        result[row] = here * values[row] + (side + across)
    return result


def heun_rows(values, weights):
    count = len(values)
    predicted = step_rows(values, range(1, count - 1), weights)
    stepped = step_rows(predicted, range(2, count - 2), weights)
    return [0.5 * (values[row] + stepped[row]) for row in stepped]


def start_grid(fields_ref, winds_ref, grid_ref, sems):
    fields, tiles = fields_ref.shape[0], grid_ref.shape[1]

    def copy(array, tile, source):
        lanes = pl.ds(tile * LANES, LANES)
        return pltpu.make_async_copy(
            source.at[:, lanes], grid_ref.at[array, tile], sems.at[array, tile]
        )

    for wind in range(2):
        for tile in range(tiles):
            copy(fields + wind, tile, winds_ref.at[wind]).start()
    for field in range(fields):
        for tile in range(tiles):
            copy(field, tile, fields_ref.at[field]).start()

    def wait(array):
        for tile in range(tiles):
            copy(array, tile, fields_ref.at[0]).wait()

    return wait


def load_row(grid_ref, array, row, group, size, rows):
    start = group * (size * rows) + row
    pieces = [
        grid_ref[array, tile, pl.ds(start, size, stride=rows), :]
        for tile in range(grid_ref.shape[1])
    ]
    return jnp.concatenate(pieces, axis=1)


def store_weights(weight_ref, levels, east_winds, north_winds, wall=None):
    count = len(north_winds)
    faces = {}
    for face in range(1, count):
        pair = face_weights(north_winds[face - 1], north_winds[face])
        shut = wall is not None and wall[0] == face
        faces[face] = [part * wall[1] for part in pair] if shut else pair
    for row in range(1, count - 1):
        west, own = face_weights(from_west(east_winds[row]), east_winds[row])
        here = 1.0 + (own - from_east(west)) + (faces[row][1] - faces[row + 1][0])
        parts = (here, west, -from_east(own), faces[row][0], -faces[row + 1][1])
        for part, value in enumerate(parts):
            weight_ref[row, part, levels, :] = value


def keep_row(kept_ref, index, levels, value):
    for tile in range(value.shape[1] // LANES):
        kept_ref[tile, index, levels, :] = value[:, tile * LANES : (tile + 1) * LANES]


def clear_tail(kept_ref, tiles):
    for tile in range(tiles, kept_ref.shape[0]):
        kept_ref[tile] = jnp.zeros(kept_ref.shape[1:], kept_ref.dtype)


def keep_starts(counts_ref, start_ref):
    total = jnp.int32(0)
    for owner in range(start_ref.shape[0]):
        start_ref[owner] = total
        total = total + counts_ref[0, owner]


def turned_starts(start_ref, by_turn, slots):
    own = lax.axis_index("lev") if by_turn else 0
    return [start_ref[own ^ turn] for turn in range(slots)]


def pack_rows(kept_ref, starts, blocks, store):
    _, rows, levels, _ = kept_ref.shape
    lane = lax.broadcasted_iota(jnp.int32, (levels, LANES), 1)
    for slot, start in enumerate(starts):
        tile = start // LANES
        inside = start - tile * LANES
        shift = (LANES - inside) % LANES
        keep = lane < LANES - inside
        for row in range(rows):
            turned = [
                pltpu.roll(kept_ref[tile + j, row], shift, 1) for j in range(blocks + 1)
            ]
            for j in range(blocks):
                joined = jnp.where(keep, turned[j], turned[j + 1])
                store(slot, j, row, joined.astype(jnp.bfloat16))


def inner_kernel(
    rows,
    by_turn,
    counts_ref,
    fields_ref,
    winds_ref,
    *refs,
):
    outs, scratch = refs[:-9], refs[-9:]
    grid_ref, weight_ref, kept_ref, sems = scratch[:4]
    start_ref, packed_ref, raw_ref, halo_ref, sent = scratch[4:]
    *outs, first_ref, last_ref = outs
    fields = fields_ref.shape[0]
    owners = start_ref.shape[0]
    _, slots, blocks, _, levels, _ = packed_ref.shape
    tiles = grid_ref.shape[1]
    size = min(8, levels)
    groups = levels // size
    wait = start_grid(fields_ref, winds_ref, grid_ref, sems)
    clear_tail(kept_ref, grid_ref.shape[1])
    keep_starts(counts_ref, start_ref)

    def field_out(field):
        if not by_turn:
            return [
                pltpu.make_async_copy(
                    packed_ref.at[field], outs[0].at[:, field], sent.at[field, 0]
                )
            ]
        return [pltpu.make_async_copy(raw_ref.at[field], outs[0].at[field], sent.at[field, 0])]

    def keep_halo(array):
        for row in range(HALO):
            for side, source in enumerate((row, rows - HALO + row)):
                value = [
                    load_row(grid_ref, array, source, group, size, rows) for group in range(groups)
                ]
                halo_ref[side, array, row] = jnp.concatenate(value, axis=0).astype(halo_ref.dtype)

    def halo_out(array):
        return [
            pltpu.make_async_copy(
                halo_ref.at[side, array], ref.at[array], sent.at[array, slots + 1 + side]
            )
            for side, ref in enumerate((first_ref, last_ref))
        ]

    wait(fields)
    wait(fields + 1)

    def weights(group, carry):
        east = [load_row(grid_ref, fields, row, group, size, rows) for row in range(rows)]
        north = [load_row(grid_ref, fields + 1, row, group, size, rows) for row in range(rows)]
        store_weights(weight_ref, pl.ds(group * size, size), east, north)
        return carry

    lax.fori_loop(0, groups, weights, 0)
    for array in (fields, fields + 1):
        keep_halo(array)
        for copy in halo_out(array):
            copy.start()

    def one_field(field, carry):
        wait(field)
        keep_halo(field)

        def one_group(group, carry):
            place = pl.ds(group * size, size)
            values = [load_row(grid_ref, field, row, group, size, rows) for row in range(rows)]

            def row_weights(row):
                return [weight_ref[row, part, place, :] for part in range(5)]

            for index, value in enumerate(heun_rows(values, row_weights)):
                keep_row(kept_ref, index, place, value)
            return carry

        lax.fori_loop(0, groups, one_group, 0)

        def store(slot, block, row, value):
            packed_ref[field, slot, block, row] = value

        if by_turn:
            for tile in range(tiles):
                raw_ref[field, tile] = kept_ref[tile].astype(raw_ref.dtype)
        else:
            pack_rows(kept_ref, turned_starts(start_ref, False, slots), blocks, store)
        for copy in halo_out(field) + field_out(field):
            copy.start()
        return carry

    lax.fori_loop(0, fields, one_field, 0)
    for field in range(fields):
        for copy in field_out(field):
            copy.wait()
    for array in range(fields + 2):
        for copy in halo_out(array):
            copy.wait()


def mirror_kernel(counts_ref, raw_ref, *refs):
    outs, (kept_ref, start_ref) = refs[:-2], refs[-2:]
    fields, tiles = raw_ref.shape[:2]
    keep_starts(counts_ref, start_ref)
    clear_tail(kept_ref, tiles)

    def one_field(field, carry):
        for tile in range(tiles):
            kept_ref[tile] = raw_ref[field, tile].astype(jnp.float32)

        def store(slot, block, row, value):
            outs[slot][field, block, row] = value

        starts = turned_starts(start_ref, True, len(outs))
        pack_rows(kept_ref, starts, outs[0].shape[1], store)
        return carry

    lax.fori_loop(0, fields, one_field, 0)


def edge_kernel(
    rows,
    by_turn,
    counts_ref,
    fields_ref,
    winds_ref,
    before_ref,
    after_ref,
    *refs,
):
    outs, scratch = refs[:-6], refs[-6:]
    grid_ref, weight_ref, kept_ref, sems, start_ref, halo_ref = scratch
    fields = fields_ref.shape[0]
    owners = start_ref.shape[0]
    blocks = outs[0].shape[-4]
    levels = before_ref.shape[2]
    size = min(8, levels)
    groups = levels // size
    wait = start_grid(fields_ref, winds_ref, grid_ref, sems)
    clear_tail(kept_ref, grid_ref.shape[1])
    keep_starts(counts_ref, start_ref)
    count = 3 * HALO

    def run(array, group, top):
        own = range(2 * HALO) if top else range(rows - 2 * HALO, rows)
        own = [load_row(grid_ref, array, row, group, size, rows) for row in own]
        place = pl.ds(group * size, size)
        halo = [halo_ref[int(top), array, row, place, :] for row in range(HALO)]
        return halo + own if top else own + halo

    for side, ref in enumerate((after_ref, before_ref)):
        for array in range(fields + 2):
            for row in range(HALO):
                halo_ref[side, array, row] = ref[array, row].astype(jnp.float32)

    wait(fields)
    wait(fields + 1)
    for top in (True, False):
        wall = HALO if top else count - HALO
        band = lax.axis_index("lat")
        is_open = jnp.where(band == (0 if top else lax.axis_size("lat") - 1), 0.0, 1.0)

        def weights(group, carry):
            store_weights(
                weight_ref.at[int(top)],
                pl.ds(group * size, size),
                run(fields, group, top),
                run(fields + 1, group, top),
                (wall, is_open),
            )
            return carry

        lax.fori_loop(0, groups, weights, 0)

    def one_field(field, carry):
        wait(field)

        def one_group(group, carry):
            place = pl.ds(group * size, size)
            for top in (True, False):
                side = int(top)

                def row_weights(row):
                    return [weight_ref[side, row, part, place, :] for part in range(5)]

                done = heun_rows(run(field, group, top), row_weights)
                for index, value in enumerate(done):
                    keep_row(kept_ref, index + (0 if top else HALO), place, value)
            return carry

        lax.fori_loop(0, groups, one_group, 0)

        def store(slot, block, row, value):
            if by_turn:
                outs[slot][field, block, row] = value
            else:
                outs[0][slot, field, block, row] = value

        pack_rows(kept_ref, turned_starts(start_ref, by_turn, owners), blocks, store)
        return carry

    lax.fori_loop(0, fields, one_field, 0)


def silu(x):
    half = 0.5 * x
    return half + half * jnp.tanh(half)


def dot(a, b):
    return jnp.dot(a, b, preferred_element_type=jnp.float32)


def gathered(block_ref, field):
    sources, _, _, rows = block_ref.shape[:4]
    by_row = [
        jnp.concatenate([block_ref[source, field, 0, row] for source in range(sources)], axis=0)
        for row in range(rows)
    ]
    return jnp.concatenate(by_row, axis=1)


def sort_turns(own, refs, sorted_ref):
    fields, _, rows, levels, _ = refs[0].shape
    for turn, ref in enumerate(refs):
        place = pl.ds(pl.multiple_of((own ^ turn) * levels, levels), levels)
        for field in range(fields):
            for row in range(rows):
                sorted_ref[field, place, row * LANES : (row + 1) * LANES] = ref[field, 0, row]


def column_update(columns, fields, remap_ref, first_ref, second_ref, third_ref):
    remapped = []
    for field in range(fields):
        values = columns(field)
        remapped.append(values.astype(jnp.float32) + dot(remap_ref[...], values))
    remapped = jnp.concatenate(remapped, axis=0)
    hidden = silu(dot(first_ref[...], remapped.astype(jnp.bfloat16))).astype(jnp.bfloat16)
    hidden = silu(dot(second_ref[...], hidden)).astype(jnp.bfloat16)
    tendency = dot(third_ref[...], hidden).astype(jnp.bfloat16).astype(jnp.float32)
    return remapped, tendency


def finished_row(remapped, tendency, listed, index, live):
    lanes = slice(index * LANES, (index + 1) * LANES)
    updated = remapped[:, lanes] + jnp.where(listed, tendency[:, lanes], 0.0)
    return jnp.where(live, updated, 0.0)


def live_lanes(counts_ref, features, block):
    lane = lax.broadcasted_iota(jnp.int32, (features, LANES), 1)
    return lane + block * LANES < counts_ref[0, lax.axis_index("lev")]


def is_listed(groups_ref, row):
    found = jnp.bool_(False)
    for owner in range(groups_ref.shape[0]):
        for index in range(groups_ref.shape[1]):
            found = found | (groups_ref[owner, index] == row)
    return found


def column_source(by_turn, refs, sorted_ref):
    if not by_turn:
        return functools.partial(gathered, refs[0])
    sort_turns(lax.axis_index("lev"), refs, sorted_ref)
    return lambda field: sorted_ref[field]


def turn_kernel(*refs):
    count = len(refs) // 2
    for source_ref, out_ref in zip(refs[:count], refs[count:]):
        out_ref[...] = source_ref[...].T


def half_kernel(rows, row_list, by_turn, groups_ref, counts_ref, *refs):
    out_ref, sorted_ref = refs[-2:]
    *refs, remap_ref, first_ref, second_ref, third_ref = refs[:-2]
    columns = column_source(by_turn, refs, sorted_ref)
    fields = sorted_ref.shape[0]
    remapped, tendency = column_update(
        columns, fields, remap_ref, first_ref, second_ref, third_ref
    )
    live = live_lanes(counts_ref, remapped.shape[0], pl.program_id(0))
    first_row = lax.axis_index("lat") * rows
    for index, row in enumerate(row_list):
        listed = is_listed(groups_ref, first_row + row)
        updated = finished_row(remapped, tendency, listed, index, live)
        out_ref[index] = updated.astype(jnp.bfloat16)


def last_kernel(row_list, done_list, by_turn, groups_ref, counts_ref, *refs):
    *refs, done_ref, remap_ref, first_ref, second_ref, third_ref, out_ref, tiles_ref, sorted_ref = (
        refs
    )
    features, rows, _ = out_ref.shape
    fields = sorted_ref.shape[0]
    columns = column_source(by_turn, refs, sorted_ref)
    remapped, tendency = column_update(
        columns, fields, remap_ref, first_ref, second_ref, third_ref
    )
    live = live_lanes(counts_ref, features, pl.program_id(0))
    first_row = lax.axis_index("lat") * rows
    for index, row in enumerate(done_list):
        tiles_ref[pl.ds(row, features, stride=rows), :] = done_ref[index].astype(jnp.float32)
    for index, row in enumerate(row_list):
        listed = is_listed(groups_ref, first_row + row)
        tiles_ref[pl.ds(row, features, stride=rows), :] = finished_row(
            remapped, tendency, listed, index, live
        )
    out_ref[...] = tiles_ref[...].reshape(features, rows, LANES).astype(jnp.bfloat16)


def shards(fields, winds, remap_weight, w_first, w_second, w_third, lon_counts, group_list):
    field_count, level_count, lat_rows, lon_total = fields.shape
    band_count = lax.axis_size("lat")
    owner_count = lax.axis_size("lev")
    all_levels = level_count * owner_count
    features = field_count * all_levels
    blocks = (2 * lon_total // owner_count + LANES - 1) // LANES
    slot_width = blocks * LANES
    inner_rows = tuple(range(HALO, lat_rows - HALO))
    edge_rows = tuple(range(HALO)) + tuple(range(lat_rows - HALO, lat_rows))
    half = len(inner_rows)
    stacked = field_count + 2
    tiles = lon_total // LANES
    smem = pl.BlockSpec(memory_space=pltpu.SMEM)
    anywhere = pl.BlockSpec(memory_space=pl.ANY)
    params = pltpu.CompilerParams(vmem_limit_bytes=60 * MIB)
    light = pltpu.CompilerParams(vmem_limit_bytes=24 * MIB)
    values = field_count * level_count * lat_rows * lon_total

    def payload(count):
        return (owner_count, field_count, count, half, level_count, LANES)

    flat_fields = fields.reshape(field_count, level_count * lat_rows, lon_total)
    flat_winds = winds.reshape(2, level_count * lat_rows, lon_total)
    halo_shape = jax.ShapeDtypeStruct((stacked, HALO, level_count, lon_total), jnp.bfloat16)

    def scratch(sides, count):
        return [
            pltpu.VMEM((stacked, tiles, level_count * lat_rows, LANES), jnp.float32),
            pltpu.VMEM(sides + (count - 1, 5, level_count, lon_total), jnp.float32),
            pltpu.VMEM((tiles + blocks, half, level_count, LANES), jnp.float32),
            pltpu.SemaphoreType.DMA((stacked, tiles)),
        ]

    by_turn = owner_count == 8
    near = owner_count // 2
    slots = near if by_turn else owner_count
    raw_shape = (field_count, tiles, half, level_count, LANES)
    piece = jax.ShapeDtypeStruct(payload(blocks)[1:], jnp.bfloat16)
    whole_payload = jax.ShapeDtypeStruct(payload(blocks), jnp.bfloat16)
    raw = jax.ShapeDtypeStruct(raw_shape, jnp.bfloat16)
    inner_shapes = [raw] if by_turn else [whole_payload]
    starts_scratch = pltpu.SMEM((owner_count,), jnp.int32)
    *inner, first, last = pl.pallas_call(
        functools.partial(inner_kernel, lat_rows, by_turn),
        in_specs=[smem, anywhere, anywhere],
        out_specs=[anywhere] * (len(inner_shapes) + 2),
        out_shape=inner_shapes + [halo_shape, halo_shape],
        scratch_shapes=scratch((), lat_rows)
        + [
            starts_scratch,
            pltpu.VMEM((field_count, slots) + payload(blocks)[2:], jnp.bfloat16),
            pltpu.VMEM(raw_shape, jnp.bfloat16),
            pltpu.VMEM((2,) + halo_shape.shape, halo_shape.dtype),
            pltpu.SemaphoreType.DMA((stacked, slots + 3)),
        ],
        compiler_params=params,
        cost_estimate=pl.CostEstimate(flops=1, bytes_accessed=1, transcendentals=0),
        name="inner_rows",
    )(lon_counts, flat_fields, flat_winds)

    up = [(i, i + 1) for i in range(band_count - 1)]
    down = [(j, i) for i, j in up]

    def exchange(x):
        return lax.all_to_all(x, "lev", split_axis=0, concat_axis=0, tiled=True)

    def turned_exchange(x, turn):
        return lax.ppermute(x, "lev", [(i, i ^ turn) for i in range(owner_count)]) if turn else x

    def pack_half(raw_rows):
        return pl.pallas_call(
            mirror_kernel,
            in_specs=[smem, pl.BlockSpec(memory_space=pltpu.VMEM)],
            out_shape=[piece] * near,
            scratch_shapes=[scratch((), lat_rows)[2], starts_scratch],
            compiler_params=light,
            cost_estimate=pl.CostEstimate(flops=1, bytes_accessed=1, transcendentals=0),
            name="half_slots",
        )(lon_counts, raw_rows)

    if by_turn:
        crossed = turned_exchange(inner[0], near + near // 2)
        inner_parts = [turned_exchange(x, turn) for turn, x in enumerate(pack_half(inner[0]))]
    else:
        inner_parts = [exchange(inner[0])]
    before = lax.ppermute(last, "lat", up)
    after = lax.ppermute(first, "lat", down)

    edge_shapes = [piece] * owner_count if by_turn else [whole_payload]
    edge = pl.pallas_call(
        functools.partial(edge_kernel, lat_rows, by_turn),
        in_specs=[smem, anywhere, anywhere] + [pl.BlockSpec(memory_space=pltpu.VMEM)] * 2,
        out_shape=edge_shapes,
        scratch_shapes=scratch((2,), 3 * HALO)
        + [
            starts_scratch,
            pltpu.VMEM((2,) + halo_shape.shape, jnp.float32),
        ],
        compiler_params=params,
        cost_estimate=pl.CostEstimate(flops=1, bytes_accessed=1, transcendentals=0),
        name="edge_rows",
    )(lon_counts, flat_fields, flat_winds, before, after)

    weights = (w_first, w_second, w_third)
    weights, _ = lax.optimization_barrier((weights, edge[0]))
    turned = pl.pallas_call(
        turn_kernel,
        in_specs=[pl.BlockSpec(memory_space=pltpu.VMEM)] * len(weights),
        out_shape=[jax.ShapeDtypeStruct(w.shape[::-1], w.dtype) for w in weights],
        compiler_params=light,
        cost_estimate=pl.CostEstimate(flops=1, bytes_accessed=1, transcendentals=0),
        name="turned_weights",
    )(*weights)
    if by_turn:
        edge = list(edge)
        edge[near:], _ = lax.optimization_barrier((edge[near:], turned))
        mirrored = pack_half(crossed)
        edge[2:near], mirrored = lax.optimization_barrier((edge[2:near], mirrored))
        near_parts = inner_parts[1:]
        near_parts, edge[near + 1 :] = lax.optimization_barrier(
            (near_parts, edge[near + 1 :])
        )
        inner_parts = inner_parts[:1] + near_parts
        edge_parts = [turned_exchange(x, turn) for turn, x in enumerate(edge)]
        mirrored = [turned_exchange(x, turn) for turn, x in enumerate(mirrored)]
        inner_parts += [mirrored[turn ^ (near // 2)] for turn in range(near)]
    else:
        edge_parts = [exchange(edge[0])]

    def by_level(block):
        if level_count % 16 == 0:
            return block
        return block.transpose(1, 2, 3, 0, 4, 5).reshape(
            1, field_count, block.shape[2], half, all_levels, LANES
        )

    def block_spec(block):
        return pl.BlockSpec(
            block.shape[:2] + (1,) + block.shape[3:], lambda i: (0, 0, i, 0, 0, 0)
        )

    def cost(count):
        return pl.CostEstimate(flops=1, bytes_accessed=1, transcendentals=0)

    weight_specs = [pl.BlockSpec(memory_space=pltpu.VMEM)] * 4
    if by_turn:
        part_specs = [
            pl.BlockSpec((field_count, 1, half, level_count, LANES), lambda i: (0, i, 0, 0, 0))
        ] * owner_count
    else:
        inner_parts = [by_level(inner_parts[0])]
        edge_parts = [by_level(edge_parts[0])]
        part_specs = [block_spec(edge_parts[0])]
    sorted_scratch = pltpu.VMEM((field_count, all_levels, half * LANES), jnp.bfloat16)
    done_spec = pl.BlockSpec((half, features, LANES), lambda i: (0, 0, i))
    done = pl.pallas_call(
        functools.partial(half_kernel, lat_rows, inner_rows, by_turn),
        grid=(blocks,),
        in_specs=[smem, smem] + part_specs + weight_specs,
        out_specs=done_spec,
        out_shape=jax.ShapeDtypeStruct((half, features, slot_width), jnp.bfloat16),
        scratch_shapes=[sorted_scratch],
        compiler_params=light,
        cost_estimate=cost(blocks),
        name="inner_columns",
    )(group_list, lon_counts, *inner_parts, remap_weight, *turned)
    out = pl.pallas_call(
        functools.partial(last_kernel, edge_rows, inner_rows, by_turn),
        grid=(blocks,),
        in_specs=[smem, smem] + part_specs + [done_spec] + weight_specs,
        out_specs=pl.BlockSpec((features, lat_rows, LANES), lambda i: (0, 0, i)),
        out_shape=jax.ShapeDtypeStruct((features, lat_rows, slot_width), jnp.bfloat16),
        scratch_shapes=[pltpu.VMEM((features * lat_rows, LANES), jnp.float32), sorted_scratch],
        compiler_params=light,
        cost_estimate=cost(blocks),
        name="edge_columns",
    )(group_list, lon_counts, *edge_parts, done, remap_weight, *turned)
    return out.reshape(field_count, all_levels, lat_rows, slot_width)


def solution(mesh):
    in_specs = (
        P(None, "lev", "lat", None),
        P(None, "lev", "lat", None),
        P(),
        P(),
        P(),
        P(),
        P("lat", None),
        P(),
    )
    out_specs = P(None, None, "lat", "lev")
    return jax.shard_map(shards, mesh=mesh, in_specs=in_specs, out_specs=out_specs, check_vma=False)
```

```python
import functools

import jax
import jax.numpy as jnp
from jax import lax
from jax.experimental import pallas as pl
from jax.experimental.pallas import tpu as pltpu
from jax.sharding import PartitionSpec as P

DIFFUSION = 0.15
LANES = 128
HALO = 2
MIB = 1024 * 1024


def from_west(x):
    return pltpu.roll(x, 1, 1)


def from_east(x):
    return pltpu.roll(x, x.shape[1] - 1, 1)


def face_weights(before, after):
    half = 0.25 * (before + after)
    return half + DIFFUSION, half - DIFFUSION


def step_rows(values, rows, weights):
    result = {}
    for row in rows:
        here, west, away, above, below = weights(row)
        side = west * from_west(values[row]) + away * from_east(values[row])
        across = above * values[row - 1] + below * values[row + 1]
        result[row] = here * values[row] + (side + across)
    return result


def heun_rows(values, weights):
    count = len(values)
    predicted = step_rows(values, range(1, count - 1), weights)
    stepped = step_rows(predicted, range(2, count - 2), weights)
    return [0.5 * (values[row] + stepped[row]) for row in stepped]


def start_grid(fields_ref, winds_ref, grid_ref, sems):
    fields, tiles = fields_ref.shape[0], grid_ref.shape[1]

    def copy(array, tile, source):
        lanes = pl.ds(tile * LANES, LANES)
        return pltpu.make_async_copy(
            source.at[:, lanes], grid_ref.at[array, tile], sems.at[array, tile]
        )

    for wind in range(2):
        for tile in range(tiles):
            copy(fields + wind, tile, winds_ref.at[wind]).start()
    for field in range(fields):
        for tile in range(tiles):
            copy(field, tile, fields_ref.at[field]).start()

    def wait(array):
        for tile in range(tiles):
            copy(array, tile, fields_ref.at[0]).wait()

    return wait


def load_row(grid_ref, array, row, group, size, rows):
    start = group * (size * rows) + row
    pieces = [
        grid_ref[array, tile, pl.ds(start, size, stride=rows), :]
        for tile in range(grid_ref.shape[1])
    ]
    return jnp.concatenate(pieces, axis=1)


def store_weights(weight_ref, levels, east_winds, north_winds, wall=None):
    count = len(north_winds)
    faces = {}
    for face in range(1, count):
        pair = face_weights(north_winds[face - 1], north_winds[face])
        shut = wall is not None and wall[0] == face
        faces[face] = [part * wall[1] for part in pair] if shut else pair
    for row in range(1, count - 1):
        west, own = face_weights(from_west(east_winds[row]), east_winds[row])
        here = 1.0 + (own - from_east(west)) + (faces[row][1] - faces[row + 1][0])
        parts = (here, west, -from_east(own), faces[row][0], -faces[row + 1][1])
        for part, value in enumerate(parts):
            weight_ref[row, part, levels, :] = value


def keep_row(kept_ref, index, levels, value):
    for tile in range(value.shape[1] // LANES):
        kept_ref[tile, index, levels, :] = value[:, tile * LANES : (tile + 1) * LANES]


def clear_tail(kept_ref, tiles):
    for tile in range(tiles, kept_ref.shape[0]):
        kept_ref[tile] = jnp.zeros(kept_ref.shape[1:], kept_ref.dtype)


def keep_starts(counts_ref, start_ref):
    total = jnp.int32(0)
    for owner in range(start_ref.shape[0]):
        start_ref[owner] = total
        total = total + counts_ref[0, owner]


def turned_starts(start_ref, by_turn, slots):
    own = lax.axis_index("lev") if by_turn else 0
    return [start_ref[own ^ turn] for turn in range(slots)]


def pack_rows(kept_ref, starts, blocks, store):
    _, rows, levels, _ = kept_ref.shape
    lane = lax.broadcasted_iota(jnp.int32, (levels, LANES), 1)
    for slot, start in enumerate(starts):
        tile = start // LANES
        inside = start - tile * LANES
        shift = (LANES - inside) % LANES
        keep = lane < LANES - inside
        for row in range(rows):
            turned = [
                pltpu.roll(kept_ref[tile + j, row], shift, 1) for j in range(blocks + 1)
            ]
            for j in range(blocks):
                joined = jnp.where(keep, turned[j], turned[j + 1])
                store(slot, j, row, joined.astype(jnp.bfloat16))


def inner_kernel(
    rows,
    by_turn,
    counts_ref,
    fields_ref,
    winds_ref,
    *refs,
):
    outs, scratch = refs[:-9], refs[-9:]
    grid_ref, weight_ref, kept_ref, sems = scratch[:4]
    start_ref, packed_ref, raw_ref, halo_ref, sent = scratch[4:]
    *outs, first_ref, last_ref = outs
    fields = fields_ref.shape[0]
    owners = start_ref.shape[0]
    _, slots, blocks, _, levels, _ = packed_ref.shape
    tiles = grid_ref.shape[1]
    size = min(8, levels)
    groups = levels // size
    wait = start_grid(fields_ref, winds_ref, grid_ref, sems)
    clear_tail(kept_ref, grid_ref.shape[1])
    keep_starts(counts_ref, start_ref)

    def field_out(field):
        if not by_turn:
            return [
                pltpu.make_async_copy(
                    packed_ref.at[field], outs[0].at[:, field], sent.at[field, 0]
                )
            ]
        return [pltpu.make_async_copy(raw_ref.at[field], outs[0].at[field], sent.at[field, 0])]

    def keep_halo(array):
        for row in range(HALO):
            for side, source in enumerate((row, rows - HALO + row)):
                value = [
                    load_row(grid_ref, array, source, group, size, rows) for group in range(groups)
                ]
                halo_ref[side, array, row] = jnp.concatenate(value, axis=0).astype(halo_ref.dtype)

    def halo_out(array):
        return [
            pltpu.make_async_copy(
                halo_ref.at[side, array], ref.at[array], sent.at[array, slots + 1 + side]
            )
            for side, ref in enumerate((first_ref, last_ref))
        ]

    wait(fields)
    wait(fields + 1)

    def weights(group, carry):
        east = [load_row(grid_ref, fields, row, group, size, rows) for row in range(rows)]
        north = [load_row(grid_ref, fields + 1, row, group, size, rows) for row in range(rows)]
        store_weights(weight_ref, pl.ds(group * size, size), east, north)
        return carry

    lax.fori_loop(0, groups, weights, 0)
    for array in (fields, fields + 1):
        keep_halo(array)
        for copy in halo_out(array):
            copy.start()

    def one_field(field, carry):
        wait(field)

        def one_group(group, carry):
            place = pl.ds(group * size, size)
            values = [load_row(grid_ref, field, row, group, size, rows) for row in range(rows)]

            def row_weights(row):
                return [weight_ref[row, part, place, :] for part in range(5)]

            for index, value in enumerate(heun_rows(values, row_weights)):
                keep_row(kept_ref, index, place, value)
            return carry

        lax.fori_loop(0, groups, one_group, 0)

        def store(slot, block, row, value):
            packed_ref[field, slot, block, row] = value

        if by_turn:
            for tile in range(tiles):
                raw_ref[field, tile] = kept_ref[tile].astype(raw_ref.dtype)
        else:
            pack_rows(kept_ref, turned_starts(start_ref, False, slots), blocks, store)
        for copy in field_out(field):
            copy.start()
        return carry

    lax.fori_loop(0, fields, one_field, 0)
    for field in range(fields):
        keep_halo(field)
        for copy in halo_out(field):
            copy.start()
    for field in range(fields):
        for copy in field_out(field):
            copy.wait()
    for array in range(fields + 2):
        for copy in halo_out(array):
            copy.wait()


def mirror_kernel(counts_ref, raw_ref, *refs):
    outs, (kept_ref, start_ref) = refs[:-2], refs[-2:]
    fields, tiles = raw_ref.shape[:2]
    keep_starts(counts_ref, start_ref)
    clear_tail(kept_ref, tiles)

    def one_field(field, carry):
        for tile in range(tiles):
            kept_ref[tile] = raw_ref[field, tile].astype(jnp.float32)

        def store(slot, block, row, value):
            outs[slot][field, block, row] = value

        starts = turned_starts(start_ref, True, len(outs))
        pack_rows(kept_ref, starts, outs[0].shape[1], store)
        return carry

    lax.fori_loop(0, fields, one_field, 0)


def edge_kernel(
    rows,
    by_turn,
    counts_ref,
    fields_ref,
    winds_ref,
    before_ref,
    after_ref,
    *refs,
):
    outs, scratch = refs[:-6], refs[-6:]
    grid_ref, weight_ref, kept_ref, sems, start_ref, halo_ref = scratch
    fields = fields_ref.shape[0]
    owners = start_ref.shape[0]
    blocks = outs[0].shape[-4]
    levels = before_ref.shape[2]
    size = min(8, levels)
    groups = levels // size
    wait = start_grid(fields_ref, winds_ref, grid_ref, sems)
    clear_tail(kept_ref, grid_ref.shape[1])
    keep_starts(counts_ref, start_ref)
    count = 3 * HALO

    def run(array, group, top):
        own = range(2 * HALO) if top else range(rows - 2 * HALO, rows)
        own = [load_row(grid_ref, array, row, group, size, rows) for row in own]
        place = pl.ds(group * size, size)
        halo = [halo_ref[int(top), array, row, place, :] for row in range(HALO)]
        return halo + own if top else own + halo

    for side, ref in enumerate((after_ref, before_ref)):
        for array in range(fields + 2):
            for row in range(HALO):
                halo_ref[side, array, row] = ref[array, row].astype(jnp.float32)

    wait(fields)
    wait(fields + 1)
    for top in (True, False):
        wall = HALO if top else count - HALO
        band = lax.axis_index("lat")
        is_open = jnp.where(band == (0 if top else lax.axis_size("lat") - 1), 0.0, 1.0)

        def weights(group, carry):
            store_weights(
                weight_ref.at[int(top)],
                pl.ds(group * size, size),
                run(fields, group, top),
                run(fields + 1, group, top),
                (wall, is_open),
            )
            return carry

        lax.fori_loop(0, groups, weights, 0)

    def one_field(field, carry):
        wait(field)

        def one_group(group, carry):
            place = pl.ds(group * size, size)
            for top in (True, False):
                side = int(top)

                def row_weights(row):
                    return [weight_ref[side, row, part, place, :] for part in range(5)]

                done = heun_rows(run(field, group, top), row_weights)
                for index, value in enumerate(done):
                    keep_row(kept_ref, index + (0 if top else HALO), place, value)
            return carry

        lax.fori_loop(0, groups, one_group, 0)

        def store(slot, block, row, value):
            if by_turn:
                outs[slot][field, block, row] = value
            else:
                outs[0][slot, field, block, row] = value

        pack_rows(kept_ref, turned_starts(start_ref, by_turn, owners), blocks, store)
        return carry

    lax.fori_loop(0, fields, one_field, 0)


def silu(x):
    half = 0.5 * x
    return half + half * jnp.tanh(half)


def dot(a, b):
    return jnp.dot(a, b, preferred_element_type=jnp.float32)


def gathered(block_ref, field):
    sources, _, _, rows = block_ref.shape[:4]
    by_row = [
        jnp.concatenate([block_ref[source, field, 0, row] for source in range(sources)], axis=0)
        for row in range(rows)
    ]
    return jnp.concatenate(by_row, axis=1)


def sort_turns(own, refs, sorted_ref):
    fields, _, rows, levels, _ = refs[0].shape
    for turn, ref in enumerate(refs):
        place = pl.ds(pl.multiple_of((own ^ turn) * levels, levels), levels)
        for field in range(fields):
            for row in range(rows):
                sorted_ref[field, place, row * LANES : (row + 1) * LANES] = ref[field, 0, row]


def column_update(columns, fields, remap_ref, first_ref, second_ref, third_ref):
    remapped = []
    for field in range(fields):
        values = columns(field)
        remapped.append(values.astype(jnp.float32) + dot(remap_ref[...], values))
    remapped = jnp.concatenate(remapped, axis=0)
    hidden = silu(dot(first_ref[...], remapped.astype(jnp.bfloat16))).astype(jnp.bfloat16)
    hidden = silu(dot(second_ref[...], hidden)).astype(jnp.bfloat16)
    tendency = dot(third_ref[...], hidden).astype(jnp.bfloat16).astype(jnp.float32)
    return remapped, tendency


def finished_row(remapped, tendency, listed, index, live):
    lanes = slice(index * LANES, (index + 1) * LANES)
    updated = remapped[:, lanes] + jnp.where(listed, tendency[:, lanes], 0.0)
    return jnp.where(live, updated, 0.0)


def live_lanes(counts_ref, features, block):
    lane = lax.broadcasted_iota(jnp.int32, (features, LANES), 1)
    return lane + block * LANES < counts_ref[0, lax.axis_index("lev")]


def is_listed(groups_ref, row):
    found = jnp.bool_(False)
    for owner in range(groups_ref.shape[0]):
        for index in range(groups_ref.shape[1]):
            found = found | (groups_ref[owner, index] == row)
    return found


def column_source(by_turn, refs, sorted_ref):
    if not by_turn:
        return functools.partial(gathered, refs[0])
    sort_turns(lax.axis_index("lev"), refs, sorted_ref)
    return lambda field: sorted_ref[field]


def turn_kernel(*refs):
    count = len(refs) // 2
    for source_ref, out_ref in zip(refs[:count], refs[count:]):
        out_ref[...] = source_ref[...].T


def half_kernel(rows, row_list, by_turn, groups_ref, counts_ref, *refs):
    out_ref, sorted_ref = refs[-2:]
    *refs, remap_ref, first_ref, second_ref, third_ref = refs[:-2]
    columns = column_source(by_turn, refs, sorted_ref)
    fields = sorted_ref.shape[0]
    remapped, tendency = column_update(
        columns, fields, remap_ref, first_ref, second_ref, third_ref
    )
    live = live_lanes(counts_ref, remapped.shape[0], pl.program_id(0))
    first_row = lax.axis_index("lat") * rows
    for index, row in enumerate(row_list):
        listed = is_listed(groups_ref, first_row + row)
        updated = finished_row(remapped, tendency, listed, index, live)
        out_ref[index] = updated.astype(jnp.bfloat16)


def last_kernel(row_list, done_list, by_turn, groups_ref, counts_ref, *refs):
    *refs, done_ref, remap_ref, first_ref, second_ref, third_ref, out_ref, tiles_ref, sorted_ref = (
        refs
    )
    features, rows, _ = out_ref.shape
    fields = sorted_ref.shape[0]
    columns = column_source(by_turn, refs, sorted_ref)
    remapped, tendency = column_update(
        columns, fields, remap_ref, first_ref, second_ref, third_ref
    )
    live = live_lanes(counts_ref, features, pl.program_id(0))
    first_row = lax.axis_index("lat") * rows
    for index, row in enumerate(done_list):
        tiles_ref[pl.ds(row, features, stride=rows), :] = done_ref[index].astype(jnp.float32)
    for index, row in enumerate(row_list):
        listed = is_listed(groups_ref, first_row + row)
        tiles_ref[pl.ds(row, features, stride=rows), :] = finished_row(
            remapped, tendency, listed, index, live
        )
    out_ref[...] = tiles_ref[...].reshape(features, rows, LANES).astype(jnp.bfloat16)


def shards(fields, winds, remap_weight, w_first, w_second, w_third, lon_counts, group_list):
    field_count, level_count, lat_rows, lon_total = fields.shape
    band_count = lax.axis_size("lat")
    owner_count = lax.axis_size("lev")
    all_levels = level_count * owner_count
    features = field_count * all_levels
    blocks = (2 * lon_total // owner_count + LANES - 1) // LANES
    slot_width = blocks * LANES
    inner_rows = tuple(range(HALO, lat_rows - HALO))
    edge_rows = tuple(range(HALO)) + tuple(range(lat_rows - HALO, lat_rows))
    half = len(inner_rows)
    stacked = field_count + 2
    tiles = lon_total // LANES
    smem = pl.BlockSpec(memory_space=pltpu.SMEM)
    anywhere = pl.BlockSpec(memory_space=pl.ANY)
    params = pltpu.CompilerParams(vmem_limit_bytes=60 * MIB)
    light = pltpu.CompilerParams(vmem_limit_bytes=24 * MIB)
    values = field_count * level_count * lat_rows * lon_total

    def payload(count):
        return (owner_count, field_count, count, half, level_count, LANES)

    flat_fields = fields.reshape(field_count, level_count * lat_rows, lon_total)
    flat_winds = winds.reshape(2, level_count * lat_rows, lon_total)
    halo_shape = jax.ShapeDtypeStruct((stacked, HALO, level_count, lon_total), jnp.bfloat16)

    def scratch(sides, count):
        return [
            pltpu.VMEM((stacked, tiles, level_count * lat_rows, LANES), jnp.float32),
            pltpu.VMEM(sides + (count - 1, 5, level_count, lon_total), jnp.float32),
            pltpu.VMEM((tiles + blocks, half, level_count, LANES), jnp.float32),
            pltpu.SemaphoreType.DMA((stacked, tiles)),
        ]

    by_turn = owner_count == 8
    near = owner_count // 2
    slots = near if by_turn else owner_count
    raw_shape = (field_count, tiles, half, level_count, LANES)
    piece = jax.ShapeDtypeStruct(payload(blocks)[1:], jnp.bfloat16)
    whole_payload = jax.ShapeDtypeStruct(payload(blocks), jnp.bfloat16)
    raw = jax.ShapeDtypeStruct(raw_shape, jnp.bfloat16)
    inner_shapes = [raw] if by_turn else [whole_payload]
    starts_scratch = pltpu.SMEM((owner_count,), jnp.int32)
    *inner, first, last = pl.pallas_call(
        functools.partial(inner_kernel, lat_rows, by_turn),
        in_specs=[smem, anywhere, anywhere],
        out_specs=[anywhere] * (len(inner_shapes) + 2),
        out_shape=inner_shapes + [halo_shape, halo_shape],
        scratch_shapes=scratch((), lat_rows)
        + [
            starts_scratch,
            pltpu.VMEM((field_count, slots) + payload(blocks)[2:], jnp.bfloat16),
            pltpu.VMEM(raw_shape, jnp.bfloat16),
            pltpu.VMEM((2,) + halo_shape.shape, halo_shape.dtype),
            pltpu.SemaphoreType.DMA((stacked, slots + 3)),
        ],
        compiler_params=params,
        cost_estimate=pl.CostEstimate(flops=1, bytes_accessed=1, transcendentals=0),
        name="inner_rows",
    )(lon_counts, flat_fields, flat_winds)

    up = [(i, i + 1) for i in range(band_count - 1)]
    down = [(j, i) for i, j in up]

    def exchange(x):
        return lax.all_to_all(x, "lev", split_axis=0, concat_axis=0, tiled=True)

    def turned_exchange(x, turn):
        return lax.ppermute(x, "lev", [(i, i ^ turn) for i in range(owner_count)]) if turn else x

    def pack_half(raw_rows):
        return pl.pallas_call(
            mirror_kernel,
            in_specs=[smem, pl.BlockSpec(memory_space=pltpu.VMEM)],
            out_shape=[piece] * near,
            scratch_shapes=[scratch((), lat_rows)[2], starts_scratch],
            compiler_params=light,
            cost_estimate=pl.CostEstimate(flops=1, bytes_accessed=1, transcendentals=0),
            name="half_slots",
        )(lon_counts, raw_rows)

    if by_turn:
        crossed = turned_exchange(inner[0], near + near // 2)
        inner_parts = [turned_exchange(x, turn) for turn, x in enumerate(pack_half(inner[0]))]
    else:
        inner_parts = [exchange(inner[0])]
    before = lax.ppermute(last, "lat", up)
    after = lax.ppermute(first, "lat", down)

    edge_shapes = [piece] * owner_count if by_turn else [whole_payload]
    edge = pl.pallas_call(
        functools.partial(edge_kernel, lat_rows, by_turn),
        in_specs=[smem, anywhere, anywhere] + [pl.BlockSpec(memory_space=pltpu.VMEM)] * 2,
        out_shape=edge_shapes,
        scratch_shapes=scratch((2,), 3 * HALO)
        + [
            starts_scratch,
            pltpu.VMEM((2,) + halo_shape.shape, jnp.float32),
        ],
        compiler_params=params,
        cost_estimate=pl.CostEstimate(flops=1, bytes_accessed=1, transcendentals=0),
        name="edge_rows",
    )(lon_counts, flat_fields, flat_winds, before, after)

    weights = (w_first, w_second, w_third)
    weights, _ = lax.optimization_barrier((weights, edge[0]))
    turned = pl.pallas_call(
        turn_kernel,
        in_specs=[pl.BlockSpec(memory_space=pltpu.VMEM)] * len(weights),
        out_shape=[jax.ShapeDtypeStruct(w.shape[::-1], w.dtype) for w in weights],
        compiler_params=light,
        cost_estimate=pl.CostEstimate(flops=1, bytes_accessed=1, transcendentals=0),
        name="turned_weights",
    )(*weights)
    if by_turn:
        edge = list(edge)
        edge[near:], _ = lax.optimization_barrier((edge[near:], turned))
        mirrored = pack_half(crossed)
        edge[2:near], mirrored = lax.optimization_barrier((edge[2:near], mirrored))
        near_parts = inner_parts[1:]
        near_parts, edge[near + 1 :] = lax.optimization_barrier(
            (near_parts, edge[near + 1 :])
        )
        inner_parts = inner_parts[:1] + near_parts
        edge_parts = [turned_exchange(x, turn) for turn, x in enumerate(edge)]
        mirrored = [turned_exchange(x, turn) for turn, x in enumerate(mirrored)]
        inner_parts += [mirrored[turn ^ (near // 2)] for turn in range(near)]
    else:
        edge_parts = [exchange(edge[0])]

    def by_level(block):
        if level_count % 16 == 0:
            return block
        return block.transpose(1, 2, 3, 0, 4, 5).reshape(
            1, field_count, block.shape[2], half, all_levels, LANES
        )

    def block_spec(block):
        return pl.BlockSpec(
            block.shape[:2] + (1,) + block.shape[3:], lambda i: (0, 0, i, 0, 0, 0)
        )

    def cost(count):
        return pl.CostEstimate(flops=1, bytes_accessed=1, transcendentals=0)

    weight_specs = [pl.BlockSpec(memory_space=pltpu.VMEM)] * 4
    if by_turn:
        part_specs = [
            pl.BlockSpec((field_count, 1, half, level_count, LANES), lambda i: (0, i, 0, 0, 0))
        ] * owner_count
    else:
        inner_parts = [by_level(inner_parts[0])]
        edge_parts = [by_level(edge_parts[0])]
        part_specs = [block_spec(edge_parts[0])]
    sorted_scratch = pltpu.VMEM((field_count, all_levels, half * LANES), jnp.bfloat16)
    done_spec = pl.BlockSpec((half, features, LANES), lambda i: (0, 0, i))
    done = pl.pallas_call(
        functools.partial(half_kernel, lat_rows, inner_rows, by_turn),
        grid=(blocks,),
        in_specs=[smem, smem] + part_specs + weight_specs,
        out_specs=done_spec,
        out_shape=jax.ShapeDtypeStruct((half, features, slot_width), jnp.bfloat16),
        scratch_shapes=[sorted_scratch],
        compiler_params=light,
        cost_estimate=cost(blocks),
        name="inner_columns",
    )(group_list, lon_counts, *inner_parts, remap_weight, *turned)
    out = pl.pallas_call(
        functools.partial(last_kernel, edge_rows, inner_rows, by_turn),
        grid=(blocks,),
        in_specs=[smem, smem] + part_specs + [done_spec] + weight_specs,
        out_specs=pl.BlockSpec((features, lat_rows, LANES), lambda i: (0, 0, i)),
        out_shape=jax.ShapeDtypeStruct((features, lat_rows, slot_width), jnp.bfloat16),
        scratch_shapes=[pltpu.VMEM((features * lat_rows, LANES), jnp.float32), sorted_scratch],
        compiler_params=light,
        cost_estimate=cost(blocks),
        name="edge_columns",
    )(group_list, lon_counts, *edge_parts, done, remap_weight, *turned)
    return out.reshape(field_count, all_levels, lat_rows, slot_width)


def solution(mesh):
    in_specs = (
        P(None, "lev", "lat", None),
        P(None, "lev", "lat", None),
        P(),
        P(),
        P(),
        P(),
        P("lat", None),
        P(),
    )
    out_specs = P(None, None, "lat", "lev")
    return jax.shard_map(shards, mesh=mesh, in_specs=in_specs, out_specs=out_specs, check_vma=False)
```
